256 devices in a mesh: pb: 8 (over y, core), ka: 32 (over x, z).
Axes of the slice: x: 4, y: 4, z: 8, core: 2. Of those that a mesh axis runs over, the one named last changes fastest.
Arguments:
- query_vectors: bfloat16 [32768, 1024], P(('pb', 'ka')), may hold values from -1.5 to 1.5
- key_vectors: bfloat16 [16384, 1024], P(('ka', 'pb')), may hold values from -1.5 to 1.5
- value_vectors: bfloat16 [16384, 1024], P(('ka', 'pb')), may hold values from -4 to 4
- forward_out: bfloat16 [32768, 1024], P(('pb', 'ka')), may hold values from -4 to 4
- grad_out: bfloat16 [32768, 1024], P(('pb', 'ka')), may hold values from -4 to 4
- logsumexp: float32 [16, 32768], P(None, ('pb', 'ka')), may hold values from 2 to 4
- block_pairs: int32 [8, 32, 2, 24], P('pb'), may hold values from 0 to 31, as said below
- counts: int32 [8, 32], P('pb'), may hold values from 1 to 24, as said below
Outputs:
- grad_queries: bfloat16 [32768, 1024], P(('pb', 'ka'))
- grad_keys: bfloat16 [16384, 1024], P(('ka', 'pb'))
- grad_values: bfloat16 [16384, 1024], P(('ka', 'pb'))
The draws below stay inside these ranges and needn't reach their ends.
Inputs may be any that keep to these rules, and one draw needn't show every extreme that they name: `block_pairs`: the 24 pairs of one query shard with one key shard are distinct; entry 0 is a query block below 32, entry 1 a key block below 4; slots at or after the count are to be ignored. `counts`: some query shard and key shard have exactly 24 used slots in every draw.
All inputs are finite; a program needn't handle non-finite values.
Results may differ from the reference program's by a relative error of at most 0.005.
Values may be sent and summed in bfloat16 or wider, within the bound.
A program may use at most 128 MiB of HBM per device.

```python
import jax
import jax.numpy as jnp
from jax import lax

D = 1024
HEADS = 16
HEAD_DIM = 64
BLK = 128
QB = 32
KB = 4
PMAX = 24
NQ = 32768
NK = 16384
N_PB = 8
N_KA = 32


def draw_block_pairs(key, part):
    choices_all = QB * KB
    ranks = jax.random.randint(key, (N_PB, N_KA, choices_all), 0, 65536)
    ranked = ranks * choices_all + jnp.arange(choices_all, dtype=jnp.int32)
    picked = jnp.argsort(ranked, axis=-1)[:, :, :PMAX].astype(jnp.int32)
    return jnp.stack([picked // KB, picked % KB], axis=2).astype(jnp.int32)


def draw_counts(key, part):
    base_count = jax.random.randint(jax.random.fold_in(key, 1), (N_PB, N_KA), 1, PMAX // 2 + 1)
    hot_flag = jax.random.randint(jax.random.fold_in(key, 2), (N_PB, N_KA), 0, 8) == 0
    hot_count = jax.random.randint(jax.random.fold_in(key, 3), (N_PB, N_KA), PMAX // 2, PMAX + 1)
    merged = jnp.where(hot_flag, hot_count, base_count).reshape(-1)
    fullest = jax.random.randint(jax.random.fold_in(key, 4), (), 0, N_PB * N_KA)
    merged = merged.at[fullest].set(PMAX)
    return merged.reshape(N_PB, N_KA).astype(jnp.int32)


def block_scale(key, dims, shards, smallest, largest):
    def one(position, blocks):
        heights = jax.random.uniform(jax.random.fold_in(jax.random.fold_in(key, 6), position), (blocks,), jnp.float32, smallest / len(shards), largest / len(shards))
        return jnp.repeat(jnp.exp(heights), dims[position] // blocks).reshape((-1,) + (1,) * (len(dims) - position - 1))

    level = one(*shards[0])
    for cut in shards[1:]:
        level = level * one(*cut)
    return level


def normal_values(stream_key, extent, scale, reach, cuts=(), held_as=jnp.bfloat16):
    entries = scale * jax.random.normal(stream_key, extent, jnp.float32)
    if cuts:
        entries = entries * block_scale(stream_key, extent, cuts, -0.22, 0.18)
    return jnp.clip(entries, -reach, reach).astype(held_as)


def setup_inputs(seed: int = 0) -> dict:
    splits = jax.random.split(jax.random.key(seed), 9)
    return {
        "query_vectors": normal_values(splits[0], (NQ, D), 0.6, 1.5, ((0, 256),)),
        "key_vectors": normal_values(splits[1], (NK, D), 0.6, 1.5, ((0, 256),)),
        "value_vectors": normal_values(splits[2], (NK, D), 1.0, 4.0, ((0, 256),)),
        "forward_out": normal_values(splits[3], (NQ, D), 1.0, 4.0, ((0, 256),)),
        "grad_out": normal_values(splits[4], (NQ, D), 1.0, 4.0, ((0, 256),)),
        "logsumexp": jnp.clip(2.0 + 2.0 * jax.random.uniform(splits[5], (HEADS, NQ), jnp.float32) ** block_scale(splits[5], (HEADS, NQ), ((1, 256),), -0.2, 0.2), 2.0, 4.0),
        "block_pairs": draw_block_pairs(jax.random.fold_in(splits[8], 71), 0),
        "counts": draw_counts(jax.random.fold_in(splits[8], 71), 0),
    }


def head_grads(query_block, dout_block, stat_block, key_block, value_block):
    precise = lax.Precision.HIGHEST
    count_rows = query_block.shape[0]
    score_scale = HEAD_DIM ** -0.5
    query_heads = query_block.astype(jnp.float32).reshape(count_rows, HEADS, HEAD_DIM)
    dout_heads = dout_block.astype(jnp.float32).reshape(count_rows, HEADS, HEAD_DIM)
    key_heads = key_block.astype(jnp.float32).reshape(count_rows, HEADS, HEAD_DIM)
    value_heads = value_block.astype(jnp.float32).reshape(count_rows, HEADS, HEAD_DIM)
    scores = jnp.einsum("qhd,khd->hqk", query_heads, key_heads, precision=precise) * score_scale
    attn_prob = jnp.exp(scores - stat_block[0][:, :, None])
    prob_half = lax.optimization_barrier(attn_prob.astype(jnp.bfloat16)).astype(jnp.float32)
    value_add = jnp.einsum("hqk,qhd->khd", prob_half, dout_heads, precision=precise)
    dprob = jnp.einsum("qhd,khd->hqk", dout_heads, value_heads, precision=precise)
    dscore = attn_prob * (dprob - stat_block[1][:, :, None])
    dscore = lax.optimization_barrier(dscore.astype(jnp.bfloat16)).astype(jnp.float32)
    query_add = jnp.einsum("hqk,khd->qhd", dscore, key_heads, precision=precise) * score_scale
    key_add = jnp.einsum("hqk,qhd->khd", dscore, query_heads, precision=precise) * score_scale
    return (query_add.reshape(count_rows, D), key_add.reshape(count_rows, D), value_add.reshape(count_rows, D))


def reference(query_vectors, key_vectors, value_vectors, forward_out, grad_out, logsumexp, block_pairs, counts):
    products = grad_out.astype(jnp.float32) * forward_out.astype(jnp.float32)
    row_delta = jnp.sum(products.reshape(NQ, HEADS, HEAD_DIM), axis=2).T
    stats = jnp.stack([logsumexp, row_delta], axis=0)
    shard_ids = jnp.arange(N_PB, dtype=jnp.int32)[:, None, None]
    key_ids = jnp.arange(N_KA, dtype=jnp.int32)[None, :, None]
    slot_ids = jnp.arange(PMAX, dtype=jnp.int32)[None, None, :]
    query_list = (shard_ids * QB + block_pairs[:, :, 0, :]).reshape(-1).astype(jnp.int32)
    key_list = (key_ids * KB + block_pairs[:, :, 1, :]).reshape(-1).astype(jnp.int32)
    used_list = (slot_ids < counts[:, :, None]).reshape(-1)

    def pair_step(totals, pair_entry):
        query_grad, key_grad, value_grad = totals
        query_block, key_block, is_used = pair_entry
        query_row = (query_block * BLK).astype(jnp.int32)
        key_row = (key_block * BLK).astype(jnp.int32)
        q_rows = lax.dynamic_slice_in_dim(query_vectors, query_row, BLK, 0)
        d_rows = lax.dynamic_slice_in_dim(grad_out, query_row, BLK, 0)
        s_rows = lax.dynamic_slice_in_dim(stats, query_row, BLK, 2)
        k_rows = lax.dynamic_slice_in_dim(key_vectors, key_row, BLK, 0)
        v_rows = lax.dynamic_slice_in_dim(value_vectors, key_row, BLK, 0)

        def compute():
            return head_grads(q_rows, d_rows, s_rows, k_rows, v_rows)

        def nothing():
            zero_block = jnp.zeros((BLK, D), jnp.float32)
            return (zero_block, zero_block, zero_block)

        query_add, key_add, value_add = lax.cond(is_used, compute, nothing)
        query_grad = lax.dynamic_update_slice_in_dim(query_grad, lax.dynamic_slice_in_dim(query_grad, query_row, BLK, 0) + query_add, query_row, 0)
        key_grad = lax.dynamic_update_slice_in_dim(key_grad, lax.dynamic_slice_in_dim(key_grad, key_row, BLK, 0) + key_add, key_row, 0)
        value_grad = lax.dynamic_update_slice_in_dim(value_grad, lax.dynamic_slice_in_dim(value_grad, key_row, BLK, 0) + value_add, key_row, 0)
        return (query_grad, key_grad, value_grad), None

    initial = (jnp.zeros((NQ, D), jnp.float32), jnp.zeros((NK, D), jnp.float32), jnp.zeros((NK, D), jnp.float32))
    totals, unused = lax.scan(pair_step, initial, (query_list, key_list, used_list))
    query_grad, key_grad, value_grad = totals
    return (query_grad.astype(jnp.bfloat16), key_grad.astype(jnp.bfloat16), value_grad.astype(jnp.bfloat16))
```

```python
import jax
import jax.numpy as jnp
from jax import lax
from jax.experimental import pallas as pl
from jax.experimental.pallas import tpu as pltpu
from jax.sharding import PartitionSpec as P

NX, NY, NZ = 4, 4, 8
HEADS = 16
BLK = 128
HALF = BLK // 2
WIDTH = 1024
HEAD_PAIRS = WIDTH // 128
KEY_BLOCKS = NX * NY
BUCKET = 16
SCALE = 64**-0.5
LOG2E = 1.4426950408889634
MESH = pl.DeviceIdType.MESH
ANY = pl.BlockSpec(memory_space=pl.ANY)
F32 = jnp.float32
BF16 = jnp.bfloat16


class Place:
    def __init__(self):
        pb = lax.axis_index("pb")
        ka = lax.axis_index("ka")
        self.y = lax.div(pb, 2)
        self.core = lax.rem(pb, 2)
        self.x = lax.div(ka, NZ)
        self.z = lax.rem(ka, NZ)
        self.sibling = (self.y * 2 + 1 - self.core, ka)

    def over_x(self, step):
        return (self.y * 2 + self.core, self.xs(step) * NZ + self.z)

    def over_y(self, step):
        return (self.ys(step) * 2 + self.core, self.x * NZ + self.z)

    def over_z(self, step):
        return (self.y * 2 + self.core, self.x * NZ + self.zs(step))

    def xs(self, step):
        return lax.rem(self.x + step + NX, NX)

    def ys(self, step):
        return lax.rem(self.y + step + NY, NY)

    def zs(self, step):
        return lax.rem(self.z + step + NZ, NZ)

    def greet(self):
        barrier = pltpu.get_barrier_semaphore()
        neighbours = [self.sibling]
        for step in (1, -1):
            neighbours += [self.over_x(step), self.over_y(step), self.over_z(step)]
        for neighbour in neighbours:
            pl.semaphore_signal(barrier, inc=1, device_id=neighbour, device_id_type=MESH)
        pl.semaphore_wait(barrier, len(neighbours))


class Sender:
    def __init__(self, send_sems, recv_sems):
        self.send_sems = send_sems
        self.recv_sems = recv_sems
        self.copies = []

    def __call__(self, source, target, device):
        index = len(self.copies)
        copy = pltpu.make_async_remote_copy(
            src_ref=source,
            dst_ref=target,
            send_sem=self.send_sems.at[index],
            recv_sem=self.recv_sems.at[index],
            device_id=device,
            device_id_type=MESH,
        )
        copy.start()
        self.copies.append(copy)
        return copy

    def finish(self):
        for copy in self.copies:
            copy.wait_send()


GATHER_COPIES = 45


def gather_kernel(
    q_ref, do_ref, k_ref, v_ref, out_ref, lse_ref,
    q_all, do_all, st_all, k_all, v_all,
    do_buf, out_buf, st_buf, send_sems, recv_sems, local_sems,
):
    me = Place()
    x, y, z = me.x, me.y, me.z
    rows = pl.ds(pl.multiple_of(me.core * HALF, HALF), HALF)

    def part(which):
        return pl.ds(pl.multiple_of(me.core * HALF + which * (HALF // 2), HALF // 2), HALF // 2)

    loads = [
        pltpu.make_async_copy(do_ref, do_buf, local_sems.at[0]),
        pltpu.make_async_copy(out_ref, out_buf, local_sems.at[1]),
        pltpu.make_async_copy(lse_ref, st_buf.at[pl.ds(0, HEADS)], local_sems.at[2]),
    ]
    for load in loads:
        load.start()
    owns = [
        pltpu.make_async_copy(k_ref, k_all.at[y, x, rows], local_sems.at[3]),
        pltpu.make_async_copy(v_ref, v_all.at[x, y, rows], local_sems.at[4]),
        pltpu.make_async_copy(q_ref, q_all.at[z], local_sems.at[5]),
        pltpu.make_async_copy(do_ref, do_all.at[z], local_sems.at[6]),
    ]
    for own in owns:
        own.start()
    me.greet()
    send = Sender(send_sems, recv_sems)
    up, down = me.over_z(1), me.over_z(-1)
    q_up = [send(q_ref, q_all.at[z], up)]
    do_down = [send(do_ref, do_all.at[z], down)]
    k_right = send(k_ref, k_all.at[y, x, rows], me.over_x(1))
    k_left = send(k_ref, k_all.at[y, x, rows], me.over_x(-1))
    v_right = send(v_ref, v_all.at[x, y, rows], me.over_y(1))
    v_left = send(v_ref, v_all.at[x, y, rows], me.over_y(-1))
    do_up = [send(do_ref, do_all.at[z], up)]
    q_down = [send(q_ref, q_all.at[z], down)]

    for load in loads:
        load.wait()
    products = do_buf[...].astype(F32) * out_buf[...].astype(F32)
    high = products.astype(BF16)
    low = (products - high.astype(F32)).astype(BF16)
    head = lax.broadcasted_iota(jnp.int32, (HEADS, WIDTH), 0) * 64
    feature = lax.broadcasted_iota(jnp.int32, (HEADS, WIDTH), 1)
    member = jnp.where((feature >= head) & (feature < head + 64), 1.0, 0.0).astype(BF16)
    over_features = (((1,), (1,)), ((), ()))
    delta = lax.dot_general(member, high, over_features, preferred_element_type=F32)
    delta = delta + lax.dot_general(member, low, over_features, preferred_element_type=F32)
    st_buf[pl.ds(0, HEADS), :] = st_buf[pl.ds(0, HEADS), :] * LOG2E
    st_buf[pl.ds(HEADS, HEADS), :] = delta
    st_own = pltpu.make_async_copy(st_buf, st_all.at[z], local_sems.at[7])
    st_own.start()
    st_up = [send(st_buf, st_all.at[z], up)]
    st_down = [send(st_buf, st_all.at[z], down)]

    k_right.wait_recv()
    k_far = [send(k_all.at[y, me.xs(-1), part(0)], k_all.at[y, me.xs(-1), part(0)], me.over_x(1))]
    v_right.wait_recv()
    v_far = [send(v_all.at[x, me.ys(-1), part(0)], v_all.at[x, me.ys(-1), part(0)], me.over_y(1))]
    k_left.wait_recv()
    k_far.append(send(k_all.at[y, me.xs(1), part(1)], k_all.at[y, me.xs(1), part(1)], me.over_x(-1)))
    v_left.wait_recv()
    v_far.append(send(v_all.at[x, me.ys(1), part(1)], v_all.at[x, me.ys(1), part(1)], me.over_y(-1)))

    for own in owns:
        own.wait()
    every = slice(None)
    for copy in k_far:
        copy.wait_recv()
    k_own = k_all.at[y, every, rows]
    k_right = send(k_own, k_own, me.over_y(1))
    k_left = send(k_own, k_own, me.over_y(-1))
    for copy in v_far:
        copy.wait_recv()
    v_own = v_all.at[x, every, rows]
    v_right = send(v_own, v_own, me.over_x(1))
    v_left = send(v_own, v_own, me.over_x(-1))
    from_sibling = [send(k_own, k_own, me.sibling), send(v_own, v_own, me.sibling)]

    def forward_up(hop, which, blocks, copies):
        copies[hop - 1].wait_recv()
        block = blocks.at[me.zs(-hop)]
        copies.append(send(block, block, up))

    def forward_down(hop, which, blocks, copies):
        copies[hop - 1].wait_recv()
        block = blocks.at[me.zs(hop)]
        copies.append(send(block, block, down))

    def hop_first(hop):
        forward_up(hop, 0, q_all, q_up)
        forward_down(hop, 0, do_all, do_down)

    def hop_second(hop):
        forward_up(hop, 1, do_all, do_up)
        forward_down(hop, 1, q_all, q_down)
        forward_up(hop, 2, st_all, st_up)
        forward_down(hop, 2, st_all, st_down)

    hop_first(1)
    hop_second(1)

    def across(blocks, line, step, low, device):
        part = blocks.at[line(step), pl.ds(low, 2), rows]
        return send(part, part, device)

    k_right.wait_recv()
    k_far = [across(k_all, me.ys, -1, 0, me.over_y(1))]
    v_right.wait_recv()
    v_far = [across(v_all, me.xs, -1, 0, me.over_x(1))]
    k_left.wait_recv()
    k_far.append(across(k_all, me.ys, 1, 2, me.over_y(-1)))
    v_left.wait_recv()
    v_far.append(across(v_all, me.xs, 1, 2, me.over_x(-1)))
    for step in (-1, 1):
        k_near = k_all.at[me.ys(step), every, rows]
        from_sibling.append(send(k_near, k_near, me.sibling))
        v_near = v_all.at[me.xs(step), every, rows]
        from_sibling.append(send(v_near, v_near, me.sibling))

    hop_first(2)
    for copy in k_far + v_far:
        copy.wait_recv()
    k_last = k_all.at[me.ys(2), every, rows]
    from_sibling.append(send(k_last, k_last, me.sibling))
    v_last = v_all.at[me.xs(2), every, rows]
    from_sibling.append(send(v_last, v_last, me.sibling))
    hop_second(2)

    forward_up(3, 0, q_all, q_up)
    forward_down(3, 0, do_all, do_down)
    do_up[2].wait_recv()
    q_down[2].wait_recv()
    forward_up(3, 2, st_all, st_up)
    st_down[2].wait_recv()
    for copy in from_sibling:
        copy.wait_recv()
    st_own.wait()
    q_up[3].wait_recv()
    do_down[3].wait_recv()
    st_up[3].wait_recv()
    send.finish()
    assert len(send.copies) == GATHER_COPIES, len(send.copies)


def gather(q, do, k, v, out, lse):
    return pl.pallas_call(
        gather_kernel,
        out_shape=[
            jax.ShapeDtypeStruct((NZ, BLK, WIDTH), BF16),
            jax.ShapeDtypeStruct((NZ, BLK, WIDTH), BF16),
            jax.ShapeDtypeStruct((NZ, 2 * HEADS, BLK), F32),
            jax.ShapeDtypeStruct((NY, NX, BLK, WIDTH), BF16),
            jax.ShapeDtypeStruct((NX, NY, BLK, WIDTH), BF16),
        ],
        in_specs=[ANY] * 6,
        out_specs=[ANY] * 5,
        scratch_shapes=[
            pltpu.VMEM((BLK, WIDTH), BF16),
            pltpu.VMEM((BLK, WIDTH), BF16),
            pltpu.VMEM((2 * HEADS, BLK), F32),
            pltpu.SemaphoreType.DMA((GATHER_COPIES,)),
            pltpu.SemaphoreType.DMA((GATHER_COPIES,)),
            pltpu.SemaphoreType.DMA((8,)),
        ],
        compiler_params=pltpu.CompilerParams(
            collective_id=0, has_side_effects=True, vmem_limit_bytes=16 << 20
        ),
        name="gather_blocks",
    )(q, do, k, v, out, lse)


def pair_kernel(
    pairs, counts, place, q_all, do_all, st_all, k_all, v_all,
    dq_out, dk_out, dv_out,
    q_buf, do_buf, st_buf, k_buf, v_buf, k_turned, dq_sum, dk_sum, dv_sum, dq_stage, dk_stage, dv_stage, zeros,
    listed, filled, flat, in_sems, out_sems, zero_sems, dq_sems,
):
    x = place[0]
    z = place[1]
    for block in range(KEY_BLOCKS):
        filled[block] = 0
    for column in range(NX):
        shard = column * NZ + z

        def enlist(slot, carry, column=column, shard=shard):
            query = pairs[0, shard, 0, slot]
            block = pairs[0, shard, 1, slot] * NX + column
            have = filled[block]
            listed[block * BUCKET + have] = block * NZ + lax.rem(query, NZ)
            filled[block] = have + jnp.where(lax.div(query, NZ) == x, 1, 0)
            return carry

        lax.fori_loop(0, counts[0, shard], enlist, 0)
    zeros[...] = jnp.zeros_like(zeros)
    total = jnp.int32(0)
    for block in range(KEY_BLOCKS):

        def append(slot, position, block=block):
            flat[position] = listed[block * BUCKET + slot]
            return position + 1

        total = lax.fori_loop(0, filled[block], append, total)
        empty = filled[block] == 0
        up, across = divmod(block, NX)

        @pl.when(empty)
        def _(up=up, across=across):
            pltpu.make_async_copy(zeros, dk_out.at[up, across], zero_sems.at[0]).start()
            pltpu.make_async_copy(zeros, dv_out.at[across, up], zero_sems.at[1]).start()

    def fetches(index, slot):
        entry = flat[index]
        block = lax.div(entry, NZ)
        query = lax.rem(entry, NZ)
        up, across = lax.div(block, NX), lax.rem(block, NX)
        return [
            pltpu.make_async_copy(k_all.at[up, across], k_buf.at[slot], in_sems.at[slot, 0]),
            pltpu.make_async_copy(q_all.at[query], q_buf.at[slot], in_sems.at[slot, 1]),
            pltpu.make_async_copy(st_all.at[query], st_buf.at[slot], in_sems.at[slot, 2]),
            pltpu.make_async_copy(v_all.at[across, up], v_buf.at[slot], in_sems.at[slot, 3]),
            pltpu.make_async_copy(do_all.at[query], do_buf.at[slot], in_sems.at[slot, 4]),
        ]

    @pl.when(total > 0)
    def _():
        for fetch in fetches(0, 0):
            fetch.start()

    def clear(query, carry):
        dq_sum[query] = jnp.zeros((WIDTH, BLK), F32)
        return carry

    lax.fori_loop(0, NZ, clear, 0)

    lane = lax.broadcasted_iota(jnp.int32, (1, 128), 1)
    first_half = jnp.where(lane < 64, 1.0, 0.0).astype(BF16)
    second_half = jnp.where(lane < 64, 0.0, 1.0).astype(BF16)
    nt = (((1,), (1,)), ((), ()))
    nn = (((1,), (0,)), ((), ()))

    def flush_copies(slot, block):
        up, across = lax.div(block, NX), lax.rem(block, NX)
        return [
            pltpu.make_async_copy(dk_stage.at[slot], dk_out.at[up, across], out_sems.at[slot, 0]),
            pltpu.make_async_copy(dv_stage.at[slot], dv_out.at[across, up], out_sems.at[slot, 1]),
        ]

    def step(index, flushed):
        slot = lax.rem(index, 2)
        block = lax.div(flat[index], NZ)
        query = lax.rem(flat[index], NZ)
        before = jnp.where(index > 0, lax.div(flat[jnp.maximum(index - 1, 0)], NZ), -1)
        after = jnp.where(
            index + 1 < total, lax.div(flat[jnp.minimum(index + 1, total - 1)], NZ), -1
        )

        @pl.when(index + 1 < total)
        def _():
            for fetch in fetches(index + 1, 1 - slot):
                fetch.start()

        for fetch in fetches(index, slot):
            fetch.wait()

        @pl.when(before != block)
        def _():
            dk_sum[...] = jnp.zeros_like(dk_sum)
            dv_sum[...] = jnp.zeros_like(dv_sum)
            for pair in range(HEAD_PAIRS):
                lanes = slice(pair * 128, pair * 128 + 128)
                turned = jnp.transpose(k_buf[slot, :, lanes].astype(F32)).astype(BF16)
                k_turned[lanes, :] = turned

        for pair in range(HEAD_PAIRS):
            lanes = slice(pair * 128, pair * 128 + 128)
            keys = k_buf[slot, :, lanes]
            values = v_buf[slot, :, lanes]
            queries = q_buf[slot, :, lanes]
            douts = do_buf[slot, :, lanes]
            q_two = jnp.concatenate([queries * first_half, queries * second_half], axis=0)
            do_two = jnp.concatenate([douts * first_half, douts * second_half], axis=0)
            scores = lax.dot_general(keys, q_two, nt, preferred_element_type=F32)
            dprob = lax.dot_general(values, do_two, nt, preferred_element_type=F32)
            probs, dscores = [], []
            for side in range(2):
                head = 2 * pair + side
                cut = slice(side * BLK, side * BLK + BLK)
                lse = st_buf[slot, head : head + 1, :]
                delta = st_buf[slot, HEADS + head : HEADS + head + 1, :]
                prob = jnp.exp2(scores[:, cut] * (SCALE * LOG2E) - lse)
                probs.append(prob.astype(BF16))
                dscores.append((prob * (dprob[:, cut] - delta)).astype(BF16))
            dv_sum[:, lanes] += lax.dot_general(
                jnp.concatenate(probs, axis=1), do_two, nn, preferred_element_type=F32
            )
            dk_sum[:, lanes] += lax.dot_general(
                jnp.concatenate(dscores, axis=1), q_two, nn, preferred_element_type=F32
            )
            turned = k_turned[lanes, :]
            for side in range(2):
                low = pair * 128 + side * 64
                dq_sum[query, low : low + 64, :] += lax.dot_general(
                    turned[side * 64 : side * 64 + 64], dscores[side], nn, preferred_element_type=F32
                )

        @pl.when(after != block)
        def _():
            stage = lax.rem(flushed, 2)

            @pl.when(flushed >= 2)
            def _():
                for copy in flush_copies(stage, block):
                    copy.wait()

            dk_stage[stage] = (dk_sum[...] * SCALE).astype(BF16)
            dv_stage[stage] = dv_sum[...].astype(BF16)
            for copy in flush_copies(stage, block):
                copy.start()

        return flushed + jnp.where(after != block, 1, 0)

    flushed = lax.fori_loop(0, total, step, 0)

    def turn_in(query, carry):
        dq_stage[query] = (dq_sum[query] * SCALE).astype(BF16)
        pltpu.make_async_copy(dq_stage.at[query], dq_out.at[query], dq_sems.at[query]).start()
        return carry

    lax.fori_loop(0, NZ, turn_in, 0)
    for slot in range(2):

        @pl.when(flushed > slot)
        def _(slot=slot):
            for copy in flush_copies(slot, 0):
                copy.wait()

    for block in range(KEY_BLOCKS):
        up, across = divmod(block, NX)

        @pl.when(filled[block] == 0)
        def _(up=up, across=across):
            pltpu.make_async_copy(zeros, dk_out.at[up, across], zero_sems.at[0]).wait()
            pltpu.make_async_copy(zeros, dv_out.at[across, up], zero_sems.at[1]).wait()

    def finish(query, carry):
        pltpu.make_async_copy(dq_stage.at[query], dq_out.at[query], dq_sems.at[query]).wait()
        return carry

    lax.fori_loop(0, NZ, finish, 0)


def pairs_over_blocks(pairs, counts, place, q_all, do_all, st_all, k_all, v_all):
    smem = pl.BlockSpec(memory_space=pltpu.SMEM)
    return pl.pallas_call(
        pair_kernel,
        out_shape=[
            jax.ShapeDtypeStruct((NZ, WIDTH, BLK), BF16),
            jax.ShapeDtypeStruct((NY, NX, BLK, WIDTH), BF16),
            jax.ShapeDtypeStruct((NX, NY, BLK, WIDTH), BF16),
        ],
        in_specs=[smem] * 3 + [ANY] * 5,
        out_specs=[ANY] * 3,
        scratch_shapes=[
            pltpu.VMEM((2, BLK, WIDTH), BF16),
            pltpu.VMEM((2, BLK, WIDTH), BF16),
            pltpu.VMEM((2, 2 * HEADS, BLK), F32),
            pltpu.VMEM((2, BLK, WIDTH), BF16),
            pltpu.VMEM((2, BLK, WIDTH), BF16),
            pltpu.VMEM((WIDTH, BLK), BF16),
            pltpu.VMEM((NZ, WIDTH, BLK), F32),
            pltpu.VMEM((BLK, WIDTH), F32),
            pltpu.VMEM((BLK, WIDTH), F32),
            pltpu.VMEM((NZ, WIDTH, BLK), BF16),
            pltpu.VMEM((2, BLK, WIDTH), BF16),
            pltpu.VMEM((2, BLK, WIDTH), BF16),
            pltpu.VMEM((BLK, WIDTH), BF16),
            pltpu.SMEM((KEY_BLOCKS * BUCKET,), jnp.int32),
            pltpu.SMEM((KEY_BLOCKS,), jnp.int32),
            pltpu.SMEM((KEY_BLOCKS * NZ,), jnp.int32),
            pltpu.SemaphoreType.DMA((2, 5)),
            pltpu.SemaphoreType.DMA((2, 2)),
            pltpu.SemaphoreType.DMA((2,)),
            pltpu.SemaphoreType.DMA((NZ,)),
        ],
        compiler_params=pltpu.CompilerParams(vmem_limit_bytes=48 << 20),
        name="used_pairs",
    )(pairs, counts, place, q_all, do_all, st_all, k_all, v_all)


REDUCE_COPIES = 38
ROW_STEP = 16


def reduce_kernel(
    dq_part, dk_part, dv_part,
    gq_out, gk_out, gv_out,
    dq_own, dq_in_up, dq_in_down, k_own, v_own, k_sib, v_sib,
    k_far_a, k_far_b, v_far_a, v_far_b, k_near_a, k_near_b, v_near_a, v_near_b,
    k_mid, v_mid, k_end_far_a, k_end_far_b, v_end_far_a, v_end_far_b,
    k_end_a, k_end_b, v_end_a, v_end_b,
    send_sems, recv_sems, local_sems,
):
    me = Place()
    x, y, z = me.x, me.y, me.z
    mine = pl.ds(pl.multiple_of(me.core * HALF, HALF), HALF)
    other = pl.ds(pl.multiple_of((1 - me.core) * HALF, HALF), HALF)
    every = slice(None)
    line = (2, 1, -1, 0)
    loads = {}
    for order, step in enumerate((4, -1, 1, -2, 2, -3, 3, 0)):
        loads["q", step] = pltpu.make_async_copy(
            dq_part.at[me.zs(step)], dq_own.at[me.zs(step)], local_sems.at[8 + order]
        )
    for order, step in enumerate(line):
        loads["k", step] = pltpu.make_async_copy(
            dk_part.at[me.ys(step), every, mine], k_own.at[me.ys(step)], local_sems.at[order]
        )
        loads["v", step] = pltpu.make_async_copy(
            dv_part.at[me.xs(step), every, mine], v_own.at[me.xs(step)], local_sems.at[4 + order]
        )
    for load in loads.values():
        load.start()
    me.greet()
    send = Sender(send_sems, recv_sems)
    up, down = me.over_z(1), me.over_z(-1)
    upper, lower = pl.ds(0, WIDTH // 2), pl.ds(WIDTH // 2, WIDTH // 2)

    loads["q", 4].wait()
    far = me.zs(4)
    arrive = {}
    arrive["up", 0, 1] = send(dq_own.at[far, upper], dq_in_up.at[0, upper], up)
    arrive["down", 1, 1] = send(dq_own.at[far, lower], dq_in_down.at[0, lower], down)

    sib = {}
    for step in line:
        sib["k", step] = send(dk_part.at[me.ys(step), every, other], k_sib.at[me.ys(step)], me.sibling)
        sib["v", step] = send(dv_part.at[me.xs(step), every, other], v_sib.at[me.xs(step)], me.sibling)

    def add_rows(total, terms, count):
        def one(index, carry):
            at = pl.ds(pl.multiple_of(index * ROW_STEP, ROW_STEP), ROW_STEP)
            value = terms[0][at, :].astype(F32)
            for term in terms[1:]:
                value = value + term[at, :].astype(F32)
            total[at, :] = value.astype(total.dtype)
            return carry

        lax.fori_loop(0, count // ROW_STEP, one, 0, unroll=4)

    def hop_q(direction, half, hop):
        side = upper if half == 0 else lower
        if direction == "up":
            step, inbox, device, sign = 4 - hop, dq_in_up, up, 1
        else:
            step, inbox, device, sign = hop - 4, dq_in_down, down, -1
        target = me.zs(step)
        key = (direction, half, hop)
        if key in arrive:
            arrive[key].wait_recv()
            add_rows(
                dq_own.at[target, side],
                [dq_own.at[target, side], inbox.at[hop - 1, side]],
                WIDTH // 2,
            )
        if step:
            arrive[direction, half, hop + 1] = send(
                dq_own.at[target, side], inbox.at[hop, side], device
            )

    for step in (-1, 1, -2, 2, -3, 3, 0):
        loads["q", step].wait()
    hop_q("up", 1, 1)
    hop_q("down", 0, 1)

    def join(name, own, other_core, step, place):
        loads[name, step].wait()
        sib[name, step].wait_recv()
        for row in range(4):
            add_rows(
                own.at[place, row], [own.at[place, row], other_core.at[place, row]], HALF
            )

    far_y, far_x = me.ys(2), me.xs(2)
    join("k", k_own, k_sib, 2, far_y)
    kf_a = send(k_own.at[far_y, pl.ds(0, 2)], k_far_a, me.over_y(1))
    kf_b = send(k_own.at[far_y, pl.ds(2, 2)], k_far_b, me.over_y(-1))
    join("v", v_own, v_sib, 2, far_x)
    vf_a = send(v_own.at[far_x, pl.ds(0, 2)], v_far_a, me.over_x(1))
    vf_b = send(v_own.at[far_x, pl.ds(2, 2)], v_far_b, me.over_x(-1))

    hop_q("up", 0, 1)
    hop_q("down", 1, 1)

    for step in (1, -1):
        join("k", k_own, k_sib, step, me.ys(step))
        join("v", v_own, v_sib, step, me.xs(step))
    hop_q("up", 1, 2)
    hop_q("down", 0, 2)

    def onward(own, place, base, inbox, arrival):
        arrival.wait_recv()
        for row in range(2):
            add_rows(
                own.at[place, base + row], [own.at[place, base + row], inbox.at[row]], HALF
            )

    onward(k_own, me.ys(1), 0, k_far_a, kf_a)
    kn_a = send(k_own.at[me.ys(1)], k_near_a, me.over_y(1))
    onward(v_own, me.xs(1), 0, v_far_a, vf_a)
    vn_a = send(v_own.at[me.xs(1)], v_near_a, me.over_x(1))
    onward(k_own, me.ys(-1), 2, k_far_b, kf_b)
    kn_b = send(k_own.at[me.ys(-1)], k_near_b, me.over_y(-1))
    onward(v_own, me.xs(-1), 2, v_far_b, vf_b)
    vn_b = send(v_own.at[me.xs(-1)], v_near_b, me.over_x(-1))
    hop_q("up", 0, 2)
    hop_q("down", 1, 2)
    join("k", k_own, k_sib, 0, y)
    join("v", v_own, v_sib, 0, x)
    hop_q("up", 1, 3)
    hop_q("down", 0, 3)
    hop_q("up", 0, 3)
    hop_q("down", 1, 3)

    def settle(own, place, near_a, near_b, arrivals, middle, row, far_place):
        at = row
        add_rows(
            middle.at[at],
            [own.at[place, at], near_a.at[at], near_b.at[at]],
            HALF,
        )

    for arrival in (kn_a, kn_b):
        arrival.wait_recv()
    for row in range(4):
        settle(k_own, y, k_near_a, k_near_b, None, k_mid, row, None)
    half_rows = (pl.ds(0, HALF // 2), pl.ds(HALF // 2, HALF // 2))
    ke_a = send(k_mid.at[far_x, half_rows[0]], k_end_far_a, me.over_x(1))
    ke_b = send(k_mid.at[far_x, half_rows[1]], k_end_far_b, me.over_x(-1))
    for arrival in (vn_a, vn_b):
        arrival.wait_recv()
    for row in range(4):
        settle(v_own, x, v_near_a, v_near_b, None, v_mid, row, None)
    ve_a = send(v_mid.at[far_y, half_rows[0]], v_end_far_a, me.over_y(1))
    ve_b = send(v_mid.at[far_y, half_rows[1]], v_end_far_b, me.over_y(-1))

    def last(middle, place, half, inbox, arrival, target, device):
        arrival.wait_recv()
        part = middle.at[place, half_rows[half]]
        add_rows(part, [part, inbox], HALF // 2)
        return send(middle.at[place], target, device)

    kz_a = last(k_mid, me.xs(1), 0, k_end_far_a, ke_a, k_end_a, me.over_x(1))
    kz_b = last(k_mid, me.xs(-1), 1, k_end_far_b, ke_b, k_end_b, me.over_x(-1))
    vz_a = last(v_mid, me.ys(1), 0, v_end_far_a, ve_a, v_end_a, me.over_y(1))
    vz_b = last(v_mid, me.ys(-1), 1, v_end_far_b, ve_b, v_end_b, me.over_y(-1))

    for direction in ("up", "down"):
        for half in range(2):
            arrive[direction, half, 4].wait_recv()
    for tile in range(WIDTH // 128):
        at = pl.ds(tile * 128, 128)
        value = (
            dq_own[z, at, :].astype(F32)
            + dq_in_up[3, at, :].astype(F32)
            + dq_in_down[3, at, :].astype(F32)
        )
        gq_out[:, at] = jnp.transpose(value).astype(BF16)

    for arrival in (kz_a, kz_b):
        arrival.wait_recv()
    add_rows(gk_out, [k_mid.at[x], k_end_a, k_end_b], HALF)
    for arrival in (vz_a, vz_b):
        arrival.wait_recv()
    add_rows(gv_out, [v_mid.at[y], v_end_a, v_end_b], HALF)
    send.finish()
    assert len(send.copies) == REDUCE_COPIES, len(send.copies)


def reduce_parts(dq_part, dk_part, dv_part):
    vmem = pl.BlockSpec(memory_space=pltpu.VMEM)
    line = pltpu.VMEM((4, 4, HALF, WIDTH), BF16)
    two = pltpu.VMEM((2, HALF, WIDTH), BF16)
    four = pltpu.VMEM((4, HALF, WIDTH), BF16)
    quarter = pltpu.VMEM((HALF // 2, WIDTH), BF16)
    one = pltpu.VMEM((HALF, WIDTH), BF16)
    return pl.pallas_call(
        reduce_kernel,
        out_shape=[
            jax.ShapeDtypeStruct((BLK, WIDTH), BF16),
            jax.ShapeDtypeStruct((HALF, WIDTH), BF16),
            jax.ShapeDtypeStruct((HALF, WIDTH), BF16),
        ],
        in_specs=[ANY] * 3,
        out_specs=[vmem] * 3,
        scratch_shapes=[
            pltpu.VMEM((NZ, WIDTH, BLK), BF16),
            pltpu.VMEM((4, WIDTH, BLK), BF16),
            pltpu.VMEM((4, WIDTH, BLK), BF16),
            line, line, line, line,
            two, two, two, two,
            four, four, four, four,
            four, four,
            quarter, quarter, quarter, quarter,
            one, one, one, one,
            pltpu.SemaphoreType.DMA((REDUCE_COPIES,)),
            pltpu.SemaphoreType.DMA((REDUCE_COPIES,)),
            pltpu.SemaphoreType.DMA((16,)),
        ],
        compiler_params=pltpu.CompilerParams(
            collective_id=1, has_side_effects=True, vmem_limit_bytes=48 << 20
        ),
        name="reduce_parts",
    )(dq_part, dk_part, dv_part)


def body(q, k, v, out, do, lse, block_pairs, counts):
    ka = lax.axis_index("ka")
    place = jnp.stack([ka // NZ, ka % NZ]).astype(jnp.int32)
    gathered = gather(q, do, k, v, out, lse)
    parts = pairs_over_blocks(block_pairs, counts, place, *gathered)
    return tuple(reduce_parts(*parts))


def solution(mesh):
    placed = (
        P(("pb", "ka"), None),
        P(("ka", "pb"), None),
        P(("ka", "pb"), None),
        P(("pb", "ka"), None),
        P(("pb", "ka"), None),
        P(None, ("pb", "ka")),
        P("pb", None, None, None),
        P("pb", None),
    )
    return jax.shard_map(
        body,
        mesh=mesh,
        in_specs=placed,
        out_specs=(P(("pb", "ka"), None), P(("ka", "pb"), None), P(("ka", "pb"), None)),
        check_vma=False,
    )
```

```python
import jax
import jax.numpy as jnp
from jax import lax
from jax.experimental import pallas as pl
from jax.experimental.pallas import tpu as pltpu
from jax.sharding import PartitionSpec as P

NX, NY, NZ, CORES = 4, 4, 8, 2
HEADS = 16
OWN_HEADS = HEADS // CORES
BLK = 128
HALF = BLK // 2
WIDTH = 1024
COLS = WIDTH // CORES
HEAD_PAIRS = COLS // 128
SLOTS = 24
KEY_SHARDS = NX * NZ
QUERY_BLOCKS = NZ * CORES
KEY_BLOCKS = NX * NY
BUCKET = 32
SCALE = 64**-0.5
LOG2E = 1.4426950408889634
VMEM_LIMIT = 60 << 20
MESH = pl.DeviceIdType.MESH
ANY = pl.BlockSpec(memory_space=pl.ANY)
F32 = jnp.float32
BF16 = jnp.bfloat16


class Place:
    def __init__(self):
        pb = lax.axis_index("pb")
        ka = lax.axis_index("ka")
        self.y = lax.div(pb, CORES)
        self.core = lax.rem(pb, CORES)
        self.x = lax.div(ka, NZ)
        self.z = lax.rem(ka, NZ)
        self.sibling = (self.y * CORES + 1 - self.core, ka)

    def over_x(self, step):
        return (self.y * CORES + self.core, self.xs(step) * NZ + self.z)

    def over_y(self, step):
        return (self.ys(step) * CORES + self.core, self.x * NZ + self.z)

    def over_z(self, step):
        return (self.y * CORES + self.core, self.x * NZ + self.zs(step))

    def xs(self, step):
        return lax.rem(self.x + step + NX, NX)

    def ys(self, step):
        return lax.rem(self.y + step + NY, NY)

    def zs(self, step):
        return lax.rem(self.z + step + NZ, NZ)

    def greet(self):
        barrier = pltpu.get_barrier_semaphore()
        neighbours = [self.sibling]
        for step in (1, -1):
            neighbours += [self.over_x(step), self.over_y(step), self.over_z(step)]
        for neighbour in neighbours:
            pl.semaphore_signal(barrier, inc=1, device_id=neighbour, device_id_type=MESH)
        pl.semaphore_wait(barrier, len(neighbours))


class Sender:
    def __init__(self, send_sems, recv_sems):
        self.send_sems = send_sems
        self.recv_sems = recv_sems
        self.copies = []

    def __call__(self, source, target, device):
        index = len(self.copies)
        copy = pltpu.make_async_remote_copy(
            src_ref=source,
            dst_ref=target,
            send_sem=self.send_sems.at[index],
            recv_sem=self.recv_sems.at[index],
            device_id=device,
            device_id_type=MESH,
        )
        copy.start()
        self.copies.append(copy)
        return copy

    def finish(self):
        for copy in self.copies:
            copy.wait_send()


def half_of(core, size):
    return pl.ds(pl.multiple_of(core * size, size), size)


GATHER_COPIES = 46


def gather_kernel(
    q_ref, do_ref, k_ref, v_ref, out_ref, lse_ref, list_ref, count_ref,
    q_all, do_all, st_all, k_all, v_all, list_all, count_all,
    do_buf, out_buf, lse_buf, st_buf, send_sems, recv_sems, local_sems,
):
    me = Place()
    x, y, z, core = me.x, me.y, me.z, me.core
    every = slice(None)
    rows = half_of(core, HALF)
    mine = half_of(core, COLS)
    theirs = half_of(1 - core, COLS)

    owns = [
        pltpu.make_async_copy(q_ref.at[every, mine], q_all.at[z, core], local_sems.at[0]),
        pltpu.make_async_copy(do_ref.at[every, mine], do_all.at[z, core], local_sems.at[1]),
        pltpu.make_async_copy(k_ref.at[every, mine], k_all.at[y, x, rows], local_sems.at[2]),
        pltpu.make_async_copy(v_ref.at[every, mine], v_all.at[x, y, rows], local_sems.at[3]),
        pltpu.make_async_copy(list_ref, list_all.at[core], local_sems.at[4]),
        pltpu.make_async_copy(count_ref, count_all.at[core], local_sems.at[8]),
    ]
    for own in owns:
        own.start()
    loads = [
        pltpu.make_async_copy(do_ref, do_buf, local_sems.at[5]),
        pltpu.make_async_copy(out_ref, out_buf, local_sems.at[6]),
        pltpu.make_async_copy(lse_ref, lse_buf, local_sems.at[7]),
    ]
    for load in loads:
        load.start()
    me.greet()
    send = Sender(send_sems, recv_sems)
    up, down = me.over_z(1), me.over_z(-1)

    k_swap = send(k_ref.at[every, theirs], k_all.at[y, x, rows], me.sibling)
    v_swap = send(v_ref.at[every, theirs], v_all.at[x, y, rows], me.sibling)
    q_swap = send(q_ref.at[every, theirs], q_all.at[z, core], me.sibling)
    do_swap = send(do_ref.at[every, theirs], do_all.at[z, core], me.sibling)
    list_swap = send(list_ref, list_all.at[core], me.sibling)
    count_swap = send(count_ref, count_all.at[core], me.sibling)

    q_first = [send(q_ref.at[every, mine], q_all.at[z, core], up)]
    do_first = [send(do_ref.at[every, mine], do_all.at[z, core], down)]
    for own in owns:
        own.wait()
    k_swap.wait_recv()
    k_right = send(k_all.at[y, x], k_all.at[y, x], me.over_x(1))
    k_left = send(k_all.at[y, x], k_all.at[y, x], me.over_x(-1))
    v_swap.wait_recv()
    v_right = send(v_all.at[x, y], v_all.at[x, y], me.over_y(1))
    v_left = send(v_all.at[x, y], v_all.at[x, y], me.over_y(-1))
    q_swap.wait_recv()
    other_q = q_all.at[z, 1 - core]
    q_first.append(send(other_q, other_q, up))
    do_swap.wait_recv()
    other_do = do_all.at[z, 1 - core]
    do_first.append(send(other_do, other_do, down))
    do_up = [send(do_all.at[z], do_all.at[z], up)]
    q_down = [send(q_all.at[z], q_all.at[z], down)]

    for load in loads:
        load.wait()
    products = do_buf[...].astype(F32) * out_buf[...].astype(F32)
    high = products.astype(BF16)
    low = (products - high.astype(F32)).astype(BF16)
    head = lax.broadcasted_iota(jnp.int32, (HEADS, WIDTH), 0) * 64
    feature = lax.broadcasted_iota(jnp.int32, (HEADS, WIDTH), 1)
    member = jnp.where((feature >= head) & (feature < head + 64), 1.0, 0.0).astype(BF16)
    over_features = (((1,), (1,)), ((), ()))
    delta = lax.dot_general(member, high, over_features, preferred_element_type=F32)
    delta = delta + lax.dot_general(member, low, over_features, preferred_element_type=F32)
    for side in range(CORES):
        heads = slice(side * OWN_HEADS, side * OWN_HEADS + OWN_HEADS)
        st_buf[side, 0:OWN_HEADS, :] = lse_buf[heads, :] * LOG2E
        st_buf[side, OWN_HEADS : 2 * OWN_HEADS, :] = delta[heads, :]
    st_own = pltpu.make_async_copy(st_buf.at[core], st_all.at[z, core], local_sems.at[0])
    st_own.start()
    st_swap = send(st_buf.at[1 - core], st_all.at[z, core], me.sibling)

    upper, lower = pl.ds(0, HALF), pl.ds(HALF, HALF)
    k_right.wait_recv()
    k_far = [k_all.at[y, me.xs(-1), upper]]
    k_far = [send(k_far[0], k_far[0], me.over_x(1))]
    v_right.wait_recv()
    v_part = v_all.at[x, me.ys(-1), upper]
    v_far = [send(v_part, v_part, me.over_y(1))]
    k_left.wait_recv()
    k_part = k_all.at[y, me.xs(1), lower]
    k_far.append(send(k_part, k_part, me.over_x(-1)))
    v_left.wait_recv()
    v_part = v_all.at[x, me.ys(1), lower]
    v_far.append(send(v_part, v_part, me.over_y(-1)))

    st_swap.wait_recv()
    st_own.wait()
    st_up = [send(st_all.at[z], st_all.at[z], up)]
    st_down = [send(st_all.at[z], st_all.at[z], down)]

    for copy in k_far:
        copy.wait_recv()
    k_right = send(k_all.at[y], k_all.at[y], me.over_y(1))
    k_left = send(k_all.at[y], k_all.at[y], me.over_y(-1))
    for copy in v_far:
        copy.wait_recv()
    v_right = send(v_all.at[x], v_all.at[x], me.over_x(1))
    v_left = send(v_all.at[x], v_all.at[x], me.over_x(-1))

    def forward_up(hop, blocks, copies):
        for copy in copies[hop - 1] if isinstance(copies[hop - 1], list) else [copies[hop - 1]]:
            copy.wait_recv()
        block = blocks.at[me.zs(-hop)]
        copies.append(send(block, block, up))

    def forward_down(hop, blocks, copies):
        for copy in copies[hop - 1] if isinstance(copies[hop - 1], list) else [copies[hop - 1]]:
            copy.wait_recv()
        block = blocks.at[me.zs(hop)]
        copies.append(send(block, block, down))

    q_up, do_down = [q_first], [do_first]
    forward_up(1, q_all, q_up)
    forward_down(1, do_all, do_down)
    forward_up(1, do_all, do_up)
    forward_down(1, q_all, q_down)
    forward_up(1, st_all, st_up)
    forward_down(1, st_all, st_down)

    def across(blocks, start, low, device):
        part = blocks.at[start, pl.ds(low, 2)]
        return send(part, part, device)

    k_right.wait_recv()
    k_far = [across(k_all, me.ys(-1), 0, me.over_y(1))]
    v_right.wait_recv()
    v_far = [across(v_all, me.xs(-1), 0, me.over_x(1))]
    k_left.wait_recv()
    k_far.append(across(k_all, me.ys(1), 2, me.over_y(-1)))
    v_left.wait_recv()
    v_far.append(across(v_all, me.xs(1), 2, me.over_x(-1)))

    forward_up(2, q_all, q_up)
    forward_down(2, do_all, do_down)
    forward_up(2, do_all, do_up)
    forward_down(2, q_all, q_down)
    forward_up(2, st_all, st_up)
    forward_down(2, st_all, st_down)

    forward_up(3, q_all, q_up)
    forward_down(3, do_all, do_down)
    forward_up(3, st_all, st_up)
    for copy in k_far + v_far:
        copy.wait_recv()
    do_up[2].wait_recv()
    q_down[2].wait_recv()
    st_down[2].wait_recv()
    list_swap.wait_recv()
    count_swap.wait_recv()
    q_up[3].wait_recv()
    do_down[3].wait_recv()
    st_up[3].wait_recv()
    send.finish()
    assert len(send.copies) == GATHER_COPIES, len(send.copies)


def gather(q, do, k, v, out, lse, lists, counts):
    return pl.pallas_call(
        gather_kernel,
        out_shape=[
            jax.ShapeDtypeStruct((NZ, CORES, BLK, COLS), BF16),
            jax.ShapeDtypeStruct((NZ, CORES, BLK, COLS), BF16),
            jax.ShapeDtypeStruct((NZ, CORES, 2 * OWN_HEADS, BLK), F32),
            jax.ShapeDtypeStruct((NY, NX, BLK, COLS), BF16),
            jax.ShapeDtypeStruct((NX, NY, BLK, COLS), BF16),
            jax.ShapeDtypeStruct((CORES, 2 * SLOTS, KEY_SHARDS), jnp.int32),
            jax.ShapeDtypeStruct((CORES, 1, KEY_SHARDS), jnp.int32),
        ],
        in_specs=[ANY] * 8,
        out_specs=[ANY] * 7,
        scratch_shapes=[
            pltpu.VMEM((BLK, WIDTH), BF16),
            pltpu.VMEM((BLK, WIDTH), BF16),
            pltpu.VMEM((HEADS, BLK), F32),
            pltpu.VMEM((CORES, 2 * OWN_HEADS, BLK), F32),
            pltpu.SemaphoreType.DMA((GATHER_COPIES,)),
            pltpu.SemaphoreType.DMA((GATHER_COPIES,)),
            pltpu.SemaphoreType.DMA((9,)),
        ],
        compiler_params=pltpu.CompilerParams(
            collective_id=0, has_side_effects=True, vmem_limit_bytes=VMEM_LIMIT
        ),
        name="gather_blocks",
    )(q, do, k, v, out, lse, lists, counts)


def pair_kernel(
    lists, counts, place, q_all, do_all, st_all, k_all, v_all,
    dq_out, dk_out, dv_out,
    q_buf, do_buf, st_buf, k_buf, v_buf, k_turned, dq_sum, dk_sum, dv_sum, dq_stage, dk_stage, dv_stage, zeros,
    listed, filled, flat, in_sems, out_sems, zero_sems, dq_sems,
):
    x = place[0]
    z = place[1]
    for block in range(KEY_BLOCKS):
        filled[block] = 0
    for owner in range(CORES):
        for column in range(NX):
            shard = column * NZ + z

            def enlist(slot, carry, owner=owner, column=column, shard=shard):
                query = lists[owner, slot, shard]
                block = lists[owner, SLOTS + slot, shard] * NX + column
                have = filled[block]
                where = lax.rem(query, NZ) * CORES + owner
                listed[block * BUCKET + have] = block * QUERY_BLOCKS + where
                filled[block] = have + jnp.where(lax.div(query, NZ) == x, 1, 0)
                return carry

            lax.fori_loop(0, counts[owner, 0, shard], enlist, 0)
    zeros[...] = jnp.zeros_like(zeros)
    total = jnp.int32(0)
    for block in range(KEY_BLOCKS):

        def append(slot, position, block=block):
            flat[position] = listed[block * BUCKET + slot]
            return position + 1

        total = lax.fori_loop(0, filled[block], append, total)
        up, across = divmod(block, NX)

        @pl.when(filled[block] == 0)
        def _(up=up, across=across):
            pltpu.make_async_copy(zeros, dk_out.at[up, across], zero_sems.at[0]).start()
            pltpu.make_async_copy(zeros, dv_out.at[across, up], zero_sems.at[1]).start()

    def fetches(index, slot):
        entry = flat[index]
        block = lax.div(entry, QUERY_BLOCKS)
        up, across = lax.div(block, NX), lax.rem(block, NX)
        query = lax.rem(entry, QUERY_BLOCKS)
        return [
            pltpu.make_async_copy(k_all.at[up, across], k_buf.at[slot], in_sems.at[slot, 0]),
            pltpu.make_async_copy(q_all.at[query], q_buf.at[slot], in_sems.at[slot, 1]),
            pltpu.make_async_copy(st_all.at[query], st_buf.at[slot], in_sems.at[slot, 2]),
            pltpu.make_async_copy(v_all.at[across, up], v_buf.at[slot], in_sems.at[slot, 3]),
            pltpu.make_async_copy(do_all.at[query], do_buf.at[slot], in_sems.at[slot, 4]),
        ]

    @pl.when(total > 0)
    def _():
        for fetch in fetches(0, 0):
            fetch.start()

    def clear(query, carry):
        dq_sum[query] = jnp.zeros((COLS, BLK), F32)
        return carry

    lax.fori_loop(0, QUERY_BLOCKS, clear, 0)

    lane = lax.broadcasted_iota(jnp.int32, (1, 128), 1)
    first_half = jnp.where(lane < 64, 1.0, 0.0).astype(BF16)
    second_half = jnp.where(lane < 64, 0.0, 1.0).astype(BF16)
    nt = (((1,), (1,)), ((), ()))
    nn = (((1,), (0,)), ((), ()))

    def flush_copies(slot, block):
        up, across = lax.div(block, NX), lax.rem(block, NX)
        return [
            pltpu.make_async_copy(dk_stage.at[slot], dk_out.at[up, across], out_sems.at[slot, 0]),
            pltpu.make_async_copy(dv_stage.at[slot], dv_out.at[across, up], out_sems.at[slot, 1]),
        ]

    def step(index, flushed):
        slot = lax.rem(index, 2)
        block = lax.div(flat[index], QUERY_BLOCKS)
        query = lax.rem(flat[index], QUERY_BLOCKS)
        before = jnp.where(index > 0, lax.div(flat[jnp.maximum(index - 1, 0)], QUERY_BLOCKS), -1)
        after = jnp.where(
            index + 1 < total, lax.div(flat[jnp.minimum(index + 1, total - 1)], QUERY_BLOCKS), -1
        )

        @pl.when(index + 1 < total)
        def _():
            for fetch in fetches(index + 1, 1 - slot):
                fetch.start()

        for fetch in fetches(index, slot):
            fetch.wait()

        @pl.when(before != block)
        def _():
            dk_sum[...] = jnp.zeros_like(dk_sum)
            dv_sum[...] = jnp.zeros_like(dv_sum)
            for pair in range(HEAD_PAIRS):
                lanes = slice(pair * 128, pair * 128 + 128)
                turned = jnp.transpose(k_buf[slot, :, lanes].astype(F32)).astype(BF16)
                k_turned[lanes, :] = turned

        for pair in range(HEAD_PAIRS):
            lanes = slice(pair * 128, pair * 128 + 128)
            keys = k_buf[slot, :, lanes]
            values = v_buf[slot, :, lanes]
            queries = q_buf[slot, :, lanes]
            douts = do_buf[slot, :, lanes]
            q_two = jnp.concatenate([queries * first_half, queries * second_half], axis=0)
            do_two = jnp.concatenate([douts * first_half, douts * second_half], axis=0)
            scores = lax.dot_general(keys, q_two, nt, preferred_element_type=F32)
            dprob = lax.dot_general(values, do_two, nt, preferred_element_type=F32)
            probs, dscores = [], []
            for side in range(2):
                head = 2 * pair + side
                cut = slice(side * BLK, side * BLK + BLK)
                lse = st_buf[slot, head : head + 1, :]
                delta = st_buf[slot, OWN_HEADS + head : OWN_HEADS + head + 1, :]
                prob = jnp.exp2(scores[:, cut] * (SCALE * LOG2E) - lse)
                probs.append(prob.astype(BF16))
                dscores.append((prob * (dprob[:, cut] - delta)).astype(BF16))
            dv_sum[:, lanes] += lax.dot_general(
                jnp.concatenate(probs, axis=1), do_two, nn, preferred_element_type=F32
            )
            dk_sum[:, lanes] += lax.dot_general(
                jnp.concatenate(dscores, axis=1), q_two, nn, preferred_element_type=F32
            )
            turned = k_turned[lanes, :]
            for side in range(2):
                low = pair * 128 + side * 64
                dq_sum[query, low : low + 64, :] += lax.dot_general(
                    turned[side * 64 : side * 64 + 64], dscores[side], nn, preferred_element_type=F32
                )

        @pl.when(after != block)
        def _():
            stage = lax.rem(flushed, 2)

            @pl.when(flushed >= 2)
            def _():
                for copy in flush_copies(stage, block):
                    copy.wait()

            dk_stage[stage] = (dk_sum[...] * SCALE).astype(BF16)
            dv_stage[stage] = dv_sum[...].astype(BF16)
            for copy in flush_copies(stage, block):
                copy.start()

        return flushed + jnp.where(after != block, 1, 0)

    flushed = lax.fori_loop(0, total, step, 0)

    def turn_in(query, carry):
        dq_stage[query] = (dq_sum[query] * SCALE).astype(BF16)
        pltpu.make_async_copy(dq_stage.at[query], dq_out.at[query], dq_sems.at[query]).start()
        return carry

    lax.fori_loop(0, QUERY_BLOCKS, turn_in, 0)
    for slot in range(2):

        @pl.when(flushed > slot)
        def _(slot=slot):
            for copy in flush_copies(slot, 0):
                copy.wait()

    for block in range(KEY_BLOCKS):
        up, across = divmod(block, NX)

        @pl.when(filled[block] == 0)
        def _(up=up, across=across):
            pltpu.make_async_copy(zeros, dk_out.at[up, across], zero_sems.at[0]).wait()
            pltpu.make_async_copy(zeros, dv_out.at[across, up], zero_sems.at[1]).wait()

    def finish(query, carry):
        pltpu.make_async_copy(dq_stage.at[query], dq_out.at[query], dq_sems.at[query]).wait()
        return carry

    lax.fori_loop(0, QUERY_BLOCKS, finish, 0)


def pairs_over_blocks(q_all, do_all, st_all, k_all, v_all, lists, counts, place):
    smem = pl.BlockSpec(memory_space=pltpu.SMEM)
    block_pair = pltpu.VMEM((2, BLK, COLS), BF16)
    return pl.pallas_call(
        pair_kernel,
        out_shape=[
            jax.ShapeDtypeStruct((QUERY_BLOCKS, COLS, BLK), BF16),
            jax.ShapeDtypeStruct((NY, NX, BLK, COLS), BF16),
            jax.ShapeDtypeStruct((NX, NY, BLK, COLS), BF16),
        ],
        in_specs=[smem] * 3 + [ANY] * 5,
        out_specs=[ANY] * 3,
        scratch_shapes=[
            block_pair,
            block_pair,
            pltpu.VMEM((2, 2 * OWN_HEADS, BLK), F32),
            block_pair,
            block_pair,
            pltpu.VMEM((COLS, BLK), BF16),
            pltpu.VMEM((QUERY_BLOCKS, COLS, BLK), F32),
            pltpu.VMEM((BLK, COLS), F32),
            pltpu.VMEM((BLK, COLS), F32),
            pltpu.VMEM((QUERY_BLOCKS, COLS, BLK), BF16),
            block_pair,
            block_pair,
            pltpu.VMEM((BLK, COLS), BF16),
            pltpu.SMEM((KEY_BLOCKS * BUCKET,), jnp.int32),
            pltpu.SMEM((KEY_BLOCKS,), jnp.int32),
            pltpu.SMEM((KEY_BLOCKS * QUERY_BLOCKS,), jnp.int32),
            pltpu.SemaphoreType.DMA((2, 5)),
            pltpu.SemaphoreType.DMA((2, 2)),
            pltpu.SemaphoreType.DMA((2,)),
            pltpu.SemaphoreType.DMA((QUERY_BLOCKS,)),
        ],
        compiler_params=pltpu.CompilerParams(vmem_limit_bytes=VMEM_LIMIT),
        name="used_pairs",
    )(
        lists,
        counts,
        place,
        q_all.reshape(QUERY_BLOCKS, BLK, COLS),
        do_all.reshape(QUERY_BLOCKS, BLK, COLS),
        st_all.reshape(QUERY_BLOCKS, 2 * OWN_HEADS, BLK),
        k_all,
        v_all,
    )


REDUCE_COPIES = 33
ROW_STEP = 16


def reduce_kernel(
    dq_part, dk_part, dv_part,
    gq_out, gk_out, gv_out,
    dq_own, dq_in_up, dq_in_down, k_own, v_own,
    k_far_a, k_far_b, v_far_a, v_far_b, k_near_a, k_near_b, v_near_a, v_near_b,
    k_mid, v_mid, k_end_far_a, k_end_far_b, v_end_far_a, v_end_far_b,
    k_end_a, k_end_b, v_end_a, v_end_b, gq_buf, gk_buf, gv_buf,
    send_sems, recv_sems, local_sems,
):
    me = Place()
    x, y, z, core = me.x, me.y, me.z, me.core
    every = slice(None)
    loads = {}
    for order, step in enumerate((3, -3, 2, -2, 1, -1, 0)):
        loads["q", step] = pltpu.make_async_copy(
            dq_part.at[me.zs(step)], dq_own.at[me.zs(step)], local_sems.at[order]
        )
    for order, step in enumerate((1, -1, 0)):
        loads["k", step] = pltpu.make_async_copy(
            dk_part.at[me.ys(step)], k_own.at[me.ys(step)], local_sems.at[7 + order]
        )
        loads["v", step] = pltpu.make_async_copy(
            dv_part.at[me.xs(step)], v_own.at[me.xs(step)], local_sems.at[10 + order]
        )
    for load in loads.values():
        load.start()
    me.greet()
    send = Sender(send_sems, recv_sems)
    up, down = me.over_z(1), me.over_z(-1)

    def add_rows(total, terms, count):
        def one(index, carry):
            at = pl.ds(pl.multiple_of(index * ROW_STEP, ROW_STEP), ROW_STEP)
            value = terms[0][at, :].astype(F32)
            for term in terms[1:]:
                value = value + term[at, :].astype(F32)
            total[at, :] = value.astype(total.dtype)
            return carry

        lax.fori_loop(0, count // ROW_STEP, one, 0, unroll=4)

    far = me.zs(4)
    arrive = {
        ("up", 0, 1): send(dq_part.at[far, 0], dq_in_up.at[0, 0], up),
        ("down", 1, 1): send(dq_part.at[far, 1], dq_in_down.at[0, 1], down),
    }
    far_y, far_x = me.ys(2), me.xs(2)
    kf_a = send(dk_part.at[far_y, pl.ds(0, 2)], k_far_a, me.over_y(1))
    kf_b = send(dk_part.at[far_y, pl.ds(2, 2)], k_far_b, me.over_y(-1))
    vf_a = send(dv_part.at[far_x, pl.ds(0, 2)], v_far_a, me.over_x(1))
    vf_b = send(dv_part.at[far_x, pl.ds(2, 2)], v_far_b, me.over_x(-1))
    arrive["up", 1, 2] = send(dq_part.at[me.zs(3), 1], dq_in_up.at[1, 1], up)
    arrive["down", 0, 2] = send(dq_part.at[me.zs(-3), 0], dq_in_down.at[1, 0], down)

    def hop_q(direction, shard, hop):
        if direction == "up":
            step, inbox, device = 4 - hop, dq_in_up, up
        else:
            step, inbox, device = hop - 4, dq_in_down, down
        own = dq_own.at[me.zs(step), shard]
        arrive[direction, shard, hop].wait_recv()
        add_rows(own, [own, inbox.at[hop - 1, shard]], COLS)
        arrive[direction, shard, hop + 1] = send(own, inbox.at[hop, shard], device)

    for load in loads.values():
        load.wait()
    hop_q("up", 0, 1)
    hop_q("down", 1, 1)

    def onward(own, place, base, inbox, arrival):
        arrival.wait_recv()
        for row in range(2):
            part = own.at[place, base + row]
            add_rows(part, [part, inbox.at[row]], BLK)

    onward(k_own, me.ys(1), 0, k_far_a, kf_a)
    kn_a = send(k_own.at[me.ys(1)], k_near_a, me.over_y(1))
    onward(v_own, me.xs(1), 0, v_far_a, vf_a)
    vn_a = send(v_own.at[me.xs(1)], v_near_a, me.over_x(1))
    onward(k_own, me.ys(-1), 2, k_far_b, kf_b)
    kn_b = send(k_own.at[me.ys(-1)], k_near_b, me.over_y(-1))
    onward(v_own, me.xs(-1), 2, v_far_b, vf_b)
    vn_b = send(v_own.at[me.xs(-1)], v_near_b, me.over_x(-1))
    hop_q("up", 1, 2)
    hop_q("down", 0, 2)
    hop_q("up", 0, 2)
    hop_q("down", 1, 2)
    hop_q("up", 1, 3)
    hop_q("down", 0, 3)
    hop_q("up", 0, 3)
    hop_q("down", 1, 3)

    for arrival in (kn_a, kn_b):
        arrival.wait_recv()
    for row in range(4):
        add_rows(k_mid.at[row], [k_own.at[y, row], k_near_a.at[row], k_near_b.at[row]], BLK)
    half_rows = (pl.ds(0, HALF), pl.ds(HALF, HALF))
    ke_a = send(k_mid.at[far_x, half_rows[0]], k_end_far_a, me.over_x(1))
    ke_b = send(k_mid.at[far_x, half_rows[1]], k_end_far_b, me.over_x(-1))
    for arrival in (vn_a, vn_b):
        arrival.wait_recv()
    for row in range(4):
        add_rows(v_mid.at[row], [v_own.at[x, row], v_near_a.at[row], v_near_b.at[row]], BLK)
    ve_a = send(v_mid.at[far_y, half_rows[0]], v_end_far_a, me.over_y(1))
    ve_b = send(v_mid.at[far_y, half_rows[1]], v_end_far_b, me.over_y(-1))

    def last(middle, place, half, inbox, arrival, target, device):
        arrival.wait_recv()
        part = middle.at[place, half_rows[half]]
        add_rows(part, [part, inbox], HALF)
        return send(middle.at[place], target, device)

    kz_a = last(k_mid, me.xs(1), 0, k_end_far_a, ke_a, k_end_a, me.over_x(1))
    kz_b = last(k_mid, me.xs(-1), 1, k_end_far_b, ke_b, k_end_b, me.over_x(-1))
    vz_a = last(v_mid, me.ys(1), 0, v_end_far_a, ve_a, v_end_a, me.over_y(1))
    vz_b = last(v_mid, me.ys(-1), 1, v_end_far_b, ve_b, v_end_b, me.over_y(-1))

    mine = half_of(core, COLS)
    swaps, stores = [], []
    for direction in ("up", "down"):
        for shard in range(CORES):
            arrive[direction, shard, 4].wait_recv()
    for shard in range(CORES):
        for tile in range(COLS // 128):
            at = pl.ds(tile * 128, 128)
            value = (
                dq_own[z, shard, at, :].astype(F32)
                + dq_in_up[3, shard, at, :].astype(F32)
                + dq_in_down[3, shard, at, :].astype(F32)
            )
            gq_buf[shard, :, at] = jnp.transpose(value).astype(BF16)
    swaps.append(send(gq_buf.at[1 - core], gq_out.at[every, mine], me.sibling))
    stores.append(pltpu.make_async_copy(gq_buf.at[core], gq_out.at[every, mine], local_sems.at[0]))
    stores[-1].start()

    own_rows, other_rows = half_of(core, HALF), half_of(1 - core, HALF)
    for arrival in (kz_a, kz_b):
        arrival.wait_recv()
    add_rows(gk_buf, [k_mid.at[x], k_end_a, k_end_b], BLK)
    swaps.append(send(gk_buf.at[other_rows], gk_out.at[every, mine], me.sibling))
    stores.append(pltpu.make_async_copy(gk_buf.at[own_rows], gk_out.at[every, mine], local_sems.at[1]))
    stores[-1].start()
    for arrival in (vz_a, vz_b):
        arrival.wait_recv()
    add_rows(gv_buf, [v_mid.at[y], v_end_a, v_end_b], BLK)
    swaps.append(send(gv_buf.at[other_rows], gv_out.at[every, mine], me.sibling))
    stores.append(pltpu.make_async_copy(gv_buf.at[own_rows], gv_out.at[every, mine], local_sems.at[2]))
    stores[-1].start()
    for store in stores:
        store.wait()
    for swap in swaps:
        swap.wait_recv()
    send.finish()
    assert len(send.copies) == REDUCE_COPIES, len(send.copies)


def reduce_parts(dq_part, dk_part, dv_part):
    line = pltpu.VMEM((4, 4, BLK, COLS), BF16)
    two = pltpu.VMEM((2, BLK, COLS), BF16)
    four = pltpu.VMEM((4, BLK, COLS), BF16)
    half = pltpu.VMEM((HALF, COLS), BF16)
    one = pltpu.VMEM((BLK, COLS), BF16)
    inbox = pltpu.VMEM((4, CORES, COLS, BLK), BF16)
    return pl.pallas_call(
        reduce_kernel,
        out_shape=[
            jax.ShapeDtypeStruct((BLK, WIDTH), BF16),
            jax.ShapeDtypeStruct((HALF, WIDTH), BF16),
            jax.ShapeDtypeStruct((HALF, WIDTH), BF16),
        ],
        in_specs=[ANY] * 3,
        out_specs=[ANY] * 3,
        scratch_shapes=[
            pltpu.VMEM((NZ, CORES, COLS, BLK), BF16),
            inbox, inbox,
            line, line,
            two, two, two, two,
            four, four, four, four,
            four, four,
            half, half, half, half,
            one, one, one, one,
            pltpu.VMEM((CORES, BLK, COLS), BF16), one, one,
            pltpu.SemaphoreType.DMA((REDUCE_COPIES,)),
            pltpu.SemaphoreType.DMA((REDUCE_COPIES,)),
            pltpu.SemaphoreType.DMA((13,)),
        ],
        compiler_params=pltpu.CompilerParams(
            collective_id=1, has_side_effects=True, vmem_limit_bytes=VMEM_LIMIT
        ),
        name="reduce_parts",
    )(dq_part.reshape(NZ, CORES, COLS, BLK), dk_part, dv_part)


def body(q, k, v, out, do, lse, block_pairs, counts):
    ka = lax.axis_index("ka")
    place = jnp.stack([ka // NZ, ka % NZ]).astype(jnp.int32)
    lists = block_pairs.transpose(0, 2, 3, 1).reshape(2 * SLOTS, KEY_SHARDS)
    gathered = gather(q, do, k, v, out, lse, lists, counts)
    parts = pairs_over_blocks(*gathered, place)
    return tuple(reduce_parts(*parts))


def solution(mesh):
    placed = (
        P(("pb", "ka"), None),
        P(("ka", "pb"), None),
        P(("ka", "pb"), None),
        P(("pb", "ka"), None),
        P(("pb", "ka"), None),
        P(None, ("pb", "ka")),
        P("pb", None, None, None),
        P("pb", None),
    )
    return jax.shard_map(
        body,
        mesh=mesh,
        in_specs=placed,
        out_specs=(P(("pb", "ka"), None), P(("ka", "pb"), None), P(("ka", "pb"), None)),
        check_vma=False,
    )
```

```python
import jax
import jax.numpy as jnp
from jax import lax
from jax.experimental import pallas as pl
from jax.experimental.pallas import tpu as pltpu
from jax.sharding import PartitionSpec as P

NX, NY, NZ, CORES = 4, 4, 8, 2
HEADS = 16
OWN_HEADS = HEADS // CORES
BLK = 128
HALF = BLK // 2
WIDTH = 1024
COLS = WIDTH // CORES
HEAD_PAIRS = COLS // 128
SLOTS = 24
KEY_SHARDS = NX * NZ
QUERY_BLOCKS = NZ * CORES
KEY_BLOCKS = NX * NY
BUCKET = 32
SCALE = 64**-0.5
LOG2E = 1.4426950408889634
VMEM_LIMIT = 60 << 20
MESH = pl.DeviceIdType.MESH
ANY = pl.BlockSpec(memory_space=pl.ANY)
F32 = jnp.float32
BF16 = jnp.bfloat16


class Place:
    def __init__(self):
        pb = lax.axis_index("pb")
        ka = lax.axis_index("ka")
        self.y = lax.div(pb, CORES)
        self.core = lax.rem(pb, CORES)
        self.x = lax.div(ka, NZ)
        self.z = lax.rem(ka, NZ)
        self.sibling = (self.y * CORES + 1 - self.core, ka)

    def aim(self, crossed, owner):
        if owner is not None:
            return owner
        return 1 - self.core if crossed else self.core

    def over_x(self, step, crossed=0, owner=None):
        return (self.y * CORES + self.aim(crossed, owner), self.xs(step) * NZ + self.z)

    def over_y(self, step, crossed=0, owner=None):
        return (self.ys(step) * CORES + self.aim(crossed, owner), self.x * NZ + self.z)

    def over_z(self, step, crossed=0, owner=None):
        return (self.y * CORES + self.aim(crossed, owner), self.x * NZ + self.zs(step))

    def xs(self, step):
        return lax.rem(self.x + step + NX, NX)

    def ys(self, step):
        return lax.rem(self.y + step + NY, NY)

    def zs(self, step):
        return lax.rem(self.z + step + NZ, NZ)

    def greet(self, both_cores=False):
        barrier = pltpu.get_barrier_semaphore()
        neighbours = [self.sibling]
        for step in (1, -1):
            for crossed in (0, 1) if both_cores else (0,):
                for over in (self.over_x, self.over_y, self.over_z):
                    neighbours.append(over(step, crossed))
        for neighbour in neighbours:
            pl.semaphore_signal(barrier, inc=1, device_id=neighbour, device_id_type=MESH)
        pl.semaphore_wait(barrier, len(neighbours))


class Sender:
    def __init__(self, send_sems, recv_sems):
        self.send_sems = send_sems
        self.recv_sems = recv_sems
        self.copies = []

    def __call__(self, source, target, device, recv_sem=None):
        index = len(self.copies)
        copy = pltpu.make_async_remote_copy(
            src_ref=source,
            dst_ref=target,
            send_sem=self.send_sems.at[index],
            recv_sem=self.recv_sems.at[index] if recv_sem is None else recv_sem,
            device_id=device,
            device_id_type=MESH,
        )
        copy.start()
        self.copies.append(copy)
        return copy

    def finish(self):
        for copy in self.copies:
            copy.wait_send()


def half_of(core, size):
    return pl.ds(pl.multiple_of(core * size, size), size)


GATHER_COPIES = 54


def gather_kernel(
    q_ref, do_ref, k_ref, v_ref, out_ref, lse_ref, list_ref, count_ref,
    q_all, do_all, st_all, k_all, v_all, list_all, count_all,
    do_buf, out_buf, lse_buf, st_buf, send_sems, recv_sems, local_sems,
):
    me = Place()
    x, y, z, core = me.x, me.y, me.z, me.core
    every = slice(None)
    rows = half_of(core, HALF)
    mine = half_of(core, COLS)
    theirs = half_of(1 - core, COLS)

    loads = [
        pltpu.make_async_copy(do_ref, do_buf, local_sems.at[5]),
        pltpu.make_async_copy(out_ref, out_buf, local_sems.at[6]),
        pltpu.make_async_copy(lse_ref, lse_buf, local_sems.at[7]),
    ]
    for load in loads:
        load.start()
    owns = [
        pltpu.make_async_copy(q_ref.at[every, mine], q_all.at[z, core], local_sems.at[0]),
        pltpu.make_async_copy(do_ref.at[every, mine], do_all.at[z, core], local_sems.at[1]),
        pltpu.make_async_copy(k_ref.at[every, mine], k_all.at[y, x, rows], local_sems.at[2]),
        pltpu.make_async_copy(v_ref.at[every, mine], v_all.at[x, y, rows], local_sems.at[3]),
        pltpu.make_async_copy(list_ref, list_all.at[core], local_sems.at[4]),
        pltpu.make_async_copy(count_ref, count_all.at[core], local_sems.at[8]),
    ]
    for own in owns:
        own.start()
    me.greet(both_cores=True)
    send = Sender(send_sems, recv_sems)
    up, down = me.over_z(1), me.over_z(-1)

    def to_both(ref, target, straight, crossed):
        return [
            send(ref.at[every, mine], target, straight),
            send(ref.at[every, theirs], target, crossed),
        ]

    cross_up, cross_down = me.over_z(1, 1), me.over_z(-1, 1)
    q_up = [to_both(q_ref, q_all.at[z, core], up, cross_up)]
    do_down = [to_both(do_ref, do_all.at[z, core], down, cross_down)]
    k_swap = send(k_ref.at[every, theirs], k_all.at[y, x, rows], me.sibling)
    v_swap = send(v_ref.at[every, theirs], v_all.at[x, y, rows], me.sibling)
    k_right = to_both(k_ref, k_all.at[y, x, rows], me.over_x(1), me.over_x(1, 1))
    k_left = to_both(k_ref, k_all.at[y, x, rows], me.over_x(-1), me.over_x(-1, 1))
    v_right = to_both(v_ref, v_all.at[x, y, rows], me.over_y(1), me.over_y(1, 1))
    v_left = to_both(v_ref, v_all.at[x, y, rows], me.over_y(-1), me.over_y(-1, 1))
    do_up = [to_both(do_ref, do_all.at[z, core], up, cross_up)]
    q_down = [to_both(q_ref, q_all.at[z, core], down, cross_down)]
    swaps = [
        send(q_ref.at[every, theirs], q_all.at[z, core], me.sibling),
        send(do_ref.at[every, theirs], do_all.at[z, core], me.sibling),
        send(list_ref, list_all.at[core], me.sibling),
        send(count_ref, count_all.at[core], me.sibling),
    ]

    for load in loads:
        load.wait()
    products = do_buf[...].astype(F32) * out_buf[...].astype(F32)
    high = products.astype(BF16)
    low = (products - high.astype(F32)).astype(BF16)
    head = lax.broadcasted_iota(jnp.int32, (HEADS, WIDTH), 0) * 64
    feature = lax.broadcasted_iota(jnp.int32, (HEADS, WIDTH), 1)
    member = jnp.where((feature >= head) & (feature < head + 64), 1.0, 0.0).astype(BF16)
    over_features = (((1,), (1,)), ((), ()))
    delta = lax.dot_general(member, high, over_features, preferred_element_type=F32)
    delta = delta + lax.dot_general(member, low, over_features, preferred_element_type=F32)
    for side in range(CORES):
        heads = slice(side * OWN_HEADS, side * OWN_HEADS + OWN_HEADS)
        st_buf[side, 0:OWN_HEADS, :] = lse_buf[heads, :] * LOG2E
        st_buf[side, OWN_HEADS : 2 * OWN_HEADS, :] = delta[heads, :]
    for own in owns:
        own.wait()
    st_own = pltpu.make_async_copy(st_buf.at[core], st_all.at[z, core], local_sems.at[0])
    st_own.start()
    swaps.append(send(st_buf.at[1 - core], st_all.at[z, core], me.sibling))
    st_up, st_down = [], []
    for stats, straight, crossed in ((st_up, up, cross_up), (st_down, down, cross_down)):
        stats.append(
            [
                send(st_buf.at[core], st_all.at[z, core], straight),
                send(st_buf.at[1 - core], st_all.at[z, core], crossed),
            ]
        )

    def arrived(*groups):
        for group in groups:
            for copy in group:
                copy.wait_recv()

    upper, lower = pl.ds(0, HALF), pl.ds(HALF, HALF)
    arrived(k_right)
    k_part = k_all.at[y, me.xs(-1), upper]
    k_far = [send(k_part, k_part, me.over_x(1))]
    arrived(v_right)
    v_part = v_all.at[x, me.ys(-1), upper]
    v_far = [send(v_part, v_part, me.over_y(1))]
    arrived(k_left)
    k_part = k_all.at[y, me.xs(1), lower]
    k_far.append(send(k_part, k_part, me.over_x(-1)))
    arrived(v_left)
    v_part = v_all.at[x, me.ys(1), lower]
    v_far.append(send(v_part, v_part, me.over_y(-1)))

    arrived([k_swap], k_far)
    k_right = [send(k_all.at[y], k_all.at[y], me.over_y(1))]
    k_left = [send(k_all.at[y], k_all.at[y], me.over_y(-1))]
    arrived([v_swap], v_far)
    v_right = [send(v_all.at[x], v_all.at[x], me.over_x(1))]
    v_left = [send(v_all.at[x], v_all.at[x], me.over_x(-1))]

    def forward(hop, sign, blocks, copies):
        arrived(copies[hop - 1])
        block = blocks.at[me.zs(-sign * hop)]
        copies.append([send(block, block, up if sign > 0 else down)])

    forward(1, 1, q_all, q_up)
    forward(1, -1, do_all, do_down)
    forward(1, 1, do_all, do_up)
    forward(1, -1, q_all, q_down)
    forward(1, 1, st_all, st_up)
    forward(1, -1, st_all, st_down)

    def across(blocks, start, low, device):
        part = blocks.at[start, pl.ds(low, 2)]
        return send(part, part, device)

    arrived(k_right)
    k_far = [across(k_all, me.ys(-1), 0, me.over_y(1))]
    arrived(v_right)
    v_far = [across(v_all, me.xs(-1), 0, me.over_x(1))]
    arrived(k_left)
    k_far.append(across(k_all, me.ys(1), 2, me.over_y(-1)))
    arrived(v_left)
    v_far.append(across(v_all, me.xs(1), 2, me.over_x(-1)))

    forward(2, 1, q_all, q_up)
    forward(2, -1, do_all, do_down)
    forward(2, 1, do_all, do_up)
    forward(2, -1, q_all, q_down)
    forward(2, 1, st_all, st_up)
    forward(2, -1, st_all, st_down)

    forward(3, 1, q_all, q_up)
    forward(3, -1, do_all, do_down)
    forward(3, 1, st_all, st_up)
    arrived(k_far, v_far, swaps, do_up[2], q_down[2], st_down[2], q_up[3], do_down[3], st_up[3])
    st_own.wait()
    send.finish()
    assert len(send.copies) == GATHER_COPIES, len(send.copies)


def gather(q, do, k, v, out, lse, lists, counts):
    return pl.pallas_call(
        gather_kernel,
        out_shape=[
            jax.ShapeDtypeStruct((NZ, CORES, BLK, COLS), BF16),
            jax.ShapeDtypeStruct((NZ, CORES, BLK, COLS), BF16),
            jax.ShapeDtypeStruct((NZ, CORES, 2 * OWN_HEADS, BLK), F32),
            jax.ShapeDtypeStruct((NY, NX, BLK, COLS), BF16),
            jax.ShapeDtypeStruct((NX, NY, BLK, COLS), BF16),
            jax.ShapeDtypeStruct((CORES, 2 * SLOTS, KEY_SHARDS), jnp.int32),
            jax.ShapeDtypeStruct((CORES, 1, KEY_SHARDS), jnp.int32),
        ],
        in_specs=[ANY] * 8,
        out_specs=[ANY] * 7,
        scratch_shapes=[
            pltpu.VMEM((BLK, WIDTH), BF16),
            pltpu.VMEM((BLK, WIDTH), BF16),
            pltpu.VMEM((HEADS, BLK), F32),
            pltpu.VMEM((CORES, 2 * OWN_HEADS, BLK), F32),
            pltpu.SemaphoreType.DMA((GATHER_COPIES,)),
            pltpu.SemaphoreType.DMA((GATHER_COPIES,)),
            pltpu.SemaphoreType.DMA((9,)),
        ],
        compiler_params=pltpu.CompilerParams(
            collective_id=0, has_side_effects=True, vmem_limit_bytes=VMEM_LIMIT
        ),
        name="gather_blocks",
    )(q, do, k, v, out, lse, lists, counts)


def pair_kernel(
    lists, counts, place, q_all, do_all, st_all, k_all, v_all,
    dq_out, dk_out, dv_out,
    q_buf, do_buf, st_buf, k_buf, v_buf, k_turned, p_buf, ds_buf, dq_sum, dk_sum, dv_sum, dq_stage, dk_stage, dv_stage, zeros,
    listed, filled, flat, in_sems, out_sems, zero_sems, dq_sems,
):
    x = place[0]
    z = place[1]
    for block in range(KEY_BLOCKS):
        filled[block] = 0
    for owner in range(CORES):
        for column in range(NX):
            shard = column * NZ + z

            def enlist(slot, carry, owner=owner, column=column, shard=shard):
                query = lists[owner, slot, shard]
                block = lists[owner, SLOTS + slot, shard] * NX + column
                have = filled[block]
                where = lax.rem(query, NZ) * CORES + owner
                listed[block * BUCKET + have] = block * QUERY_BLOCKS + where
                filled[block] = have + jnp.where(lax.div(query, NZ) == x, 1, 0)
                return carry

            lax.fori_loop(0, counts[owner, 0, shard], enlist, 0)
    zeros[...] = jnp.zeros_like(zeros)
    total = jnp.int32(0)
    for block in range(KEY_BLOCKS):

        def append(slot, position, block=block):
            flat[position] = listed[block * BUCKET + slot]
            return position + 1

        total = lax.fori_loop(0, filled[block], append, total)
        up, across = divmod(block, NX)

        @pl.when(filled[block] == 0)
        def _(up=up, across=across):
            pltpu.make_async_copy(zeros, dk_out.at[up, across], zero_sems.at[0]).start()
            pltpu.make_async_copy(zeros, dv_out.at[across, up], zero_sems.at[1]).start()

    def fetches(index, slot):
        entry = flat[index]
        block = lax.div(entry, QUERY_BLOCKS)
        up, across = lax.div(block, NX), lax.rem(block, NX)
        query = lax.rem(entry, QUERY_BLOCKS)
        return [
            pltpu.make_async_copy(k_all.at[up, across], k_buf.at[slot], in_sems.at[slot, 0]),
            pltpu.make_async_copy(q_all.at[query], q_buf.at[slot], in_sems.at[slot, 1]),
            pltpu.make_async_copy(st_all.at[query], st_buf.at[slot], in_sems.at[slot, 2]),
            pltpu.make_async_copy(v_all.at[across, up], v_buf.at[slot], in_sems.at[slot, 3]),
            pltpu.make_async_copy(do_all.at[query], do_buf.at[slot], in_sems.at[slot, 4]),
        ]

    @pl.when(total > 0)
    def _():
        for fetch in fetches(0, 0):
            fetch.start()

    def clear(query, carry):
        dq_sum[query] = jnp.zeros((COLS, BLK), F32)
        return carry

    lax.fori_loop(0, QUERY_BLOCKS, clear, 0)

    lane = lax.broadcasted_iota(jnp.int32, (1, 128), 1)
    first_half = jnp.where(lane < 64, 1.0, 0.0).astype(BF16)
    second_half = jnp.where(lane < 64, 0.0, 1.0).astype(BF16)
    nt = (((1,), (1,)), ((), ()))
    nn = (((1,), (0,)), ((), ()))

    def flush_copies(slot, block):
        up, across = lax.div(block, NX), lax.rem(block, NX)
        return [
            pltpu.make_async_copy(dk_stage.at[slot], dk_out.at[up, across], out_sems.at[slot, 0]),
            pltpu.make_async_copy(dv_stage.at[slot], dv_out.at[across, up], out_sems.at[slot, 1]),
        ]

    def step(index, flushed):
        slot = lax.rem(index, 2)
        block = lax.div(flat[index], QUERY_BLOCKS)
        query = lax.rem(flat[index], QUERY_BLOCKS)
        before = jnp.where(index > 0, lax.div(flat[jnp.maximum(index - 1, 0)], QUERY_BLOCKS), -1)
        after = jnp.where(
            index + 1 < total, lax.div(flat[jnp.minimum(index + 1, total - 1)], QUERY_BLOCKS), -1
        )

        @pl.when(index + 1 < total)
        def _():
            for fetch in fetches(index + 1, 1 - slot):
                fetch.start()

        for fetch in fetches(index, slot):
            fetch.wait()

        @pl.when(before != block)
        def _():
            dk_sum[...] = jnp.zeros_like(dk_sum)
            dv_sum[...] = jnp.zeros_like(dv_sum)
            for pair in range(HEAD_PAIRS):
                lanes = slice(pair * 128, pair * 128 + 128)
                turned = jnp.transpose(k_buf[slot, :, lanes].astype(F32)).astype(BF16)
                k_turned[lanes, :] = turned

        def forward(pair):
            lanes = slice(pair * 128, pair * 128 + 128)
            keys = k_buf[slot, :, lanes]
            values = v_buf[slot, :, lanes]
            queries = q_buf[slot, :, lanes]
            douts = do_buf[slot, :, lanes]
            q_two = jnp.concatenate([queries * first_half, queries * second_half], axis=0)
            do_two = jnp.concatenate([douts * first_half, douts * second_half], axis=0)
            scores = lax.dot_general(keys, q_two, nt, preferred_element_type=F32)
            dprob = lax.dot_general(values, do_two, nt, preferred_element_type=F32)
            probs, dscores = [], []
            for side in range(2):
                head = 2 * pair + side
                cut = slice(side * BLK, side * BLK + BLK)
                lse = st_buf[slot, head : head + 1, :]
                delta = st_buf[slot, OWN_HEADS + head : OWN_HEADS + head + 1, :]
                prob = jnp.exp2(scores[:, cut] * (SCALE * LOG2E) - lse)
                probs.append(prob.astype(BF16))
                dscores.append((prob * (dprob[:, cut] - delta)).astype(BF16))
            p_buf[pair] = jnp.concatenate(probs, axis=1)
            ds_buf[pair] = jnp.concatenate(dscores, axis=1)

        def backward(pair):
            lanes = slice(pair * 128, pair * 128 + 128)
            queries = q_buf[slot, :, lanes]
            douts = do_buf[slot, :, lanes]
            q_two = jnp.concatenate([queries * first_half, queries * second_half], axis=0)
            do_two = jnp.concatenate([douts * first_half, douts * second_half], axis=0)
            dv_sum[:, lanes] += lax.dot_general(p_buf[pair], do_two, nn, preferred_element_type=F32)
            dk_sum[:, lanes] += lax.dot_general(ds_buf[pair], q_two, nn, preferred_element_type=F32)
            turned = k_turned[lanes, :]
            both = lax.dot_general(turned, ds_buf[pair], nn, preferred_element_type=F32)
            for side in range(2):
                low = pair * 128 + side * 64
                dq_sum[query, low : low + 64, :] += both[
                    side * 64 : side * 64 + 64, side * BLK : side * BLK + BLK
                ]

        for pair in range(HEAD_PAIRS):
            forward(pair)
        for pair in range(HEAD_PAIRS):
            backward(pair)

        @pl.when(after != block)
        def _():
            stage = lax.rem(flushed, 2)

            @pl.when(flushed >= 2)
            def _():
                for copy in flush_copies(stage, block):
                    copy.wait()

            dk_stage[stage] = (dk_sum[...] * SCALE).astype(BF16)
            dv_stage[stage] = dv_sum[...].astype(BF16)
            for copy in flush_copies(stage, block):
                copy.start()

        return flushed + jnp.where(after != block, 1, 0)

    flushed = lax.fori_loop(0, total, step, 0)

    def turn_in(query, carry):
        dq_stage[query] = (dq_sum[query] * SCALE).astype(BF16)
        pltpu.make_async_copy(dq_stage.at[query], dq_out.at[query], dq_sems.at[query]).start()
        return carry

    lax.fori_loop(0, QUERY_BLOCKS, turn_in, 0)
    for slot in range(2):

        @pl.when(flushed > slot)
        def _(slot=slot):
            for copy in flush_copies(slot, 0):
                copy.wait()

    for block in range(KEY_BLOCKS):
        up, across = divmod(block, NX)

        @pl.when(filled[block] == 0)
        def _(up=up, across=across):
            pltpu.make_async_copy(zeros, dk_out.at[up, across], zero_sems.at[0]).wait()
            pltpu.make_async_copy(zeros, dv_out.at[across, up], zero_sems.at[1]).wait()

    def finish(query, carry):
        pltpu.make_async_copy(dq_stage.at[query], dq_out.at[query], dq_sems.at[query]).wait()
        return carry

    lax.fori_loop(0, QUERY_BLOCKS, finish, 0)


def pairs_over_blocks(q_all, do_all, st_all, k_all, v_all, lists, counts, place):
    smem = pl.BlockSpec(memory_space=pltpu.SMEM)
    block_pair = pltpu.VMEM((2, BLK, COLS), BF16)
    return pl.pallas_call(
        pair_kernel,
        out_shape=[
            jax.ShapeDtypeStruct((QUERY_BLOCKS, COLS, BLK), BF16),
            jax.ShapeDtypeStruct((NY, NX, BLK, COLS), BF16),
            jax.ShapeDtypeStruct((NX, NY, BLK, COLS), BF16),
        ],
        in_specs=[smem] * 3 + [ANY] * 5,
        out_specs=[ANY] * 3,
        scratch_shapes=[
            block_pair,
            block_pair,
            pltpu.VMEM((2, 2 * OWN_HEADS, BLK), F32),
            block_pair,
            block_pair,
            pltpu.VMEM((COLS, BLK), BF16),
            pltpu.VMEM((HEAD_PAIRS, BLK, 2 * BLK), BF16),
            pltpu.VMEM((HEAD_PAIRS, BLK, 2 * BLK), BF16),
            pltpu.VMEM((QUERY_BLOCKS, COLS, BLK), F32),
            pltpu.VMEM((BLK, COLS), F32),
            pltpu.VMEM((BLK, COLS), F32),
            pltpu.VMEM((QUERY_BLOCKS, COLS, BLK), BF16),
            block_pair,
            block_pair,
            pltpu.VMEM((BLK, COLS), BF16),
            pltpu.SMEM((KEY_BLOCKS * BUCKET,), jnp.int32),
            pltpu.SMEM((KEY_BLOCKS,), jnp.int32),
            pltpu.SMEM((KEY_BLOCKS * QUERY_BLOCKS,), jnp.int32),
            pltpu.SemaphoreType.DMA((2, 5)),
            pltpu.SemaphoreType.DMA((2, 2)),
            pltpu.SemaphoreType.DMA((2,)),
            pltpu.SemaphoreType.DMA((QUERY_BLOCKS,)),
        ],
        compiler_params=pltpu.CompilerParams(vmem_limit_bytes=VMEM_LIMIT),
        name="used_pairs",
    )(
        lists,
        counts,
        place,
        q_all.reshape(QUERY_BLOCKS, BLK, COLS),
        do_all.reshape(QUERY_BLOCKS, BLK, COLS),
        st_all.reshape(QUERY_BLOCKS, 2 * OWN_HEADS, BLK),
        k_all,
        v_all,
    )


REDUCE_COPIES = 41
ROW_STEP = 16


def reduce_kernel(
    dq_part, dk_part, dv_part,
    gq_out, gk_out, gv_out,
    dq_own, dq_in_up, dq_in_down, dq_end,
    k_own, k_far, k_near, k_mid, k_mid_far, k_end,
    v_own, v_far, v_near, v_mid, v_mid_far, v_end,
    send_sems, recv_sems, local_sems, q_end_sems, k_end_sems, v_end_sems,
):
    me = Place()
    x, y, z, core = me.x, me.y, me.z, me.core
    loads = []

    def load(source, target):
        copy = pltpu.make_async_copy(source, target, local_sems.at[len(loads)])
        copy.start()
        loads.append(copy)

    first, second = pl.ds(0, 2), pl.ds(2, 2)
    load(dq_part.at[me.zs(3), 0], dq_own.at[me.zs(3), 0])
    load(dq_part.at[me.zs(-3), 1], dq_own.at[me.zs(-3), 1])
    load(dk_part.at[me.ys(1), first], k_own.at[me.ys(1), first])
    load(dv_part.at[me.xs(1), first], v_own.at[me.xs(1), first])
    load(dk_part.at[me.ys(-1), second], k_own.at[me.ys(-1), second])
    load(dv_part.at[me.xs(-1), second], v_own.at[me.xs(-1), second])
    for step in (2, -2, 1, -1):
        load(dq_part.at[me.zs(step)], dq_own.at[me.zs(step)])
    load(dk_part.at[y], k_own.at[y])
    load(dv_part.at[x], v_own.at[x])
    load(dq_part.at[z, core], dq_end.at[2, core])
    me.greet(both_cores=True)
    send = Sender(send_sems, recv_sems)
    up, down = me.over_z(1), me.over_z(-1)

    def add_rows(total, terms, count):
        def one(index, carry):
            at = pl.ds(pl.multiple_of(index * ROW_STEP, ROW_STEP), ROW_STEP)
            value = terms[0][at, :].astype(F32)
            for term in terms[1:]:
                value = value + term[at, :].astype(F32)
            total[at, :] = value.astype(total.dtype)
            return carry

        lax.fori_loop(0, count // ROW_STEP, one, 0, unroll=4)

    arrive = {
        ("up", 0, 1): send(dq_part.at[me.zs(4), 0], dq_in_up.at[0, 0], up),
        ("down", 1, 1): send(dq_part.at[me.zs(4), 1], dq_in_down.at[0, 1], down),
    }
    k_a = send(dk_part.at[me.ys(2), first], k_far.at[0], me.over_y(1))
    k_b = send(dk_part.at[me.ys(2), second], k_far.at[1], me.over_y(-1))
    v_a = send(dv_part.at[me.xs(2), first], v_far.at[0], me.over_x(1))
    v_b = send(dv_part.at[me.xs(2), second], v_far.at[1], me.over_x(-1))
    arrive["up", 1, 2] = send(dq_part.at[me.zs(3), 1], dq_in_up.at[1, 1], up)
    arrive["down", 0, 2] = send(dq_part.at[me.zs(-3), 0], dq_in_down.at[1, 0], down)
    k_in = [
        send(dk_part.at[me.ys(1), second], k_near.at[0, second], me.over_y(1)),
        send(dk_part.at[me.ys(-1), first], k_near.at[1, first], me.over_y(-1)),
    ]
    v_in = [
        send(dv_part.at[me.xs(1), second], v_near.at[0, second], me.over_x(1)),
        send(dv_part.at[me.xs(-1), first], v_near.at[1, first], me.over_x(-1)),
    ]
    q_sib = send(dq_part.at[z, 1 - core], dq_end.at[2, core], me.sibling, q_end_sems.at[2, core])

    def hop_q(direction, shard, hop):
        if direction == "up":
            side, step, inbox, way = 0, 4 - hop, dq_in_up, 1
        else:
            side, step, inbox, way = 1, hop - 4, dq_in_down, -1
        own = dq_own.at[me.zs(step), shard]
        arrive[direction, shard, hop].wait_recv()
        add_rows(own, [own, inbox.at[hop - 1, shard]], COLS)
        if hop < 3:
            arrive[direction, shard, hop + 1] = send(own, inbox.at[hop, shard], me.over_z(way))
        else:
            send(own, dq_end.at[side, core], me.over_z(way, owner=shard), q_end_sems.at[side, core])

    for copy in loads:
        copy.wait()
    hop_q("up", 0, 1)
    hop_q("down", 1, 1)

    def onward(arrival, own, place, base, inbox):
        arrival.wait_recv()
        for row in range(2):
            part = own.at[place, base + row]
            add_rows(part, [part, inbox.at[row]], BLK)

    onward(k_a, k_own, me.ys(1), 0, k_far.at[0])
    k_in.append(send(k_own.at[me.ys(1), first], k_near.at[0, first], me.over_y(1)))
    onward(v_a, v_own, me.xs(1), 0, v_far.at[0])
    v_in.append(send(v_own.at[me.xs(1), first], v_near.at[0, first], me.over_x(1)))
    onward(k_b, k_own, me.ys(-1), 2, k_far.at[1])
    k_in.append(send(k_own.at[me.ys(-1), second], k_near.at[1, second], me.over_y(-1)))
    onward(v_b, v_own, me.xs(-1), 2, v_far.at[1])
    v_in.append(send(v_own.at[me.xs(-1), second], v_near.at[1, second], me.over_x(-1)))
    for hop, shard in ((2, 1), (2, 0), (3, 1), (3, 0)):
        hop_q("up", shard, hop)
        hop_q("down", 1 - shard, hop)

    half_rows = (pl.ds(0, HALF), pl.ds(HALF, HALF))

    def turn(arrivals, own, here, near, middle, far, end, sems, axis, over, place):
        for arrival in arrivals:
            arrival.wait_recv()
        for row in range(4):
            add_rows(middle.at[row], [own.at[here, row], near.at[0, row], near.at[1, row]], BLK)
        ahead, back = axis(1), axis(-1)
        farthest = axis(2)
        far_a = send(middle.at[farthest, half_rows[0]], far.at[0], over(1))
        far_b = send(middle.at[farthest, half_rows[1]], far.at[1], over(-1))
        send(middle.at[ahead, half_rows[1]], end.at[0, core], over(1, owner=1), sems.at[0, core])
        send(middle.at[back, half_rows[0]], end.at[1, core], over(-1, owner=0), sems.at[1, core])
        send(middle.at[place, half_of(1 - core, HALF)], end.at[2, core], me.sibling, sems.at[2, core])
        end[2, core] = middle[place, half_of(core, HALF), :]
        return far_a, far_b

    def last(arrival, middle, at, half, far, end, sems, side, device):
        arrival.wait_recv()
        part = middle.at[at, half_rows[half]]
        add_rows(part, [part, far], HALF)
        send(part, end.at[side, core], device, sems.at[side, core])

    kx_a, kx_b = turn(
        k_in, k_own, y, k_near, k_mid, k_mid_far, k_end, k_end_sems, me.xs, me.over_x, x
    )
    vy_a, vy_b = turn(
        v_in, v_own, x, v_near, v_mid, v_mid_far, v_end, v_end_sems, me.ys, me.over_y, y
    )
    last(kx_a, k_mid, me.xs(1), 0, k_mid_far.at[0], k_end, k_end_sems, 0, me.over_x(1, owner=0))
    last(kx_b, k_mid, me.xs(-1), 1, k_mid_far.at[1], k_end, k_end_sems, 1, me.over_x(-1, owner=1))
    last(vy_a, v_mid, me.ys(1), 0, v_mid_far.at[0], v_end, v_end_sems, 0, me.over_y(1, owner=0))
    last(vy_b, v_mid, me.ys(-1), 1, v_mid_far.at[1], v_end, v_end_sems, 1, me.over_y(-1, owner=1))

    def ended(end, sems):
        for side in range(2):
            for column in range(CORES):
                pltpu.make_async_copy(end.at[side, column], end.at[side, column], sems.at[side, column]).wait()
        other = end.at[2, 1 - core]
        pltpu.make_async_copy(other, other, sems.at[2, 1 - core]).wait()

    ended(dq_end, q_end_sems)
    for column in range(CORES):
        for tile in range(COLS // 128):
            at = pl.ds(tile * 128, 128)
            value = (
                dq_end[0, column, at, :].astype(F32)
                + dq_end[1, column, at, :].astype(F32)
                + dq_end[2, column, at, :].astype(F32)
            )
            gq_out[:, pl.ds(column * COLS + tile * 128, 128)] = jnp.transpose(value).astype(BF16)
    for out, end, sems in ((gk_out, k_end, k_end_sems), (gv_out, v_end, v_end_sems)):
        ended(end, sems)
        for column in range(CORES):
            target = out.at[:, pl.ds(column * COLS, COLS)]
            add_rows(target, [end.at[side, column] for side in range(3)], HALF)
    send.finish()
    assert len(send.copies) == REDUCE_COPIES, len(send.copies)


def reduce_parts(dq_part, dk_part, dv_part):
    line = pltpu.VMEM((4, 4, BLK, COLS), BF16)
    two = pltpu.VMEM((2, 2, BLK, COLS), BF16)
    near = pltpu.VMEM((2, 4, BLK, COLS), BF16)
    four = pltpu.VMEM((4, BLK, COLS), BF16)
    half = pltpu.VMEM((2, HALF, COLS), BF16)
    end = pltpu.VMEM((3, CORES, HALF, COLS), BF16)
    inbox = pltpu.VMEM((3, CORES, COLS, BLK), BF16)
    vmem = pl.BlockSpec(memory_space=pltpu.VMEM)
    sems = pltpu.SemaphoreType.DMA((3, CORES))
    return pl.pallas_call(
        reduce_kernel,
        out_shape=[
            jax.ShapeDtypeStruct((BLK, WIDTH), BF16),
            jax.ShapeDtypeStruct((HALF, WIDTH), BF16),
            jax.ShapeDtypeStruct((HALF, WIDTH), BF16),
        ],
        in_specs=[ANY] * 3,
        out_specs=[vmem] * 3,
        scratch_shapes=[
            pltpu.VMEM((NZ, CORES, COLS, BLK), BF16), inbox, inbox, inbox,
            line, two, near, four, half, end,
            line, two, near, four, half, end,
            pltpu.SemaphoreType.DMA((REDUCE_COPIES,)),
            pltpu.SemaphoreType.DMA((REDUCE_COPIES,)),
            pltpu.SemaphoreType.DMA((13,)),
            sems, sems, sems,
        ],
        compiler_params=pltpu.CompilerParams(
            collective_id=1, has_side_effects=True, vmem_limit_bytes=VMEM_LIMIT
        ),
        name="reduce_parts",
    )(dq_part.reshape(NZ, CORES, COLS, BLK), dk_part, dv_part)


def body(q, k, v, out, do, lse, block_pairs, counts):
    ka = lax.axis_index("ka")
    place = jnp.stack([ka // NZ, ka % NZ]).astype(jnp.int32)
    lists = block_pairs.transpose(0, 2, 3, 1).reshape(2 * SLOTS, KEY_SHARDS)
    gathered = gather(q, do, k, v, out, lse, lists, counts)
    parts = pairs_over_blocks(*gathered, place)
    return tuple(reduce_parts(*parts))


def solution(mesh):
    placed = (
        P(("pb", "ka"), None),
        P(("ka", "pb"), None),
        P(("ka", "pb"), None),
        P(("pb", "ka"), None),
        P(("pb", "ka"), None),
        P(None, ("pb", "ka")),
        P("pb", None, None, None),
        P("pb", None),
    )
    return jax.shard_map(
        body,
        mesh=mesh,
        in_specs=placed,
        out_specs=(P(("pb", "ka"), None), P(("ka", "pb"), None), P(("ka", "pb"), None)),
        check_vma=False,
    )
```

```python
import jax
import jax.numpy as jnp
from jax import lax
from jax.experimental import pallas as pl
from jax.experimental.pallas import tpu as pltpu
from jax.sharding import PartitionSpec as P

NX, NY, NZ, CORES = 4, 4, 8, 2
HEADS = 16
OWN_HEADS = HEADS // CORES
BLK = 128
HALF = BLK // 2
WIDTH = 1024
COLS = WIDTH // CORES
HEAD_PAIRS = COLS // 128
SLOTS = 24
KEY_SHARDS = NX * NZ
QUERY_BLOCKS = NZ * CORES
KEY_BLOCKS = NX * NY
BUCKET = 32
SCALE = 64**-0.5
LOG2E = 1.4426950408889634
VMEM_LIMIT = 24 << 20
GATHER_LIMIT = 24 << 20
MESH = pl.DeviceIdType.MESH
HBM = pl.BlockSpec(memory_space=pltpu.HBM)
VMEM = pl.BlockSpec(memory_space=pltpu.VMEM)
F32 = jnp.float32
BF16 = jnp.bfloat16


class Place:
    def __init__(self):
        pb = lax.axis_index("pb")
        ka = lax.axis_index("ka")
        self.y = lax.div(pb, CORES)
        self.core = lax.rem(pb, CORES)
        self.x = lax.div(ka, NZ)
        self.z = lax.rem(ka, NZ)
        self.sibling = (self.y * CORES + 1 - self.core, ka)

    def aim(self, crossed, owner):
        if owner is not None:
            return owner
        return 1 - self.core if crossed else self.core

    def over_x(self, step, crossed=0, owner=None):
        return (self.y * CORES + self.aim(crossed, owner), self.xs(step) * NZ + self.z)

    def over_y(self, step, crossed=0, owner=None):
        return (self.ys(step) * CORES + self.aim(crossed, owner), self.x * NZ + self.z)

    def over_z(self, step, crossed=0, owner=None):
        return (self.y * CORES + self.aim(crossed, owner), self.x * NZ + self.zs(step))

    def xs(self, step):
        return lax.rem(self.x + step + NX, NX)

    def ys(self, step):
        return lax.rem(self.y + step + NY, NY)

    def zs(self, step):
        return lax.rem(self.z + step + NZ, NZ)

    def greet(self, both_cores=False):
        barrier = pltpu.get_barrier_semaphore()
        neighbours = [self.sibling]
        for step in (1, -1):
            for crossed in (0, 1) if both_cores else (0,):
                for over in (self.over_x, self.over_y, self.over_z):
                    neighbours.append(over(step, crossed))
        for neighbour in neighbours:
            pl.semaphore_signal(barrier, inc=1, device_id=neighbour, device_id_type=MESH)
        pl.semaphore_wait(barrier, len(neighbours))


class Sender:
    def __init__(self, send_sems, recv_sems):
        self.send_sems = send_sems
        self.recv_sems = recv_sems
        self.copies = []

    def __call__(self, source, target, device, recv_sem=None):
        index = len(self.copies)
        copy = pltpu.make_async_remote_copy(
            src_ref=source,
            dst_ref=target,
            send_sem=self.send_sems.at[index],
            recv_sem=self.recv_sems.at[index] if recv_sem is None else recv_sem,
            device_id=device,
            device_id_type=MESH,
        )
        copy.start()
        self.copies.append(copy)
        return copy

    def finish(self):
        for copy in self.copies:
            copy.wait_send()


def half_of(core, size):
    return pl.ds(pl.multiple_of(core * size, size), size)


GATHER_COPIES = 54


def gather_kernel(
    q_ref, do_ref, k_ref, v_ref, out_ref, lse_ref, list_ref, count_ref,
    q_all, do_all, st_all, k_all, v_all, list_all, count_all,
    do_buf, out_buf, lse_buf, st_buf, send_sems, recv_sems, local_sems,
):
    me = Place()
    x, y, z, core = me.x, me.y, me.z, me.core
    every = slice(None)
    rows = half_of(core, HALF)
    mine = half_of(core, COLS)
    theirs = half_of(1 - core, COLS)

    loads = [
        pltpu.make_async_copy(do_ref, do_buf, local_sems.at[5]),
        pltpu.make_async_copy(out_ref, out_buf, local_sems.at[6]),
        pltpu.make_async_copy(lse_ref, lse_buf, local_sems.at[7]),
    ]
    for load in loads:
        load.start()
    owns = [
        pltpu.make_async_copy(q_ref.at[every, mine], q_all.at[z, core], local_sems.at[0]),
        pltpu.make_async_copy(do_ref.at[every, mine], do_all.at[z, core], local_sems.at[1]),
        pltpu.make_async_copy(k_ref.at[every, mine], k_all.at[y, x, rows], local_sems.at[2]),
        pltpu.make_async_copy(v_ref.at[every, mine], v_all.at[x, y, rows], local_sems.at[3]),
        pltpu.make_async_copy(list_ref, list_all.at[core], local_sems.at[4]),
        pltpu.make_async_copy(count_ref, count_all.at[core], local_sems.at[8]),
    ]
    for own in owns:
        own.start()
    me.greet(both_cores=True)
    send = Sender(send_sems, recv_sems)
    up, down = me.over_z(1), me.over_z(-1)

    def to_both(ref, target, straight, crossed):
        return [
            send(ref.at[every, mine], target, straight),
            send(ref.at[every, theirs], target, crossed),
        ]

    cross_up, cross_down = me.over_z(1, 1), me.over_z(-1, 1)
    q_up = [to_both(q_ref, q_all.at[z, core], up, cross_up)]
    do_down = [to_both(do_ref, do_all.at[z, core], down, cross_down)]
    k_swap = send(k_ref.at[every, theirs], k_all.at[y, x, rows], me.sibling)
    v_swap = send(v_ref.at[every, theirs], v_all.at[x, y, rows], me.sibling)
    k_right = to_both(k_ref, k_all.at[y, x, rows], me.over_x(1), me.over_x(1, 1))
    k_left = to_both(k_ref, k_all.at[y, x, rows], me.over_x(-1), me.over_x(-1, 1))
    v_right = to_both(v_ref, v_all.at[x, y, rows], me.over_y(1), me.over_y(1, 1))
    v_left = to_both(v_ref, v_all.at[x, y, rows], me.over_y(-1), me.over_y(-1, 1))
    do_up = [to_both(do_ref, do_all.at[z, core], up, cross_up)]
    q_down = [to_both(q_ref, q_all.at[z, core], down, cross_down)]
    swaps = [
        send(q_ref.at[every, theirs], q_all.at[z, core], me.sibling),
        send(do_ref.at[every, theirs], do_all.at[z, core], me.sibling),
        send(list_ref, list_all.at[core], me.sibling),
        send(count_ref, count_all.at[core], me.sibling),
    ]

    for load in loads:
        load.wait()
    products = do_buf[...].astype(F32) * out_buf[...].astype(F32)
    high = products.astype(BF16)
    low = (products - high.astype(F32)).astype(BF16)
    head = lax.broadcasted_iota(jnp.int32, (HEADS, WIDTH), 0) * 64
    feature = lax.broadcasted_iota(jnp.int32, (HEADS, WIDTH), 1)
    member = jnp.where((feature >= head) & (feature < head + 64), 1.0, 0.0).astype(BF16)
    over_features = (((1,), (1,)), ((), ()))
    delta = lax.dot_general(member, high, over_features, preferred_element_type=F32)
    delta = delta + lax.dot_general(member, low, over_features, preferred_element_type=F32)
    for side in range(CORES):
        heads = slice(side * OWN_HEADS, side * OWN_HEADS + OWN_HEADS)
        st_buf[side, 0:OWN_HEADS, :] = lse_buf[heads, :] * LOG2E
        st_buf[side, OWN_HEADS : 2 * OWN_HEADS, :] = delta[heads, :]
    for own in owns:
        own.wait()
    st_own = pltpu.make_async_copy(st_buf.at[core], st_all.at[z, core], local_sems.at[0])
    st_own.start()
    swaps.append(send(st_buf.at[1 - core], st_all.at[z, core], me.sibling))
    st_up, st_down = [], []
    for stats, straight, crossed in ((st_up, up, cross_up), (st_down, down, cross_down)):
        stats.append(
            [
                send(st_buf.at[core], st_all.at[z, core], straight),
                send(st_buf.at[1 - core], st_all.at[z, core], crossed),
            ]
        )

    def arrived(*groups):
        for group in groups:
            for copy in group:
                copy.wait_recv()

    upper, lower = pl.ds(0, HALF), pl.ds(HALF, HALF)
    arrived(k_right)
    k_part = k_all.at[y, me.xs(-1), upper]
    k_far = [send(k_part, k_part, me.over_x(1))]
    arrived(v_right)
    v_part = v_all.at[x, me.ys(-1), upper]
    v_far = [send(v_part, v_part, me.over_y(1))]
    arrived(k_left)
    k_part = k_all.at[y, me.xs(1), lower]
    k_far.append(send(k_part, k_part, me.over_x(-1)))
    arrived(v_left)
    v_part = v_all.at[x, me.ys(1), lower]
    v_far.append(send(v_part, v_part, me.over_y(-1)))

    arrived([k_swap], k_far)
    k_right = [send(k_all.at[y], k_all.at[y], me.over_y(1))]
    k_left = [send(k_all.at[y], k_all.at[y], me.over_y(-1))]
    arrived([v_swap], v_far)
    v_right = [send(v_all.at[x], v_all.at[x], me.over_x(1))]
    v_left = [send(v_all.at[x], v_all.at[x], me.over_x(-1))]

    def forward(hop, sign, blocks, copies):
        arrived(copies[hop - 1])
        block = blocks.at[me.zs(-sign * hop)]
        copies.append([send(block, block, up if sign > 0 else down)])

    forward(1, 1, q_all, q_up)
    forward(1, -1, do_all, do_down)
    forward(1, 1, do_all, do_up)
    forward(1, -1, q_all, q_down)
    forward(1, 1, st_all, st_up)
    forward(1, -1, st_all, st_down)

    def across(blocks, start, low, device):
        part = blocks.at[start, pl.ds(low, 2)]
        return send(part, part, device)

    arrived(k_right)
    k_far = [across(k_all, me.ys(-1), 0, me.over_y(1))]
    arrived(v_right)
    v_far = [across(v_all, me.xs(-1), 0, me.over_x(1))]
    arrived(k_left)
    k_far.append(across(k_all, me.ys(1), 2, me.over_y(-1)))
    arrived(v_left)
    v_far.append(across(v_all, me.xs(1), 2, me.over_x(-1)))

    forward(2, 1, q_all, q_up)
    forward(2, -1, do_all, do_down)
    forward(2, 1, do_all, do_up)
    forward(2, -1, q_all, q_down)
    forward(2, 1, st_all, st_up)
    forward(2, -1, st_all, st_down)

    forward(3, 1, q_all, q_up)
    forward(3, -1, do_all, do_down)
    forward(3, 1, st_all, st_up)
    arrived(k_far, v_far, swaps, do_up[2], q_down[2], st_down[2], q_up[3], do_down[3], st_up[3])
    st_own.wait()
    send.finish()
    assert len(send.copies) == GATHER_COPIES, len(send.copies)


def gather(q, do, k, v, out, lse, lists, counts):
    return pl.pallas_call(
        gather_kernel,
        out_shape=[
            jax.ShapeDtypeStruct((NZ, CORES, BLK, COLS), BF16),
            jax.ShapeDtypeStruct((NZ, CORES, BLK, COLS), BF16),
            jax.ShapeDtypeStruct((NZ, CORES, 2 * OWN_HEADS, BLK), F32),
            jax.ShapeDtypeStruct((NY, NX, BLK, COLS), BF16),
            jax.ShapeDtypeStruct((NX, NY, BLK, COLS), BF16),
            jax.ShapeDtypeStruct((CORES, 2 * SLOTS, KEY_SHARDS), jnp.int32),
            jax.ShapeDtypeStruct((CORES, 1, KEY_SHARDS), jnp.int32),
        ],
        in_specs=[HBM] * 8,
        out_specs=[VMEM] * 5 + [HBM] * 2,
        scratch_shapes=[
            pltpu.VMEM((BLK, WIDTH), BF16),
            pltpu.VMEM((BLK, WIDTH), BF16),
            pltpu.VMEM((HEADS, BLK), F32),
            pltpu.VMEM((CORES, 2 * OWN_HEADS, BLK), F32),
            pltpu.SemaphoreType.DMA((GATHER_COPIES,)),
            pltpu.SemaphoreType.DMA((GATHER_COPIES,)),
            pltpu.SemaphoreType.DMA((9,)),
        ],
        compiler_params=pltpu.CompilerParams(
            collective_id=0, has_side_effects=True, vmem_limit_bytes=GATHER_LIMIT
        ),
        name="gather_blocks",
    )(q, do, k, v, out, lse, lists, counts)


def pair_kernel(
    lists, counts, place, q_all, do_all, st_all, k_all, v_all,
    dq_out, dk_out, dv_out,
    k_turned, p_buf, ds_buf, dq_sum, dk_sum, dv_sum, listed, filled,
):
    x = place[0]
    z = place[1]
    for block in range(KEY_BLOCKS):
        filled[block] = 0
    for owner in range(CORES):
        for column in range(NX):
            shard = column * NZ + z

            def enlist(slot, carry, owner=owner, column=column, shard=shard):
                query = lists[owner, slot, shard]
                block = lists[owner, SLOTS + slot, shard] * NX + column
                have = filled[block]
                listed[block * BUCKET + have] = lax.rem(query, NZ) * CORES + owner
                filled[block] = have + jnp.where(lax.div(query, NZ) == x, 1, 0)
                return carry

            lax.fori_loop(0, counts[owner, 0, shard], enlist, 0)

    def clear(query, carry):
        dq_sum[query] = jnp.zeros((COLS, BLK), F32)
        return carry

    lax.fori_loop(0, QUERY_BLOCKS, clear, 0)

    lane = lax.broadcasted_iota(jnp.int32, (1, 128), 1)
    first_half = jnp.where(lane < 64, 1.0, 0.0).astype(BF16)
    second_half = jnp.where(lane < 64, 0.0, 1.0).astype(BF16)
    nt = (((1,), (1,)), ((), ()))
    nn = (((1,), (0,)), ((), ()))

    def key_block(block, carry):
        up, across = lax.div(block, NX), lax.rem(block, NX)
        have = filled[block]

        @pl.when(have == 0)
        def _():
            dk_out[up, across] = jnp.zeros((BLK, COLS), BF16)
            dv_out[across, up] = jnp.zeros((BLK, COLS), BF16)

        def used(slot, carry):
            query = listed[block * BUCKET + slot]

            def forward(pair):
                lanes = slice(pair * 128, pair * 128 + 128)
                keys = k_all[up, across, :, lanes]
                values = v_all[across, up, :, lanes]
                queries = q_all[query, :, lanes]
                douts = do_all[query, :, lanes]
                q_two = jnp.concatenate([queries * first_half, queries * second_half], axis=0)
                do_two = jnp.concatenate([douts * first_half, douts * second_half], axis=0)
                scores = lax.dot_general(keys, q_two, nt, preferred_element_type=F32)
                dprob = lax.dot_general(values, do_two, nt, preferred_element_type=F32)
                for side in range(2):
                    head = 2 * pair + side
                    cut = slice(side * BLK, side * BLK + BLK)
                    lse = st_all[query, head : head + 1, :]
                    delta = st_all[query, OWN_HEADS + head : OWN_HEADS + head + 1, :]
                    prob = jnp.exp2(scores[:, cut] * (SCALE * LOG2E) - lse)
                    p_buf[pair, :, cut] = prob.astype(BF16)
                    ds_buf[pair, :, cut] = (prob * (dprob[:, cut] - delta)).astype(BF16)

            def backward(pair):
                lanes = slice(pair * 128, pair * 128 + 128)
                queries = q_all[query, :, lanes]
                douts = do_all[query, :, lanes]
                q_two = jnp.concatenate([queries * first_half, queries * second_half], axis=0)
                do_two = jnp.concatenate([douts * first_half, douts * second_half], axis=0)
                dv_sum[:, lanes] += lax.dot_general(
                    p_buf[pair], do_two, nn, preferred_element_type=F32
                )
                dk_sum[:, lanes] += lax.dot_general(
                    ds_buf[pair], q_two, nn, preferred_element_type=F32
                )
                both = lax.dot_general(
                    k_turned[lanes, :], ds_buf[pair], nn, preferred_element_type=F32
                )
                for side in range(2):
                    low = pair * 128 + side * 64
                    dq_sum[query, low : low + 64, :] += both[
                        side * 64 : side * 64 + 64, side * BLK : side * BLK + BLK
                    ]

            for pair in range(HEAD_PAIRS):
                forward(pair)
            for pair in range(HEAD_PAIRS):
                backward(pair)
            return carry

        @pl.when(have > 0)
        def _():
            dk_sum[...] = jnp.zeros_like(dk_sum)
            dv_sum[...] = jnp.zeros_like(dv_sum)
            for pair in range(HEAD_PAIRS):
                lanes = slice(pair * 128, pair * 128 + 128)
                turned = jnp.transpose(k_all[up, across, :, lanes].astype(F32)).astype(BF16)
                k_turned[lanes, :] = turned
            lax.fori_loop(0, have, used, 0)
            dk_out[up, across] = (dk_sum[...] * SCALE).astype(BF16)
            dv_out[across, up] = dv_sum[...].astype(BF16)

        return carry

    lax.fori_loop(0, KEY_BLOCKS, key_block, 0)

    def turn_in(query, carry):
        dq_out[query] = (dq_sum[query] * SCALE).astype(BF16)
        return carry

    lax.fori_loop(0, QUERY_BLOCKS, turn_in, 0)


def pairs_over_blocks(q_all, do_all, st_all, k_all, v_all, lists, counts, place):
    smem = pl.BlockSpec(memory_space=pltpu.SMEM)
    return pl.pallas_call(
        pair_kernel,
        out_shape=[
            jax.ShapeDtypeStruct((QUERY_BLOCKS, COLS, BLK), BF16),
            jax.ShapeDtypeStruct((NY, NX, BLK, COLS), BF16),
            jax.ShapeDtypeStruct((NX, NY, BLK, COLS), BF16),
        ],
        in_specs=[smem] * 3 + [VMEM] * 5,
        out_specs=[VMEM] * 3,
        scratch_shapes=[
            pltpu.VMEM((COLS, BLK), BF16),
            pltpu.VMEM((HEAD_PAIRS, BLK, 2 * BLK), BF16),
            pltpu.VMEM((HEAD_PAIRS, BLK, 2 * BLK), BF16),
            pltpu.VMEM((QUERY_BLOCKS, COLS, BLK), F32),
            pltpu.VMEM((BLK, COLS), F32),
            pltpu.VMEM((BLK, COLS), F32),
            pltpu.SMEM((KEY_BLOCKS * BUCKET,), jnp.int32),
            pltpu.SMEM((KEY_BLOCKS,), jnp.int32),
        ],
        compiler_params=pltpu.CompilerParams(vmem_limit_bytes=VMEM_LIMIT),
        name="used_pairs",
    )(
        lists,
        counts,
        place,
        q_all.reshape(QUERY_BLOCKS, BLK, COLS),
        do_all.reshape(QUERY_BLOCKS, BLK, COLS),
        st_all.reshape(QUERY_BLOCKS, 2 * OWN_HEADS, BLK),
        k_all,
        v_all,
    )


REDUCE_COPIES = 41
ROW_STEP = 16


def reduce_kernel(
    dq_part, dk_part, dv_part,
    gq_out, gk_out, gv_out,
    dq_own, dq_in_up, dq_in_down, dq_end,
    k_out, k_far, k_near, k_mid, k_mid_far, k_end,
    v_out, v_far, v_near, v_mid, v_mid_far, v_end,
    send_sems, recv_sems, q_end_sems, k_end_sems, v_end_sems,
):
    me = Place()
    x, y, z, core = me.x, me.y, me.z, me.core
    first, second = pl.ds(0, 2), pl.ds(2, 2)
    me.greet(both_cores=True)
    send = Sender(send_sems, recv_sems)
    up, down = me.over_z(1), me.over_z(-1)

    def add_rows(total, terms, count):
        def one(index, carry):
            at = pl.ds(pl.multiple_of(index * ROW_STEP, ROW_STEP), ROW_STEP)
            value = terms[0][at, :].astype(F32)
            for term in terms[1:]:
                value = value + term[at, :].astype(F32)
            total[at, :] = value.astype(total.dtype)
            return carry

        lax.fori_loop(0, count // ROW_STEP, one, 0, unroll=4)

    arrive = {
        ("up", 0, 1): send(dq_part.at[me.zs(4), 0], dq_in_up.at[0, 0], up),
        ("down", 1, 1): send(dq_part.at[me.zs(4), 1], dq_in_down.at[0, 1], down),
    }
    k_a = send(dk_part.at[me.ys(2), first], k_far.at[0], me.over_y(1))
    k_b = send(dk_part.at[me.ys(2), second], k_far.at[1], me.over_y(-1))
    v_a = send(dv_part.at[me.xs(2), first], v_far.at[0], me.over_x(1))
    v_b = send(dv_part.at[me.xs(2), second], v_far.at[1], me.over_x(-1))
    arrive["up", 1, 2] = send(dq_part.at[me.zs(3), 1], dq_in_up.at[1, 1], up)
    arrive["down", 0, 2] = send(dq_part.at[me.zs(-3), 0], dq_in_down.at[1, 0], down)
    k_in = [
        send(dk_part.at[me.ys(1), second], k_near.at[0, second], me.over_y(1)),
        send(dk_part.at[me.ys(-1), first], k_near.at[1, first], me.over_y(-1)),
    ]
    v_in = [
        send(dv_part.at[me.xs(1), second], v_near.at[0, second], me.over_x(1)),
        send(dv_part.at[me.xs(-1), first], v_near.at[1, first], me.over_x(-1)),
    ]
    q_sib = send(dq_part.at[z, 1 - core], dq_end.at[2, core], me.sibling, q_end_sems.at[2, core])

    def hop_q(direction, shard, hop):
        if direction == "up":
            side, step, inbox, way = 0, 4 - hop, dq_in_up, 1
        else:
            side, step, inbox, way = 1, hop - 4, dq_in_down, -1
        own = dq_own.at[me.zs(step), shard]
        arrive[direction, shard, hop].wait_recv()
        add_rows(own, [dq_part.at[me.zs(step), shard], inbox.at[hop - 1, shard]], COLS)
        if hop < 3:
            arrive[direction, shard, hop + 1] = send(own, inbox.at[hop, shard], me.over_z(way))
        else:
            send(own, dq_end.at[side, core], me.over_z(way, owner=shard), q_end_sems.at[side, core])

    add_rows(dq_end.at[2, core], [dq_part.at[z, core]], COLS)
    hop_q("up", 0, 1)
    hop_q("down", 1, 1)

    def onward(arrival, part, place, base, inbox, outbox):
        arrival.wait_recv()
        for row in range(2):
            add_rows(outbox.at[row], [part.at[place, base + row], inbox.at[row]], BLK)

    onward(k_a, dk_part, me.ys(1), 0, k_far.at[0], k_out.at[0])
    k_in.append(send(k_out.at[0], k_near.at[0, first], me.over_y(1)))
    onward(v_a, dv_part, me.xs(1), 0, v_far.at[0], v_out.at[0])
    v_in.append(send(v_out.at[0], v_near.at[0, first], me.over_x(1)))
    onward(k_b, dk_part, me.ys(-1), 2, k_far.at[1], k_out.at[1])
    k_in.append(send(k_out.at[1], k_near.at[1, second], me.over_y(-1)))
    onward(v_b, dv_part, me.xs(-1), 2, v_far.at[1], v_out.at[1])
    v_in.append(send(v_out.at[1], v_near.at[1, second], me.over_x(-1)))
    for hop, shard in ((2, 1), (2, 0), (3, 1), (3, 0)):
        hop_q("up", shard, hop)
        hop_q("down", 1 - shard, hop)

    half_rows = (pl.ds(0, HALF), pl.ds(HALF, HALF))

    def turn(arrivals, own, here, near, middle, far, end, sems, axis, over, place):
        for arrival in arrivals:
            arrival.wait_recv()
        for row in range(4):
            add_rows(middle.at[row], [own.at[here, row], near.at[0, row], near.at[1, row]], BLK)
        ahead, back = axis(1), axis(-1)
        farthest = axis(2)
        far_a = send(middle.at[farthest, half_rows[0]], far.at[0], over(1))
        far_b = send(middle.at[farthest, half_rows[1]], far.at[1], over(-1))
        send(middle.at[ahead, half_rows[1]], end.at[0, core], over(1, owner=1), sems.at[0, core])
        send(middle.at[back, half_rows[0]], end.at[1, core], over(-1, owner=0), sems.at[1, core])
        send(middle.at[place, half_of(1 - core, HALF)], end.at[2, core], me.sibling, sems.at[2, core])
        end[2, core] = middle[place, half_of(core, HALF), :]
        return far_a, far_b

    def last(arrival, middle, at, half, far, end, sems, side, device):
        arrival.wait_recv()
        part = middle.at[at, half_rows[half]]
        add_rows(part, [part, far], HALF)
        send(part, end.at[side, core], device, sems.at[side, core])

    kx_a, kx_b = turn(
        k_in, dk_part, y, k_near, k_mid, k_mid_far, k_end, k_end_sems, me.xs, me.over_x, x
    )
    vy_a, vy_b = turn(
        v_in, dv_part, x, v_near, v_mid, v_mid_far, v_end, v_end_sems, me.ys, me.over_y, y
    )
    last(kx_a, k_mid, me.xs(1), 0, k_mid_far.at[0], k_end, k_end_sems, 0, me.over_x(1, owner=0))
    last(kx_b, k_mid, me.xs(-1), 1, k_mid_far.at[1], k_end, k_end_sems, 1, me.over_x(-1, owner=1))
    last(vy_a, v_mid, me.ys(1), 0, v_mid_far.at[0], v_end, v_end_sems, 0, me.over_y(1, owner=0))
    last(vy_b, v_mid, me.ys(-1), 1, v_mid_far.at[1], v_end, v_end_sems, 1, me.over_y(-1, owner=1))

    def ended(end, sems):
        for side in range(2):
            for column in range(CORES):
                pltpu.make_async_copy(end.at[side, column], end.at[side, column], sems.at[side, column]).wait()
        other = end.at[2, 1 - core]
        pltpu.make_async_copy(other, other, sems.at[2, 1 - core]).wait()

    ended(dq_end, q_end_sems)
    for column in range(CORES):
        for tile in range(COLS // 128):
            at = pl.ds(tile * 128, 128)
            value = (
                dq_end[0, column, at, :].astype(F32)
                + dq_end[1, column, at, :].astype(F32)
                + dq_end[2, column, at, :].astype(F32)
            )
            gq_out[:, pl.ds(column * COLS + tile * 128, 128)] = jnp.transpose(value).astype(BF16)
    for out, end, sems in ((gk_out, k_end, k_end_sems), (gv_out, v_end, v_end_sems)):
        ended(end, sems)
        for column in range(CORES):
            target = out.at[:, pl.ds(column * COLS, COLS)]
            add_rows(target, [end.at[side, column] for side in range(3)], HALF)
    send.finish()
    assert len(send.copies) == REDUCE_COPIES, len(send.copies)


def reduce_parts(dq_part, dk_part, dv_part):
    two = pltpu.VMEM((2, 2, BLK, COLS), BF16)
    near = pltpu.VMEM((2, 4, BLK, COLS), BF16)
    four = pltpu.VMEM((4, BLK, COLS), BF16)
    half = pltpu.VMEM((2, HALF, COLS), BF16)
    end = pltpu.VMEM((3, CORES, HALF, COLS), BF16)
    inbox = pltpu.VMEM((3, CORES, COLS, BLK), BF16)
    sems = pltpu.SemaphoreType.DMA((3, CORES))
    return pl.pallas_call(
        reduce_kernel,
        out_shape=[
            jax.ShapeDtypeStruct((BLK, WIDTH), BF16),
            jax.ShapeDtypeStruct((HALF, WIDTH), BF16),
            jax.ShapeDtypeStruct((HALF, WIDTH), BF16),
        ],
        in_specs=[VMEM] * 3,
        out_specs=[VMEM] * 3,
        scratch_shapes=[
            pltpu.VMEM((NZ, CORES, COLS, BLK), BF16), inbox, inbox, inbox,
            two, two, near, four, half, end,
            two, two, near, four, half, end,
            pltpu.SemaphoreType.DMA((REDUCE_COPIES,)),
            pltpu.SemaphoreType.DMA((REDUCE_COPIES,)),
            sems, sems, sems,
        ],
        compiler_params=pltpu.CompilerParams(
            collective_id=1, has_side_effects=True, vmem_limit_bytes=VMEM_LIMIT
        ),
        name="reduce_parts",
    )(dq_part.reshape(NZ, CORES, COLS, BLK), dk_part, dv_part)


def body(q, k, v, out, do, lse, block_pairs, counts):
    ka = lax.axis_index("ka")
    place = jnp.stack([ka // NZ, ka % NZ]).astype(jnp.int32)
    lists = block_pairs.transpose(0, 2, 3, 1).reshape(2 * SLOTS, KEY_SHARDS)
    held = [pltpu.with_memory_space_constraint(array, pltpu.HBM) for array in (q, do, k, v, out, lse, lists, counts)]
    gathered = gather(*held)
    parts = pairs_over_blocks(*gathered, place)
    return tuple(reduce_parts(*parts))


def solution(mesh):
    placed = (
        P(("pb", "ka"), None),
        P(("ka", "pb"), None),
        P(("ka", "pb"), None),
        P(("pb", "ka"), None),
        P(("pb", "ka"), None),
        P(None, ("pb", "ka")),
        P("pb", None, None, None),
        P("pb", None),
    )
    return jax.shard_map(
        body,
        mesh=mesh,
        in_specs=placed,
        out_specs=(P(("pb", "ka"), None), P(("ka", "pb"), None), P(("ka", "pb"), None)),
        check_vma=False,
    )
```

```python
import jax
import jax.numpy as jnp
from jax import lax
from jax.experimental import pallas as pl
from jax.experimental.pallas import tpu as pltpu
from jax.sharding import PartitionSpec as P

NX, NY, NZ, CORES = 4, 4, 8, 2
HEADS = 16
OWN_HEADS = HEADS // CORES
BLK = 128
HALF = BLK // 2
WIDTH = 1024
COLS = WIDTH // CORES
HEAD_PAIRS = COLS // 128
SLOTS = 24
KEY_SHARDS = NX * NZ
QUERY_BLOCKS = NZ * CORES
KEY_BLOCKS = NX * NY
CELLS = KEY_BLOCKS * QUERY_BLOCKS
NEAR = 5
EARLY = 20
FIRST_EARLY = 8
TABLE = (8, 128)
SCALE = 64**-0.5
LOG2E = 1.4426950408889634
VMEM_LIMIT = 24 << 20
GATHER_LIMIT = 16 << 20
PAIR_LIMIT = 16 << 20
MESH = pl.DeviceIdType.MESH
HBM = pl.BlockSpec(memory_space=pltpu.HBM)
VMEM = pl.BlockSpec(memory_space=pltpu.VMEM)
F32 = jnp.float32
BF16 = jnp.bfloat16


class Place:
    def __init__(self):
        pb = lax.axis_index("pb")
        ka = lax.axis_index("ka")
        self.y = lax.div(pb, CORES)
        self.core = lax.rem(pb, CORES)
        self.x = lax.div(ka, NZ)
        self.z = lax.rem(ka, NZ)
        self.sibling = (self.y * CORES + 1 - self.core, ka)

    def aim(self, crossed, owner):
        if owner is not None:
            return owner
        return 1 - self.core if crossed else self.core

    def over_x(self, step, crossed=0, owner=None):
        return (self.y * CORES + self.aim(crossed, owner), self.xs(step) * NZ + self.z)

    def over_y(self, step, crossed=0, owner=None):
        return (self.ys(step) * CORES + self.aim(crossed, owner), self.x * NZ + self.z)

    def over_z(self, step, crossed=0, owner=None):
        return (self.y * CORES + self.aim(crossed, owner), self.x * NZ + self.zs(step))

    def xs(self, step):
        return lax.rem(self.x + step + NX, NX)

    def ys(self, step):
        return lax.rem(self.y + step + NY, NY)

    def zs(self, step):
        return lax.rem(self.z + step + NZ, NZ)

    def greet(self, both_cores=False):
        barrier = pltpu.get_barrier_semaphore()
        neighbours = [self.sibling]
        for step in (1, -1):
            for crossed in (0, 1) if both_cores else (0,):
                for over in (self.over_x, self.over_y, self.over_z):
                    neighbours.append(over(step, crossed))
        for neighbour in neighbours:
            pl.semaphore_signal(barrier, inc=1, device_id=neighbour, device_id_type=MESH)
        pl.semaphore_wait(barrier, len(neighbours))


class Sender:
    def __init__(self, send_sems, recv_sems):
        self.send_sems = send_sems
        self.recv_sems = recv_sems
        self.copies = []

    def __call__(self, source, target, device, recv_sem=None):
        index = len(self.copies)
        copy = pltpu.make_async_remote_copy(
            src_ref=source,
            dst_ref=target,
            send_sem=self.send_sems.at[index],
            recv_sem=self.recv_sems.at[index] if recv_sem is None else recv_sem,
            device_id=device,
            device_id_type=MESH,
        )
        copy.start()
        self.copies.append(copy)
        return copy

    def finish(self):
        for copy in self.copies:
            copy.wait_send()


NT = (((1,), (1,)), ((), ()))
NN = (((1,), (0,)), ((), ()))


def pair_lanes(pair):
    return slice(pair * 128, pair * 128 + 128)


def head_halves():
    lane = lax.broadcasted_iota(jnp.int32, (1, 128), 1)
    return (
        jnp.where(lane < 64, 1.0, 0.0).astype(BF16),
        jnp.where(lane < 64, 0.0, 1.0).astype(BF16),
    )


def both_heads(block, halves):
    return jnp.concatenate([block * halves[0], block * halves[1]], axis=0)


def turn_keys(keys, k_turned):
    for pair in range(HEAD_PAIRS):
        turned = jnp.transpose(keys(pair_lanes(pair)).astype(F32)).astype(BF16)
        k_turned[pair_lanes(pair), :] = turned


def pair_products(keys, values, queries, douts, stats, halves, p_buf, ds_buf, keep=None):
    for pair in range(HEAD_PAIRS):
        lanes = pair_lanes(pair)
        scores = lax.dot_general(
            keys(lanes), both_heads(queries(lanes), halves), NT, preferred_element_type=F32
        )
        dprob = lax.dot_general(
            values(lanes), both_heads(douts(lanes), halves), NT, preferred_element_type=F32
        )
        for side in range(2):
            head = 2 * pair + side
            cut = slice(side * BLK, side * BLK + BLK)
            prob = jnp.exp2(scores[:, cut] * (SCALE * LOG2E) - stats(head))
            if keep is not None:
                prob = jnp.where(keep, prob, 0.0)
            p_buf[pair, :, cut] = prob.astype(BF16)
            ds_buf[pair, :, cut] = (prob * (dprob[:, cut] - stats(OWN_HEADS + head))).astype(BF16)


def pair_gradients(queries, douts, halves, p_buf, ds_buf, k_turned, add_dv, add_dk, add_dq):
    for pair in range(HEAD_PAIRS):
        lanes = pair_lanes(pair)
        add_dv(
            lanes,
            lax.dot_general(
                p_buf[pair], both_heads(douts(lanes), halves), NN, preferred_element_type=F32
            ),
        )
        add_dk(
            lanes,
            lax.dot_general(
                ds_buf[pair], both_heads(queries(lanes), halves), NN, preferred_element_type=F32
            ),
        )
        both = lax.dot_general(k_turned[lanes, :], ds_buf[pair], NN, preferred_element_type=F32)
        for side in range(2):
            rows = slice(side * 64, side * 64 + 64)
            low = pair * 128 + side * 64
            add_dq(slice(low, low + 64), both[rows, side * BLK : side * BLK + BLK])


def tabulate(lists, counts, x, z, table):
    cell = lax.broadcasted_iota(jnp.int32, (CELLS, KEY_SHARDS), 0)
    shard = lax.broadcasted_iota(jnp.int32, (SLOTS, KEY_SHARDS), 1)
    slot = lax.broadcasted_iota(jnp.int32, (SLOTS, KEY_SHARDS), 0)
    used = jnp.zeros((CELLS, KEY_SHARDS), F32)
    for owner in range(CORES):
        queries = lists[owner, 0:SLOTS, :]
        blocks = lists[owner, SLOTS : 2 * SLOTS, :]
        column = lax.shift_right_logical(shard, 3)
        ok = (slot < counts[owner]) & ((shard & 7) == z) & (lax.shift_right_logical(queries, 3) == x)
        code = (blocks * NX + column) * QUERY_BLOCKS + (queries & 7) * CORES + owner
        code = jnp.where(ok, code, -1)
        for row in range(SLOTS):
            used = jnp.where(cell == code[row : row + 1, :], 1.0, used)
    used = jnp.max(used, axis=1, keepdims=True)
    order = lax.broadcasted_iota(jnp.int32, (CELLS, 1), 0)
    away = (lax.shift_right_logical(order & 15, 1) - z + 2 + NZ) & 7
    near = jnp.where(away < NEAR, used, 0.0)
    before = lax.broadcasted_iota(jnp.int32, (CELLS, CELLS), 0)
    before = before > lax.broadcasted_iota(jnp.int32, (CELLS, CELLS), 1)
    before = jnp.where(before, 1.0, 0.0).astype(BF16)
    spread = jnp.zeros((CELLS, 128), F32)
    near_rank = lax.dot_general(before, (near + spread).astype(BF16), NN, preferred_element_type=F32)
    early = jnp.where(near_rank < EARLY, near + spread, 0.0)
    others = (used + spread) - early
    other_rank = lax.dot_general(before, others.astype(BF16), NN, preferred_element_type=F32)
    lane = lax.broadcasted_iota(jnp.int32, (CELLS, 128), 1)
    line = lax.broadcasted_iota(jnp.int32, (CELLS, 128), 0)
    number = line.astype(F32)

    def total(values):
        return jnp.sum(values, axis=0, keepdims=True)

    place = lane.astype(F32)
    rows = [
        total(jnp.where(near_rank == place, early * number, 0.0)),
        total(jnp.where(other_rank == place, others * number, 0.0)),
        total(jnp.where(other_rank == place + 128.0, others * number, 0.0)),
        total(jnp.where(line < lane * QUERY_BLOCKS, early, 0.0)),
        total(jnp.where(line < lane * QUERY_BLOCKS, others, 0.0)),
    ]
    table[...] = jnp.zeros(TABLE, jnp.int32)
    for index, row in enumerate(rows):
        table[index : index + 1, :] = row.astype(jnp.int32)


def half_of(core, size):
    return pl.ds(pl.multiple_of(core * size, size), size)


GATHER_COPIES = 54


def gather_kernel(
    q_ref, do_ref, k_ref, v_ref, out_ref, lse_ref, list_ref, count_ref,
    q_all, do_all, st_all, k_all, v_all, table_out, dk_early, dv_early, dq_early,
    do_buf, out_buf, lse_buf, st_buf, list_all, count_all, q_near, do_near, st_near,
    k_turned, p_buf, ds_buf, table, table_s, send_sems, recv_sems, local_sems, near_sems,
):
    me = Place()
    x, y, z, core = me.x, me.y, me.z, me.core
    every = slice(None)
    rows = half_of(core, HALF)
    mine = half_of(core, COLS)
    theirs = half_of(1 - core, COLS)

    loads = [
        pltpu.make_async_copy(do_ref, do_buf, local_sems.at[5]),
        pltpu.make_async_copy(out_ref, out_buf, local_sems.at[6]),
        pltpu.make_async_copy(lse_ref, lse_buf, local_sems.at[7]),
    ]
    for load in loads:
        load.start()
    owns = [
        pltpu.make_async_copy(q_ref.at[every, mine], q_all.at[z, core], local_sems.at[0]),
        pltpu.make_async_copy(do_ref.at[every, mine], do_all.at[z, core], local_sems.at[1]),
        pltpu.make_async_copy(k_ref.at[every, mine], k_all.at[y, x, rows], local_sems.at[2]),
        pltpu.make_async_copy(v_ref.at[every, mine], v_all.at[x, y, rows], local_sems.at[3]),
        pltpu.make_async_copy(list_ref, list_all.at[core], local_sems.at[4]),
        pltpu.make_async_copy(count_ref, count_all.at[core], local_sems.at[8]),
    ]
    for own in owns:
        own.start()
    me.greet(both_cores=True)
    send = Sender(send_sems, recv_sems)
    up, down = me.over_z(1), me.over_z(-1)

    def to_both(ref, target, straight, crossed):
        return [
            send(ref.at[every, mine], target, straight),
            send(ref.at[every, theirs], target, crossed),
        ]

    cross_up, cross_down = me.over_z(1, 1), me.over_z(-1, 1)
    q_up = [to_both(q_ref, q_all.at[z, core], up, cross_up)]
    do_down = [to_both(do_ref, do_all.at[z, core], down, cross_down)]
    k_swap = send(k_ref.at[every, theirs], k_all.at[y, x, rows], me.sibling)
    v_swap = send(v_ref.at[every, theirs], v_all.at[x, y, rows], me.sibling)
    k_right = to_both(k_ref, k_all.at[y, x, rows], me.over_x(1), me.over_x(1, 1))
    k_left = to_both(k_ref, k_all.at[y, x, rows], me.over_x(-1), me.over_x(-1, 1))
    v_right = to_both(v_ref, v_all.at[x, y, rows], me.over_y(1), me.over_y(1, 1))
    v_left = to_both(v_ref, v_all.at[x, y, rows], me.over_y(-1), me.over_y(-1, 1))
    do_up = [to_both(do_ref, do_all.at[z, core], up, cross_up)]
    q_down = [to_both(q_ref, q_all.at[z, core], down, cross_down)]
    swaps = [
        send(q_ref.at[every, theirs], q_all.at[z, core], me.sibling),
        send(do_ref.at[every, theirs], do_all.at[z, core], me.sibling),
        send(list_ref, list_all.at[core], me.sibling),
        send(count_ref, count_all.at[core], me.sibling),
    ]

    for load in loads:
        load.wait()
    products = do_buf[...].astype(F32) * out_buf[...].astype(F32)
    high = products.astype(BF16)
    low = (products - high.astype(F32)).astype(BF16)
    head = lax.broadcasted_iota(jnp.int32, (HEADS, WIDTH), 0) * 64
    feature = lax.broadcasted_iota(jnp.int32, (HEADS, WIDTH), 1)
    member = jnp.where((feature >= head) & (feature < head + 64), 1.0, 0.0).astype(BF16)
    over_features = (((1,), (1,)), ((), ()))
    delta = lax.dot_general(member, high, over_features, preferred_element_type=F32)
    delta = delta + lax.dot_general(member, low, over_features, preferred_element_type=F32)
    for side in range(CORES):
        heads = slice(side * OWN_HEADS, side * OWN_HEADS + OWN_HEADS)
        st_buf[side, 0:OWN_HEADS, :] = lse_buf[heads, :] * LOG2E
        st_buf[side, OWN_HEADS : 2 * OWN_HEADS, :] = delta[heads, :]
    for own in owns:
        own.wait()
    nears = []

    def bring_near(arrays, distance):
        for blocks, held in arrays:
            copy = pltpu.make_async_copy(
                blocks.at[me.zs(distance)], held.at[distance + 2], near_sems.at[len(nears)]
            )
            copy.start()
            nears.append(copy)

    st_own = pltpu.make_async_copy(st_buf.at[core], st_all.at[z, core], local_sems.at[0])
    st_own.start()
    swaps.append(send(st_buf.at[1 - core], st_all.at[z, core], me.sibling))
    st_up, st_down = [], []
    for stats, straight, crossed in ((st_up, up, cross_up), (st_down, down, cross_down)):
        stats.append(
            [
                send(st_buf.at[core], st_all.at[z, core], straight),
                send(st_buf.at[1 - core], st_all.at[z, core], crossed),
            ]
        )

    def arrived(*groups):
        for group in groups:
            for copy in group:
                copy.wait_recv()

    upper, lower = pl.ds(0, HALF), pl.ds(HALF, HALF)
    arrived(k_right)
    k_part = k_all.at[y, me.xs(-1), upper]
    k_far = [send(k_part, k_part, me.over_x(1))]
    arrived(v_right)
    v_part = v_all.at[x, me.ys(-1), upper]
    v_far = [send(v_part, v_part, me.over_y(1))]
    arrived(k_left)
    k_part = k_all.at[y, me.xs(1), lower]
    k_far.append(send(k_part, k_part, me.over_x(-1)))
    arrived(v_left)
    v_part = v_all.at[x, me.ys(1), lower]
    v_far.append(send(v_part, v_part, me.over_y(-1)))

    arrived([k_swap], k_far)
    k_right = [send(k_all.at[y], k_all.at[y], me.over_y(1))]
    k_left = [send(k_all.at[y], k_all.at[y], me.over_y(-1))]
    arrived([v_swap], v_far)
    v_right = [send(v_all.at[x], v_all.at[x], me.over_x(1))]
    v_left = [send(v_all.at[x], v_all.at[x], me.over_x(-1))]

    def forward(hop, sign, blocks, copies):
        arrived(copies[hop - 1])
        block = blocks.at[me.zs(-sign * hop)]
        copies.append([send(block, block, up if sign > 0 else down)])

    forward(1, 1, q_all, q_up)
    forward(1, -1, do_all, do_down)
    arrived(swaps)
    st_own.wait()
    tabulate(list_all, count_all, x, z, table)
    to_scalars = pltpu.make_async_copy(table, table_s, local_sems.at[1])
    to_scalars.start()
    table_store = pltpu.make_async_copy(table, table_out, local_sems.at[2])
    table_store.start()
    every_array = ((q_all, q_near), (do_all, do_near), (st_all, st_near))
    bring_near(every_array, 0)
    forward(1, 1, do_all, do_up)
    forward(1, -1, q_all, q_down)
    forward(1, 1, st_all, st_up)
    forward(1, -1, st_all, st_down)
    bring_near(every_array, 1)
    bring_near(every_array, -1)

    def across(blocks, start, low, device):
        part = blocks.at[start, pl.ds(low, 2)]
        return send(part, part, device)

    arrived(k_right)
    k_far = [across(k_all, me.ys(-1), 0, me.over_y(1))]
    arrived(v_right)
    v_far = [across(v_all, me.xs(-1), 0, me.over_x(1))]
    arrived(k_left)
    k_far.append(across(k_all, me.ys(1), 2, me.over_y(-1)))
    arrived(v_left)
    v_far.append(across(v_all, me.xs(1), 2, me.over_x(-1)))

    forward(2, 1, q_all, q_up)
    forward(2, -1, do_all, do_down)
    forward(2, 1, do_all, do_up)
    forward(2, -1, q_all, q_down)
    forward(2, 1, st_all, st_up)
    forward(2, -1, st_all, st_down)

    bring_near(every_array, 2)
    bring_near(every_array, -2)
    forward(3, 1, q_all, q_up)
    forward(3, -1, do_all, do_down)
    arrived(k_far, v_far)
    for copy in nears:
        copy.wait()
    to_scalars.wait()
    halves = head_halves()
    used = table_s[3, KEY_BLOCKS]

    def early(index, carry):
        entry = jnp.clip(table_s[0, index], 0, CELLS - 1)
        block = lax.div(entry, QUERY_BLOCKS)
        up_block, across_block = lax.div(block, NX), lax.rem(block, NX)
        query = lax.rem(lax.div(lax.rem(entry, QUERY_BLOCKS), CORES) - z + 2 + NZ, NZ)
        query = jnp.minimum(query, NEAR - 1)
        owner = lax.rem(entry, CORES)

        def keys(lanes):
            return k_all[up_block, across_block, :, lanes]

        def values(lanes):
            return v_all[across_block, up_block, :, lanes]

        def queries(lanes):
            return q_near[query, owner, :, lanes]

        def douts(lanes):
            return do_near[query, owner, :, lanes]

        def stats(row):
            return st_near[query, owner, row : row + 1, :]

        turn_keys(keys, k_turned)
        pair_products(keys, values, queries, douts, stats, halves, p_buf, ds_buf, keep=index < used)

        def put_dv(lanes, value):
            dv_early[index, :, lanes] = value

        def put_dk(lanes, value):
            dk_early[index, :, lanes] = value

        def put_dq(rows, value):
            dq_early[index, rows, :] = value

        pair_gradients(queries, douts, halves, p_buf, ds_buf, k_turned, put_dv, put_dk, put_dq)
        return carry

    lax.fori_loop(0, FIRST_EARLY, early, 0)
    forward(3, 1, st_all, st_up)
    lax.fori_loop(FIRST_EARLY, EARLY, early, 0)
    arrived(do_up[2], q_down[2], st_down[2], q_up[3], do_down[3], st_up[3])
    table_store.wait()
    send.finish()
    assert len(send.copies) == GATHER_COPIES, len(send.copies)


def gather(q, do, k, v, out, lse, lists, counts):
    return pl.pallas_call(
        gather_kernel,
        out_shape=[
            jax.ShapeDtypeStruct((NZ, CORES, BLK, COLS), BF16),
            jax.ShapeDtypeStruct((NZ, CORES, BLK, COLS), BF16),
            jax.ShapeDtypeStruct((NZ, CORES, 2 * OWN_HEADS, BLK), F32),
            jax.ShapeDtypeStruct((NY, NX, BLK, COLS), BF16),
            jax.ShapeDtypeStruct((NX, NY, BLK, COLS), BF16),
            jax.ShapeDtypeStruct(TABLE, jnp.int32),
            jax.ShapeDtypeStruct((EARLY, BLK, COLS), F32),
            jax.ShapeDtypeStruct((EARLY, BLK, COLS), F32),
            jax.ShapeDtypeStruct((EARLY, COLS, BLK), F32),
        ],
        in_specs=[HBM] * 8,
        out_specs=[VMEM] * 5 + [HBM] + [VMEM] * 3,
        scratch_shapes=[
            pltpu.VMEM((BLK, WIDTH), BF16),
            pltpu.VMEM((BLK, WIDTH), BF16),
            pltpu.VMEM((HEADS, BLK), F32),
            pltpu.VMEM((CORES, 2 * OWN_HEADS, BLK), F32),
            pltpu.VMEM((CORES, 2 * SLOTS, KEY_SHARDS), jnp.int32),
            pltpu.VMEM((CORES, 1, KEY_SHARDS), jnp.int32),
            pltpu.VMEM((NEAR, CORES, BLK, COLS), BF16),
            pltpu.VMEM((NEAR, CORES, BLK, COLS), BF16),
            pltpu.VMEM((NEAR, CORES, 2 * OWN_HEADS, BLK), F32),
            pltpu.VMEM((COLS, BLK), BF16),
            pltpu.VMEM((HEAD_PAIRS, BLK, 2 * BLK), BF16),
            pltpu.VMEM((HEAD_PAIRS, BLK, 2 * BLK), BF16),
            pltpu.VMEM(TABLE, jnp.int32),
            pltpu.SMEM(TABLE, jnp.int32),
            pltpu.SemaphoreType.DMA((GATHER_COPIES,)),
            pltpu.SemaphoreType.DMA((GATHER_COPIES,)),
            pltpu.SemaphoreType.DMA((9,)),
            pltpu.SemaphoreType.DMA((3 * NEAR,)),
        ],
        compiler_params=pltpu.CompilerParams(
            collective_id=0, has_side_effects=True, vmem_limit_bytes=GATHER_LIMIT
        ),
        name="gather_blocks",
    )(q, do, k, v, out, lse, lists, counts)


def pair_kernel(
    table, q_all, do_all, st_all, k_all, v_all, dk_early, dv_early, dq_early,
    dq_out, dk_out, dv_out,
    k_turned, p_buf, ds_buf, dq_sum, dk_sum, dv_sum,
):
    def clear(query, carry):
        dq_sum[query] = jnp.zeros((COLS, BLK), F32)
        return carry

    lax.fori_loop(0, QUERY_BLOCKS, clear, 0)
    halves = head_halves()

    def key_block(block, carry):
        up, across = lax.div(block, NX), lax.rem(block, NX)
        early_low, early_high = table[3, block], table[3, block + 1]
        low, high = table[4, block], table[4, block + 1]
        have = (early_high - early_low) + (high - low)

        @pl.when(have == 0)
        def _():
            dk_out[up, across] = jnp.zeros((BLK, COLS), BF16)
            dv_out[across, up] = jnp.zeros((BLK, COLS), BF16)

        def keys(lanes):
            return k_all[up, across, :, lanes]

        def values(lanes):
            return v_all[across, up, :, lanes]

        def take(slot, carry):
            query = lax.rem(table[0, slot], QUERY_BLOCKS)
            dk_sum[...] += dk_early[slot]
            dv_sum[...] += dv_early[slot]
            dq_sum[query] += dq_early[slot]
            return carry

        def used(slot, carry):
            query = lax.rem(table[1 + lax.div(slot, 128), lax.rem(slot, 128)], QUERY_BLOCKS)

            def queries(lanes):
                return q_all[query, :, lanes]

            def douts(lanes):
                return do_all[query, :, lanes]

            def stats(row):
                return st_all[query, row : row + 1, :]

            pair_products(keys, values, queries, douts, stats, halves, p_buf, ds_buf)

            def add_dv(lanes, value):
                dv_sum[:, lanes] += value

            def add_dk(lanes, value):
                dk_sum[:, lanes] += value

            def add_dq(rows, value):
                dq_sum[query, rows, :] += value

            pair_gradients(queries, douts, halves, p_buf, ds_buf, k_turned, add_dv, add_dk, add_dq)
            return carry

        @pl.when(have > 0)
        def _():
            dk_sum[...] = jnp.zeros_like(dk_sum)
            dv_sum[...] = jnp.zeros_like(dv_sum)
            lax.fori_loop(early_low, early_high, take, 0)

            @pl.when(high > low)
            def _():
                turn_keys(keys, k_turned)

            lax.fori_loop(low, high, used, 0)
            dk_out[up, across] = (dk_sum[...] * SCALE).astype(BF16)
            dv_out[across, up] = dv_sum[...].astype(BF16)

        return carry

    lax.fori_loop(0, KEY_BLOCKS, key_block, 0)

    def turn_in(query, carry):
        dq_out[query] = (dq_sum[query] * SCALE).astype(BF16)
        return carry

    lax.fori_loop(0, QUERY_BLOCKS, turn_in, 0)


def pairs_over_blocks(q_all, do_all, st_all, k_all, v_all, table, dk_early, dv_early, dq_early):
    return pl.pallas_call(
        pair_kernel,
        out_shape=[
            jax.ShapeDtypeStruct((QUERY_BLOCKS, COLS, BLK), BF16),
            jax.ShapeDtypeStruct((NY, NX, BLK, COLS), BF16),
            jax.ShapeDtypeStruct((NX, NY, BLK, COLS), BF16),
        ],
        in_specs=[pl.BlockSpec(memory_space=pltpu.SMEM)] + [VMEM] * 8,
        out_specs=[VMEM] * 3,
        scratch_shapes=[
            pltpu.VMEM((COLS, BLK), BF16),
            pltpu.VMEM((HEAD_PAIRS, BLK, 2 * BLK), BF16),
            pltpu.VMEM((HEAD_PAIRS, BLK, 2 * BLK), BF16),
            pltpu.VMEM((QUERY_BLOCKS, COLS, BLK), F32),
            pltpu.VMEM((BLK, COLS), F32),
            pltpu.VMEM((BLK, COLS), F32),
        ],
        compiler_params=pltpu.CompilerParams(vmem_limit_bytes=PAIR_LIMIT),
        name="used_pairs",
    )(
        table,
        q_all.reshape(QUERY_BLOCKS, BLK, COLS),
        do_all.reshape(QUERY_BLOCKS, BLK, COLS),
        st_all.reshape(QUERY_BLOCKS, 2 * OWN_HEADS, BLK),
        k_all,
        v_all,
        dk_early,
        dv_early,
        dq_early,
    )


REDUCE_COPIES = 41
ROW_STEP = 16


def reduce_kernel(
    dq_part, dk_part, dv_part,
    gq_out, gk_out, gv_out,
    dq_own, dq_in_up, dq_in_down, dq_end,
    k_out, k_far, k_near, k_mid, k_mid_far, k_end,
    v_out, v_far, v_near, v_mid, v_mid_far, v_end,
    send_sems, recv_sems, q_end_sems, k_end_sems, v_end_sems,
):
    me = Place()
    x, y, z, core = me.x, me.y, me.z, me.core
    first, second = pl.ds(0, 2), pl.ds(2, 2)
    me.greet(both_cores=True)
    send = Sender(send_sems, recv_sems)
    up, down = me.over_z(1), me.over_z(-1)

    def add_rows(total, terms, count):
        def one(index, carry):
            at = pl.ds(pl.multiple_of(index * ROW_STEP, ROW_STEP), ROW_STEP)
            value = terms[0][at, :].astype(F32)
            for term in terms[1:]:
                value = value + term[at, :].astype(F32)
            total[at, :] = value.astype(total.dtype)
            return carry

        lax.fori_loop(0, count // ROW_STEP, one, 0, unroll=4)

    arrive = {
        ("up", 0, 1): send(dq_part.at[me.zs(4), 0], dq_in_up.at[0, 0], up),
        ("down", 1, 1): send(dq_part.at[me.zs(4), 1], dq_in_down.at[0, 1], down),
    }
    k_a = send(dk_part.at[me.ys(2), first], k_far.at[0], me.over_y(1))
    k_b = send(dk_part.at[me.ys(2), second], k_far.at[1], me.over_y(-1))
    v_a = send(dv_part.at[me.xs(2), first], v_far.at[0], me.over_x(1))
    v_b = send(dv_part.at[me.xs(2), second], v_far.at[1], me.over_x(-1))
    arrive["up", 1, 2] = send(dq_part.at[me.zs(3), 1], dq_in_up.at[1, 1], up)
    arrive["down", 0, 2] = send(dq_part.at[me.zs(-3), 0], dq_in_down.at[1, 0], down)
    k_in = [
        send(dk_part.at[me.ys(1), second], k_near.at[0, second], me.over_y(1)),
        send(dk_part.at[me.ys(-1), first], k_near.at[1, first], me.over_y(-1)),
    ]
    v_in = [
        send(dv_part.at[me.xs(1), second], v_near.at[0, second], me.over_x(1)),
        send(dv_part.at[me.xs(-1), first], v_near.at[1, first], me.over_x(-1)),
    ]
    q_sib = send(dq_part.at[z, 1 - core], dq_end.at[2, core], me.sibling, q_end_sems.at[2, core])

    def hop_q(direction, shard, hop):
        if direction == "up":
            side, step, inbox, way = 0, 4 - hop, dq_in_up, 1
        else:
            side, step, inbox, way = 1, hop - 4, dq_in_down, -1
        own = dq_own.at[me.zs(step), shard]
        arrive[direction, shard, hop].wait_recv()
        add_rows(own, [dq_part.at[me.zs(step), shard], inbox.at[hop - 1, shard]], COLS)
        if hop < 3:
            arrive[direction, shard, hop + 1] = send(own, inbox.at[hop, shard], me.over_z(way))
        else:
            send(own, dq_end.at[side, core], me.over_z(way, owner=shard), q_end_sems.at[side, core])

    add_rows(dq_end.at[2, core], [dq_part.at[z, core]], COLS)
    hop_q("up", 0, 1)
    hop_q("down", 1, 1)

    def onward(arrival, part, place, base, inbox, outbox):
        arrival.wait_recv()
        for row in range(2):
            add_rows(outbox.at[row], [part.at[place, base + row], inbox.at[row]], BLK)

    onward(k_a, dk_part, me.ys(1), 0, k_far.at[0], k_out.at[0])
    k_in.append(send(k_out.at[0], k_near.at[0, first], me.over_y(1)))
    onward(v_a, dv_part, me.xs(1), 0, v_far.at[0], v_out.at[0])
    v_in.append(send(v_out.at[0], v_near.at[0, first], me.over_x(1)))
    onward(k_b, dk_part, me.ys(-1), 2, k_far.at[1], k_out.at[1])
    k_in.append(send(k_out.at[1], k_near.at[1, second], me.over_y(-1)))
    onward(v_b, dv_part, me.xs(-1), 2, v_far.at[1], v_out.at[1])
    v_in.append(send(v_out.at[1], v_near.at[1, second], me.over_x(-1)))
    for hop, shard in ((2, 1), (2, 0), (3, 1), (3, 0)):
        hop_q("up", shard, hop)
        hop_q("down", 1 - shard, hop)

    half_rows = (pl.ds(0, HALF), pl.ds(HALF, HALF))

    def turn(arrivals, own, here, near, middle, far, end, sems, axis, over, place):
        for arrival in arrivals:
            arrival.wait_recv()
        for row in range(4):
            add_rows(middle.at[row], [own.at[here, row], near.at[0, row], near.at[1, row]], BLK)
        ahead, back = axis(1), axis(-1)
        farthest = axis(2)
        far_a = send(middle.at[farthest, half_rows[0]], far.at[0], over(1))
        far_b = send(middle.at[farthest, half_rows[1]], far.at[1], over(-1))
        send(middle.at[ahead, half_rows[1]], end.at[0, core], over(1, owner=1), sems.at[0, core])
        send(middle.at[back, half_rows[0]], end.at[1, core], over(-1, owner=0), sems.at[1, core])
        send(middle.at[place, half_of(1 - core, HALF)], end.at[2, core], me.sibling, sems.at[2, core])
        end[2, core] = middle[place, half_of(core, HALF), :]
        return far_a, far_b

    def last(arrival, middle, at, half, far, end, sems, side, device):
        arrival.wait_recv()
        part = middle.at[at, half_rows[half]]
        add_rows(part, [part, far], HALF)
        send(part, end.at[side, core], device, sems.at[side, core])

    kx_a, kx_b = turn(
        k_in, dk_part, y, k_near, k_mid, k_mid_far, k_end, k_end_sems, me.xs, me.over_x, x
    )
    vy_a, vy_b = turn(
        v_in, dv_part, x, v_near, v_mid, v_mid_far, v_end, v_end_sems, me.ys, me.over_y, y
    )
    last(kx_a, k_mid, me.xs(1), 0, k_mid_far.at[0], k_end, k_end_sems, 0, me.over_x(1, owner=0))
    last(kx_b, k_mid, me.xs(-1), 1, k_mid_far.at[1], k_end, k_end_sems, 1, me.over_x(-1, owner=1))
    last(vy_a, v_mid, me.ys(1), 0, v_mid_far.at[0], v_end, v_end_sems, 0, me.over_y(1, owner=0))
    last(vy_b, v_mid, me.ys(-1), 1, v_mid_far.at[1], v_end, v_end_sems, 1, me.over_y(-1, owner=1))

    def ended(end, sems):
        for side in range(2):
            for column in range(CORES):
                pltpu.make_async_copy(end.at[side, column], end.at[side, column], sems.at[side, column]).wait()
        other = end.at[2, 1 - core]
        pltpu.make_async_copy(other, other, sems.at[2, 1 - core]).wait()

    ended(dq_end, q_end_sems)
    for column in range(CORES):
        for tile in range(COLS // 128):
            at = pl.ds(tile * 128, 128)
            value = (
                dq_end[0, column, at, :].astype(F32)
                + dq_end[1, column, at, :].astype(F32)
                + dq_end[2, column, at, :].astype(F32)
            )
            gq_out[:, pl.ds(column * COLS + tile * 128, 128)] = jnp.transpose(value).astype(BF16)
    for out, end, sems in ((gk_out, k_end, k_end_sems), (gv_out, v_end, v_end_sems)):
        ended(end, sems)
        for column in range(CORES):
            target = out.at[:, pl.ds(column * COLS, COLS)]
            add_rows(target, [end.at[side, column] for side in range(3)], HALF)
    send.finish()
    assert len(send.copies) == REDUCE_COPIES, len(send.copies)


def reduce_parts(dq_part, dk_part, dv_part):
    two = pltpu.VMEM((2, 2, BLK, COLS), BF16)
    near = pltpu.VMEM((2, 4, BLK, COLS), BF16)
    four = pltpu.VMEM((4, BLK, COLS), BF16)
    half = pltpu.VMEM((2, HALF, COLS), BF16)
    end = pltpu.VMEM((3, CORES, HALF, COLS), BF16)
    inbox = pltpu.VMEM((3, CORES, COLS, BLK), BF16)
    sems = pltpu.SemaphoreType.DMA((3, CORES))
    return pl.pallas_call(
        reduce_kernel,
        out_shape=[
            jax.ShapeDtypeStruct((BLK, WIDTH), BF16),
            jax.ShapeDtypeStruct((HALF, WIDTH), BF16),
            jax.ShapeDtypeStruct((HALF, WIDTH), BF16),
        ],
        in_specs=[VMEM] * 3,
        out_specs=[VMEM] * 3,
        scratch_shapes=[
            pltpu.VMEM((NZ, CORES, COLS, BLK), BF16), inbox, inbox, inbox,
            two, two, near, four, half, end,
            two, two, near, four, half, end,
            pltpu.SemaphoreType.DMA((REDUCE_COPIES,)),
            pltpu.SemaphoreType.DMA((REDUCE_COPIES,)),
            sems, sems, sems,
        ],
        compiler_params=pltpu.CompilerParams(
            collective_id=1, has_side_effects=True, vmem_limit_bytes=VMEM_LIMIT
        ),
        name="reduce_parts",
    )(dq_part.reshape(NZ, CORES, COLS, BLK), dk_part, dv_part)


def body(q, k, v, out, do, lse, block_pairs, counts):
    lists = block_pairs.transpose(0, 2, 3, 1).reshape(2 * SLOTS, KEY_SHARDS)
    arguments = (q, do, k, v, out, lse, lists, counts)
    held = [pltpu.with_memory_space_constraint(array, pltpu.HBM) for array in arguments]
    parts = pairs_over_blocks(*gather(*held))
    return tuple(reduce_parts(*parts))


def solution(mesh):
    placed = (
        P(("pb", "ka"), None),
        P(("ka", "pb"), None),
        P(("ka", "pb"), None),
        P(("pb", "ka"), None),
        P(("pb", "ka"), None),
        P(None, ("pb", "ka")),
        P("pb", None, None, None),
        P("pb", None),
    )
    return jax.shard_map(
        body,
        mesh=mesh,
        in_specs=placed,
        out_specs=(P(("pb", "ka"), None), P(("ka", "pb"), None), P(("ka", "pb"), None)),
        check_vma=False,
    )
```

```python
import jax
import jax.numpy as jnp
from jax import lax
from jax.experimental import pallas as pl
from jax.experimental.pallas import tpu as pltpu
from jax.sharding import PartitionSpec as P

NX, NY, NZ, CORES = 4, 4, 8, 2
HEADS = 16
OWN_HEADS = HEADS // CORES
BLK = 128
HALF = BLK // 2
WIDTH = 1024
COLS = WIDTH // CORES
HEAD_PAIRS = COLS // 128
SLOTS = 24
KEY_SHARDS = NX * NZ
QUERY_BLOCKS = NZ * CORES
KEY_BLOCKS = NX * NY
CELLS = KEY_BLOCKS * QUERY_BLOCKS
NEAR = 5
EARLY = 20
FIRST_EARLY = 9
TABLE = (8, 128)
SCALE = 64**-0.5
LOG2E = 1.4426950408889634
VMEM_LIMIT = 24 << 20
GATHER_LIMIT = 16 << 20
PAIR_LIMIT = 16 << 20
MESH = pl.DeviceIdType.MESH
HBM = pl.BlockSpec(memory_space=pltpu.HBM)
VMEM = pl.BlockSpec(memory_space=pltpu.VMEM)
F32 = jnp.float32
BF16 = jnp.bfloat16


class Place:
    def __init__(self):
        pb = lax.axis_index("pb")
        ka = lax.axis_index("ka")
        self.y = lax.div(pb, CORES)
        self.core = lax.rem(pb, CORES)
        self.x = lax.div(ka, NZ)
        self.z = lax.rem(ka, NZ)
        self.sibling = (self.y * CORES + 1 - self.core, ka)

    def aim(self, crossed, owner):
        if owner is not None:
            return owner
        return 1 - self.core if crossed else self.core

    def over_x(self, step, crossed=0, owner=None):
        return (self.y * CORES + self.aim(crossed, owner), self.xs(step) * NZ + self.z)

    def over_y(self, step, crossed=0, owner=None):
        return (self.ys(step) * CORES + self.aim(crossed, owner), self.x * NZ + self.z)

    def over_z(self, step, crossed=0, owner=None):
        return (self.y * CORES + self.aim(crossed, owner), self.x * NZ + self.zs(step))

    def xs(self, step):
        return lax.rem(self.x + step + NX, NX)

    def ys(self, step):
        return lax.rem(self.y + step + NY, NY)

    def zs(self, step):
        return lax.rem(self.z + step + NZ, NZ)

    def greet(self, both_cores=False):
        barrier = pltpu.get_barrier_semaphore()
        neighbours = [self.sibling]
        for step in (1, -1):
            for crossed in (0, 1) if both_cores else (0,):
                for over in (self.over_x, self.over_y, self.over_z):
                    neighbours.append(over(step, crossed))
        for neighbour in neighbours:
            pl.semaphore_signal(barrier, inc=1, device_id=neighbour, device_id_type=MESH)
        pl.semaphore_wait(barrier, len(neighbours))


class Sender:
    def __init__(self, send_sems, recv_sems):
        self.send_sems = send_sems
        self.recv_sems = recv_sems
        self.copies = []

    def __call__(self, source, target, device, recv_sem=None):
        index = len(self.copies)
        copy = pltpu.make_async_remote_copy(
            src_ref=source,
            dst_ref=target,
            send_sem=self.send_sems.at[index],
            recv_sem=self.recv_sems.at[index] if recv_sem is None else recv_sem,
            device_id=device,
            device_id_type=MESH,
        )
        copy.start()
        self.copies.append(copy)
        return copy

    def finish(self):
        for copy in self.copies:
            copy.wait_send()


NT = (((1,), (1,)), ((), ()))
NN = (((1,), (0,)), ((), ()))


def pair_lanes(pair):
    return slice(pair * 128, pair * 128 + 128)


def head_halves():
    lane = lax.broadcasted_iota(jnp.int32, (1, 128), 1)
    return (
        jnp.where(lane < 64, 1.0, 0.0).astype(BF16),
        jnp.where(lane < 64, 0.0, 1.0).astype(BF16),
    )


def both_heads(block, halves):
    return jnp.concatenate([block * halves[0], block * halves[1]], axis=0)


def turn_keys(keys, k_turned):
    for pair in range(HEAD_PAIRS):
        turned = jnp.transpose(keys(pair_lanes(pair)).astype(F32)).astype(BF16)
        k_turned[pair_lanes(pair), :] = turned


def pair_products(keys, values, queries, douts, stats, halves, p_buf, ds_buf, keep=None):
    for pair in range(HEAD_PAIRS):
        lanes = pair_lanes(pair)
        scores = lax.dot_general(
            keys(lanes), both_heads(queries(lanes), halves), NT, preferred_element_type=F32
        )
        dprob = lax.dot_general(
            values(lanes), both_heads(douts(lanes), halves), NT, preferred_element_type=F32
        )
        for side in range(2):
            head = 2 * pair + side
            cut = slice(side * BLK, side * BLK + BLK)
            prob = jnp.exp2(scores[:, cut] * (SCALE * LOG2E) - stats(head))
            if keep is not None:
                prob = jnp.where(keep, prob, 0.0)
            p_buf[pair, :, cut] = prob.astype(BF16)
            ds_buf[pair, :, cut] = (prob * (dprob[:, cut] - stats(OWN_HEADS + head))).astype(BF16)


def pair_gradients(queries, douts, halves, p_buf, ds_buf, k_turned, add_dv, add_dk, add_dq):
    for pair in range(HEAD_PAIRS):
        lanes = pair_lanes(pair)
        add_dv(
            lanes,
            lax.dot_general(
                p_buf[pair], both_heads(douts(lanes), halves), NN, preferred_element_type=F32
            ),
        )
        add_dk(
            lanes,
            lax.dot_general(
                ds_buf[pair], both_heads(queries(lanes), halves), NN, preferred_element_type=F32
            ),
        )
        both = lax.dot_general(k_turned[lanes, :], ds_buf[pair], NN, preferred_element_type=F32)
        for side in range(2):
            rows = slice(side * 64, side * 64 + 64)
            low = pair * 128 + side * 64
            add_dq(slice(low, low + 64), both[rows, side * BLK : side * BLK + BLK])


def tabulate(lists, counts, x, z, table):
    cell = lax.broadcasted_iota(jnp.int32, (CELLS, KEY_SHARDS), 0)
    shard = lax.broadcasted_iota(jnp.int32, (SLOTS, KEY_SHARDS), 1)
    slot = lax.broadcasted_iota(jnp.int32, (SLOTS, KEY_SHARDS), 0)
    used = jnp.zeros((CELLS, KEY_SHARDS), F32)
    for owner in range(CORES):
        queries = lists[owner, 0:SLOTS, :]
        blocks = lists[owner, SLOTS : 2 * SLOTS, :]
        column = lax.shift_right_logical(shard, 3)
        ok = (slot < counts[owner]) & ((shard & 7) == z) & (lax.shift_right_logical(queries, 3) == x)
        code = (blocks * NX + column) * QUERY_BLOCKS + (queries & 7) * CORES + owner
        code = jnp.where(ok, code, -1)
        for row in range(SLOTS):
            used = jnp.where(cell == code[row : row + 1, :], 1.0, used)
    used = jnp.max(used, axis=1, keepdims=True)
    order = lax.broadcasted_iota(jnp.int32, (CELLS, 1), 0)
    away = (lax.shift_right_logical(order & 15, 1) - z + 2 + NZ) & 7
    near = jnp.where(away < NEAR, used, 0.0)
    before = lax.broadcasted_iota(jnp.int32, (CELLS, CELLS), 0)
    before = before > lax.broadcasted_iota(jnp.int32, (CELLS, CELLS), 1)
    before = jnp.where(before, 1.0, 0.0).astype(BF16)
    spread = jnp.zeros((CELLS, 128), F32)
    near_rank = lax.dot_general(before, (near + spread).astype(BF16), NN, preferred_element_type=F32)
    early = jnp.where(near_rank < EARLY, near + spread, 0.0)
    others = (used + spread) - early
    other_rank = lax.dot_general(before, others.astype(BF16), NN, preferred_element_type=F32)
    lane = lax.broadcasted_iota(jnp.int32, (CELLS, 128), 1)
    line = lax.broadcasted_iota(jnp.int32, (CELLS, 128), 0)
    number = line.astype(F32)

    def total(values):
        return jnp.sum(values, axis=0, keepdims=True)

    place = lane.astype(F32)
    rows = [
        total(jnp.where(near_rank == place, early * number, 0.0)),
        total(jnp.where(other_rank == place, others * number, 0.0)),
        total(jnp.where(other_rank == place + 128.0, others * number, 0.0)),
        total(jnp.where(line < lane * QUERY_BLOCKS, early, 0.0)),
        total(jnp.where(line < lane * QUERY_BLOCKS, others, 0.0)),
    ]
    table[...] = jnp.zeros(TABLE, jnp.int32)
    for index, row in enumerate(rows):
        table[index : index + 1, :] = row.astype(jnp.int32)


def half_of(core, size):
    return pl.ds(pl.multiple_of(core * size, size), size)


GATHER_COPIES = 58


def gather_kernel(
    q_ref, do_ref, k_ref, v_ref, out_ref, lse_ref, list_ref, count_ref,
    q_all, do_all, st_all, k_all, v_all, table_out, dk_early, dv_early, dq_early,
    do_buf, out_buf, lse_buf, st_buf, list_all, count_all, q_near, do_near, st_near,
    k_turned, p_buf, ds_buf, table, table_s, send_sems, recv_sems, local_sems, near_sems,
):
    me = Place()
    x, y, z, core = me.x, me.y, me.z, me.core
    every = slice(None)
    rows = half_of(core, HALF)
    mine = half_of(core, COLS)
    theirs = half_of(1 - core, COLS)

    loads = [
        pltpu.make_async_copy(do_ref, do_buf, local_sems.at[5]),
        pltpu.make_async_copy(out_ref, out_buf, local_sems.at[6]),
        pltpu.make_async_copy(lse_ref, lse_buf, local_sems.at[7]),
    ]
    for load in loads:
        load.start()
    owns = [
        pltpu.make_async_copy(q_ref.at[every, mine], q_all.at[z, core], local_sems.at[0]),
        pltpu.make_async_copy(do_ref.at[every, mine], do_all.at[z, core], local_sems.at[1]),
        pltpu.make_async_copy(k_ref.at[every, mine], k_all.at[y, x, rows], local_sems.at[2]),
        pltpu.make_async_copy(v_ref.at[every, mine], v_all.at[x, y, rows], local_sems.at[3]),
        pltpu.make_async_copy(list_ref, list_all.at[core], local_sems.at[4]),
        pltpu.make_async_copy(count_ref, count_all.at[core], local_sems.at[8]),
    ]
    for own in owns:
        own.start()
    me.greet(both_cores=True)
    send = Sender(send_sems, recv_sems)
    up, down = me.over_z(1), me.over_z(-1)

    def to_both(ref, target, straight, crossed):
        return [
            send(ref.at[every, mine], target, straight),
            send(ref.at[every, theirs], target, crossed),
        ]

    cross_up, cross_down = me.over_z(1, 1), me.over_z(-1, 1)
    q_up = [to_both(q_ref, q_all.at[z, core], up, cross_up)]
    do_down = [to_both(do_ref, do_all.at[z, core], down, cross_down)]
    k_swap = send(k_ref.at[every, theirs], k_all.at[y, x, rows], me.sibling)
    v_swap = send(v_ref.at[every, theirs], v_all.at[x, y, rows], me.sibling)
    k_right = to_both(k_ref, k_all.at[y, x, rows], me.over_x(1), me.over_x(1, 1))
    k_left = to_both(k_ref, k_all.at[y, x, rows], me.over_x(-1), me.over_x(-1, 1))
    v_right = to_both(v_ref, v_all.at[x, y, rows], me.over_y(1), me.over_y(1, 1))
    v_left = to_both(v_ref, v_all.at[x, y, rows], me.over_y(-1), me.over_y(-1, 1))
    do_up = [to_both(do_ref, do_all.at[z, core], up, cross_up)]
    q_down = [to_both(q_ref, q_all.at[z, core], down, cross_down)]
    swaps = [
        send(q_ref.at[every, theirs], q_all.at[z, core], me.sibling),
        send(do_ref.at[every, theirs], do_all.at[z, core], me.sibling),
        send(list_ref, list_all.at[core], me.sibling),
        send(count_ref, count_all.at[core], me.sibling),
    ]

    for load in loads:
        load.wait()
    products = do_buf[...].astype(F32) * out_buf[...].astype(F32)
    high = products.astype(BF16)
    low = (products - high.astype(F32)).astype(BF16)
    head = lax.broadcasted_iota(jnp.int32, (HEADS, WIDTH), 0) * 64
    feature = lax.broadcasted_iota(jnp.int32, (HEADS, WIDTH), 1)
    member = jnp.where((feature >= head) & (feature < head + 64), 1.0, 0.0).astype(BF16)
    over_features = (((1,), (1,)), ((), ()))
    delta = lax.dot_general(member, high, over_features, preferred_element_type=F32)
    delta = delta + lax.dot_general(member, low, over_features, preferred_element_type=F32)
    for side in range(CORES):
        heads = slice(side * OWN_HEADS, side * OWN_HEADS + OWN_HEADS)
        st_buf[side, 0:OWN_HEADS, :] = lse_buf[heads, :] * LOG2E
        st_buf[side, OWN_HEADS : 2 * OWN_HEADS, :] = delta[heads, :]
    for own in owns:
        own.wait()
    nears = []

    def bring_near(arrays, distance):
        for blocks, held in arrays:
            copy = pltpu.make_async_copy(
                blocks.at[me.zs(distance)], held.at[distance + 2], near_sems.at[len(nears)]
            )
            copy.start()
            nears.append(copy)

    st_own = pltpu.make_async_copy(st_buf.at[core], st_all.at[z, core], local_sems.at[0])
    st_own.start()
    swaps.append(send(st_buf.at[1 - core], st_all.at[z, core], me.sibling))
    st_up, st_down = [], []
    for stats, straight, crossed in ((st_up, up, cross_up), (st_down, down, cross_down)):
        stats.append(
            [
                send(st_buf.at[core], st_all.at[z, core], straight),
                send(st_buf.at[1 - core], st_all.at[z, core], crossed),
            ]
        )

    def arrived(*groups):
        for group in groups:
            for copy in group:
                copy.wait_recv()

    upper, lower = pl.ds(0, HALF), pl.ds(HALF, HALF)
    arrived(k_right)
    k_part = k_all.at[y, me.xs(-1), upper]
    k_far = [send(k_part, k_part, me.over_x(1))]
    arrived(v_right)
    v_part = v_all.at[x, me.ys(-1), upper]
    v_far = [send(v_part, v_part, me.over_y(1))]
    arrived(k_left)
    k_part = k_all.at[y, me.xs(1), lower]
    k_far.append(send(k_part, k_part, me.over_x(-1)))
    arrived(v_left)
    v_part = v_all.at[x, me.ys(1), lower]
    v_far.append(send(v_part, v_part, me.over_y(-1)))

    first, second = pl.ds(0, 2), pl.ds(2, 2)

    def lines(blocks, place, over):
        ahead, back = [], []
        for part_ahead, part_back in ((first, second), (second, first)):
            part = blocks.at[place, part_ahead]
            ahead.append(send(part, part, over(1)))
            part = blocks.at[place, part_back]
            back.append(send(part, part, over(-1)))
        return ahead, back

    arrived([k_swap], k_far)
    k_right, k_left = lines(k_all, y, me.over_y)
    arrived([v_swap], v_far)
    v_right, v_left = lines(v_all, x, me.over_x)

    def forward(hop, sign, blocks, copies):
        arrived(copies[hop - 1])
        block = blocks.at[me.zs(-sign * hop)]
        copies.append([send(block, block, up if sign > 0 else down)])

    forward(1, 1, q_all, q_up)
    forward(1, -1, do_all, do_down)
    arrived(swaps)
    st_own.wait()
    tabulate(list_all, count_all, x, z, table)
    to_scalars = pltpu.make_async_copy(table, table_s, local_sems.at[1])
    to_scalars.start()
    table_store = pltpu.make_async_copy(table, table_out, local_sems.at[2])
    table_store.start()
    every_array = ((q_all, q_near), (do_all, do_near), (st_all, st_near))
    bring_near(every_array, 0)

    def across(copies, blocks, start, part, device):
        arrived(copies[:1])
        part = blocks.at[start, part]
        return send(part, part, device)

    k_far = [across(k_right, k_all, me.ys(-1), first, me.over_y(1))]
    v_far = [across(v_right, v_all, me.xs(-1), first, me.over_x(1))]
    k_far.append(across(k_left, k_all, me.ys(1), second, me.over_y(-1)))
    v_far.append(across(v_left, v_all, me.xs(1), second, me.over_x(-1)))
    forward(1, 1, do_all, do_up)
    forward(1, -1, q_all, q_down)
    forward(1, 1, st_all, st_up)
    forward(1, -1, st_all, st_down)
    bring_near(every_array, 1)
    bring_near(every_array, -1)

    forward(2, 1, q_all, q_up)
    forward(2, -1, do_all, do_down)
    forward(2, 1, do_all, do_up)
    forward(2, -1, q_all, q_down)
    forward(2, 1, st_all, st_up)
    forward(2, -1, st_all, st_down)

    bring_near(every_array, 2)
    bring_near(every_array, -2)
    arrived(k_right[1:], k_left[1:], v_right[1:], v_left[1:], k_far, v_far)
    for copy in nears:
        copy.wait()
    to_scalars.wait()
    halves = head_halves()
    used = table_s[3, KEY_BLOCKS]

    def early(index, carry):
        entry = jnp.clip(table_s[0, index], 0, CELLS - 1)
        block = lax.div(entry, QUERY_BLOCKS)
        up_block, across_block = lax.div(block, NX), lax.rem(block, NX)
        query = lax.rem(lax.div(lax.rem(entry, QUERY_BLOCKS), CORES) - z + 2 + NZ, NZ)
        query = jnp.minimum(query, NEAR - 1)
        owner = lax.rem(entry, CORES)

        def keys(lanes):
            return k_all[up_block, across_block, :, lanes]

        def values(lanes):
            return v_all[across_block, up_block, :, lanes]

        def queries(lanes):
            return q_near[query, owner, :, lanes]

        def douts(lanes):
            return do_near[query, owner, :, lanes]

        def stats(row):
            return st_near[query, owner, row : row + 1, :]

        turn_keys(keys, k_turned)
        pair_products(keys, values, queries, douts, stats, halves, p_buf, ds_buf, keep=index < used)

        def put_dv(lanes, value):
            dv_early[index, :, lanes] = value

        def put_dk(lanes, value):
            dk_early[index, :, lanes] = value

        def put_dq(rows, value):
            dq_early[index, rows, :] = value

        pair_gradients(queries, douts, halves, p_buf, ds_buf, k_turned, put_dv, put_dk, put_dq)
        return carry

    lax.fori_loop(0, FIRST_EARLY, early, 0)
    forward(3, 1, q_all, q_up)
    forward(3, -1, do_all, do_down)
    forward(3, 1, st_all, st_up)
    lax.fori_loop(FIRST_EARLY, EARLY, early, 0)
    arrived(do_up[2], q_down[2], st_down[2], q_up[3], do_down[3], st_up[3])
    table_store.wait()
    send.finish()
    assert len(send.copies) == GATHER_COPIES, len(send.copies)


def gather(q, do, k, v, out, lse, lists, counts):
    return pl.pallas_call(
        gather_kernel,
        out_shape=[
            jax.ShapeDtypeStruct((NZ, CORES, BLK, COLS), BF16),
            jax.ShapeDtypeStruct((NZ, CORES, BLK, COLS), BF16),
            jax.ShapeDtypeStruct((NZ, CORES, 2 * OWN_HEADS, BLK), F32),
            jax.ShapeDtypeStruct((NY, NX, BLK, COLS), BF16),
            jax.ShapeDtypeStruct((NX, NY, BLK, COLS), BF16),
            jax.ShapeDtypeStruct(TABLE, jnp.int32),
            jax.ShapeDtypeStruct((EARLY, BLK, COLS), F32),
            jax.ShapeDtypeStruct((EARLY, BLK, COLS), F32),
            jax.ShapeDtypeStruct((EARLY, COLS, BLK), F32),
        ],
        in_specs=[HBM] * 8,
        out_specs=[VMEM] * 5 + [HBM] + [VMEM] * 3,
        scratch_shapes=[
            pltpu.VMEM((BLK, WIDTH), BF16),
            pltpu.VMEM((BLK, WIDTH), BF16),
            pltpu.VMEM((HEADS, BLK), F32),
            pltpu.VMEM((CORES, 2 * OWN_HEADS, BLK), F32),
            pltpu.VMEM((CORES, 2 * SLOTS, KEY_SHARDS), jnp.int32),
            pltpu.VMEM((CORES, 1, KEY_SHARDS), jnp.int32),
            pltpu.VMEM((NEAR, CORES, BLK, COLS), BF16),
            pltpu.VMEM((NEAR, CORES, BLK, COLS), BF16),
            pltpu.VMEM((NEAR, CORES, 2 * OWN_HEADS, BLK), F32),
            pltpu.VMEM((COLS, BLK), BF16),
            pltpu.VMEM((HEAD_PAIRS, BLK, 2 * BLK), BF16),
            pltpu.VMEM((HEAD_PAIRS, BLK, 2 * BLK), BF16),
            pltpu.VMEM(TABLE, jnp.int32),
            pltpu.SMEM(TABLE, jnp.int32),
            pltpu.SemaphoreType.DMA((GATHER_COPIES,)),
            pltpu.SemaphoreType.DMA((GATHER_COPIES,)),
            pltpu.SemaphoreType.DMA((9,)),
            pltpu.SemaphoreType.DMA((3 * NEAR,)),
        ],
        compiler_params=pltpu.CompilerParams(
            collective_id=0, has_side_effects=True, vmem_limit_bytes=GATHER_LIMIT
        ),
        name="gather_blocks",
    )(q, do, k, v, out, lse, lists, counts)


def pair_kernel(
    table, q_all, do_all, st_all, k_all, v_all, dk_early, dv_early, dq_early,
    dq_out, dk_out, dv_out,
    k_turned, p_buf, ds_buf, dq_sum, dk_sum, dv_sum,
):
    def clear(query, carry):
        dq_sum[query] = jnp.zeros((COLS, BLK), F32)
        return carry

    lax.fori_loop(0, QUERY_BLOCKS, clear, 0)
    halves = head_halves()

    def key_block(block, carry):
        up, across = lax.div(block, NX), lax.rem(block, NX)
        early_low, early_high = table[3, block], table[3, block + 1]
        low, high = table[4, block], table[4, block + 1]
        have = (early_high - early_low) + (high - low)

        @pl.when(have == 0)
        def _():
            dk_out[up, across] = jnp.zeros((BLK, COLS), BF16)
            dv_out[across, up] = jnp.zeros((BLK, COLS), BF16)

        def keys(lanes):
            return k_all[up, across, :, lanes]

        def values(lanes):
            return v_all[across, up, :, lanes]

        def take(slot, carry):
            query = lax.rem(table[0, slot], QUERY_BLOCKS)
            dk_sum[...] += dk_early[slot]
            dv_sum[...] += dv_early[slot]
            dq_sum[query] += dq_early[slot]
            return carry

        def used(slot, carry):
            query = lax.rem(table[1 + lax.div(slot, 128), lax.rem(slot, 128)], QUERY_BLOCKS)

            def queries(lanes):
                return q_all[query, :, lanes]

            def douts(lanes):
                return do_all[query, :, lanes]

            def stats(row):
                return st_all[query, row : row + 1, :]

            pair_products(keys, values, queries, douts, stats, halves, p_buf, ds_buf)

            def add_dv(lanes, value):
                dv_sum[:, lanes] += value

            def add_dk(lanes, value):
                dk_sum[:, lanes] += value

            def add_dq(rows, value):
                dq_sum[query, rows, :] += value

            pair_gradients(queries, douts, halves, p_buf, ds_buf, k_turned, add_dv, add_dk, add_dq)
            return carry

        @pl.when(have > 0)
        def _():
            dk_sum[...] = jnp.zeros_like(dk_sum)
            dv_sum[...] = jnp.zeros_like(dv_sum)
            lax.fori_loop(early_low, early_high, take, 0)

            @pl.when(high > low)
            def _():
                turn_keys(keys, k_turned)

            lax.fori_loop(low, high, used, 0)
            dk_out[up, across] = (dk_sum[...] * SCALE).astype(BF16)
            dv_out[across, up] = dv_sum[...].astype(BF16)

        return carry

    lax.fori_loop(0, KEY_BLOCKS, key_block, 0)

    def turn_in(query, carry):
        dq_out[query] = (dq_sum[query] * SCALE).astype(BF16)
        return carry

    lax.fori_loop(0, QUERY_BLOCKS, turn_in, 0)


def pairs_over_blocks(q_all, do_all, st_all, k_all, v_all, table, dk_early, dv_early, dq_early):
    return pl.pallas_call(
        pair_kernel,
        out_shape=[
            jax.ShapeDtypeStruct((QUERY_BLOCKS, COLS, BLK), BF16),
            jax.ShapeDtypeStruct((NY, NX, BLK, COLS), BF16),
            jax.ShapeDtypeStruct((NX, NY, BLK, COLS), BF16),
        ],
        in_specs=[pl.BlockSpec(memory_space=pltpu.SMEM)] + [VMEM] * 8,
        out_specs=[VMEM] * 3,
        scratch_shapes=[
            pltpu.VMEM((COLS, BLK), BF16),
            pltpu.VMEM((HEAD_PAIRS, BLK, 2 * BLK), BF16),
            pltpu.VMEM((HEAD_PAIRS, BLK, 2 * BLK), BF16),
            pltpu.VMEM((QUERY_BLOCKS, COLS, BLK), F32),
            pltpu.VMEM((BLK, COLS), F32),
            pltpu.VMEM((BLK, COLS), F32),
        ],
        compiler_params=pltpu.CompilerParams(vmem_limit_bytes=PAIR_LIMIT),
        name="used_pairs",
    )(
        table,
        q_all.reshape(QUERY_BLOCKS, BLK, COLS),
        do_all.reshape(QUERY_BLOCKS, BLK, COLS),
        st_all.reshape(QUERY_BLOCKS, 2 * OWN_HEADS, BLK),
        k_all,
        v_all,
        dk_early,
        dv_early,
        dq_early,
    )


REDUCE_COPIES = 41
ROW_STEP = 16


def reduce_kernel(
    dq_part, dk_part, dv_part,
    gq_out, gk_out, gv_out,
    dq_own, dq_in_up, dq_in_down, dq_end,
    k_out, k_far, k_near, k_mid, k_mid_far, k_end,
    v_out, v_far, v_near, v_mid, v_mid_far, v_end,
    send_sems, recv_sems, q_end_sems, k_end_sems, v_end_sems,
):
    me = Place()
    x, y, z, core = me.x, me.y, me.z, me.core
    first, second = pl.ds(0, 2), pl.ds(2, 2)
    me.greet(both_cores=True)
    send = Sender(send_sems, recv_sems)
    up, down = me.over_z(1), me.over_z(-1)

    def add_rows(total, terms, count):
        def one(index, carry):
            at = pl.ds(pl.multiple_of(index * ROW_STEP, ROW_STEP), ROW_STEP)
            value = terms[0][at, :].astype(F32)
            for term in terms[1:]:
                value = value + term[at, :].astype(F32)
            total[at, :] = value.astype(total.dtype)
            return carry

        lax.fori_loop(0, count // ROW_STEP, one, 0, unroll=4)

    arrive = {
        ("up", 0, 1): send(dq_part.at[me.zs(4), 0], dq_in_up.at[0, 0], up),
        ("down", 1, 1): send(dq_part.at[me.zs(4), 1], dq_in_down.at[0, 1], down),
    }
    k_a = send(dk_part.at[me.ys(2), first], k_far.at[0], me.over_y(1))
    k_b = send(dk_part.at[me.ys(2), second], k_far.at[1], me.over_y(-1))
    v_a = send(dv_part.at[me.xs(2), first], v_far.at[0], me.over_x(1))
    v_b = send(dv_part.at[me.xs(2), second], v_far.at[1], me.over_x(-1))
    arrive["up", 1, 2] = send(dq_part.at[me.zs(3), 1], dq_in_up.at[1, 1], up)
    arrive["down", 0, 2] = send(dq_part.at[me.zs(-3), 0], dq_in_down.at[1, 0], down)
    k_in = [
        send(dk_part.at[me.ys(1), second], k_near.at[0, second], me.over_y(1)),
        send(dk_part.at[me.ys(-1), first], k_near.at[1, first], me.over_y(-1)),
    ]
    v_in = [
        send(dv_part.at[me.xs(1), second], v_near.at[0, second], me.over_x(1)),
        send(dv_part.at[me.xs(-1), first], v_near.at[1, first], me.over_x(-1)),
    ]
    q_sib = send(dq_part.at[z, 1 - core], dq_end.at[2, core], me.sibling, q_end_sems.at[2, core])

    def hop_q(direction, shard, hop):
        if direction == "up":
            side, step, inbox, way = 0, 4 - hop, dq_in_up, 1
        else:
            side, step, inbox, way = 1, hop - 4, dq_in_down, -1
        own = dq_own.at[me.zs(step), shard]
        arrive[direction, shard, hop].wait_recv()
        add_rows(own, [dq_part.at[me.zs(step), shard], inbox.at[hop - 1, shard]], COLS)
        if hop < 3:
            arrive[direction, shard, hop + 1] = send(own, inbox.at[hop, shard], me.over_z(way))
        else:
            send(own, dq_end.at[side, core], me.over_z(way, owner=shard), q_end_sems.at[side, core])

    add_rows(dq_end.at[2, core], [dq_part.at[z, core]], COLS)
    hop_q("up", 0, 1)
    hop_q("down", 1, 1)

    def onward(arrival, part, place, base, inbox, outbox):
        arrival.wait_recv()
        for row in range(2):
            add_rows(outbox.at[row], [part.at[place, base + row], inbox.at[row]], BLK)

    onward(k_a, dk_part, me.ys(1), 0, k_far.at[0], k_out.at[0])
    k_in.append(send(k_out.at[0], k_near.at[0, first], me.over_y(1)))
    onward(v_a, dv_part, me.xs(1), 0, v_far.at[0], v_out.at[0])
    v_in.append(send(v_out.at[0], v_near.at[0, first], me.over_x(1)))
    onward(k_b, dk_part, me.ys(-1), 2, k_far.at[1], k_out.at[1])
    k_in.append(send(k_out.at[1], k_near.at[1, second], me.over_y(-1)))
    onward(v_b, dv_part, me.xs(-1), 2, v_far.at[1], v_out.at[1])
    v_in.append(send(v_out.at[1], v_near.at[1, second], me.over_x(-1)))
    for hop, shard in ((2, 1), (2, 0), (3, 1), (3, 0)):
        hop_q("up", shard, hop)
        hop_q("down", 1 - shard, hop)

    half_rows = (pl.ds(0, HALF), pl.ds(HALF, HALF))

    def mix(own, here, near, middle, row):
        add_rows(middle.at[row], [own.at[here, row], near.at[0, row], near.at[1, row]], BLK)

    def turn_far(arrivals, own, here, near, middle, far, axis, over):
        for arrival in arrivals:
            arrival.wait_recv()
        farthest = axis(2)
        mix(own, here, near, middle, farthest)
        far_a = send(middle.at[farthest, half_rows[0]], far.at[0], over(1))
        far_b = send(middle.at[farthest, half_rows[1]], far.at[1], over(-1))
        return far_a, far_b

    def turn_near(own, here, near, middle, end, sems, axis, over, place):
        for side, step in enumerate((1, -1)):
            row, owner = axis(step), 1 - side
            mix(own, here, near, middle, row)
            part = middle.at[row, half_rows[owner]]
            send(part, end.at[side, core], over(step, owner=owner), sems.at[side, core])
        mix(own, here, near, middle, place)
        send(middle.at[place, half_of(1 - core, HALF)], end.at[2, core], me.sibling, sems.at[2, core])
        end[2, core] = middle[place, half_of(core, HALF), :]

    def last(arrival, middle, at, half, far, end, sems, side, device):
        arrival.wait_recv()
        part = middle.at[at, half_rows[half]]
        add_rows(part, [part, far], HALF)
        send(part, end.at[side, core], device, sems.at[side, core])

    kx_a, kx_b = turn_far(k_in, dk_part, y, k_near, k_mid, k_mid_far, me.xs, me.over_x)
    vy_a, vy_b = turn_far(v_in, dv_part, x, v_near, v_mid, v_mid_far, me.ys, me.over_y)
    turn_near(dk_part, y, k_near, k_mid, k_end, k_end_sems, me.xs, me.over_x, x)
    turn_near(dv_part, x, v_near, v_mid, v_end, v_end_sems, me.ys, me.over_y, y)
    last(kx_a, k_mid, me.xs(1), 0, k_mid_far.at[0], k_end, k_end_sems, 0, me.over_x(1, owner=0))
    last(kx_b, k_mid, me.xs(-1), 1, k_mid_far.at[1], k_end, k_end_sems, 1, me.over_x(-1, owner=1))
    last(vy_a, v_mid, me.ys(1), 0, v_mid_far.at[0], v_end, v_end_sems, 0, me.over_y(1, owner=0))
    last(vy_b, v_mid, me.ys(-1), 1, v_mid_far.at[1], v_end, v_end_sems, 1, me.over_y(-1, owner=1))

    def ended(end, sems):
        for side in range(2):
            for column in range(CORES):
                pltpu.make_async_copy(end.at[side, column], end.at[side, column], sems.at[side, column]).wait()
        other = end.at[2, 1 - core]
        pltpu.make_async_copy(other, other, sems.at[2, 1 - core]).wait()

    ended(dq_end, q_end_sems)
    for column in range(CORES):
        for tile in range(COLS // 128):
            at = pl.ds(tile * 128, 128)
            value = (
                dq_end[0, column, at, :].astype(F32)
                + dq_end[1, column, at, :].astype(F32)
                + dq_end[2, column, at, :].astype(F32)
            )
            gq_out[:, pl.ds(column * COLS + tile * 128, 128)] = jnp.transpose(value).astype(BF16)
    for out, end, sems in ((gk_out, k_end, k_end_sems), (gv_out, v_end, v_end_sems)):
        ended(end, sems)
        for column in range(CORES):
            target = out.at[:, pl.ds(column * COLS, COLS)]
            add_rows(target, [end.at[side, column] for side in range(3)], HALF)
    send.finish()
    assert len(send.copies) == REDUCE_COPIES, len(send.copies)


def reduce_parts(dq_part, dk_part, dv_part):
    two = pltpu.VMEM((2, 2, BLK, COLS), BF16)
    near = pltpu.VMEM((2, 4, BLK, COLS), BF16)
    four = pltpu.VMEM((4, BLK, COLS), BF16)
    half = pltpu.VMEM((2, HALF, COLS), BF16)
    end = pltpu.VMEM((3, CORES, HALF, COLS), BF16)
    inbox = pltpu.VMEM((3, CORES, COLS, BLK), BF16)
    sems = pltpu.SemaphoreType.DMA((3, CORES))
    return pl.pallas_call(
        reduce_kernel,
        out_shape=[
            jax.ShapeDtypeStruct((BLK, WIDTH), BF16),
            jax.ShapeDtypeStruct((HALF, WIDTH), BF16),
            jax.ShapeDtypeStruct((HALF, WIDTH), BF16),
        ],
        in_specs=[VMEM] * 3,
        out_specs=[VMEM] * 3,
        scratch_shapes=[
            pltpu.VMEM((NZ, CORES, COLS, BLK), BF16), inbox, inbox, inbox,
            two, two, near, four, half, end,
            two, two, near, four, half, end,
            pltpu.SemaphoreType.DMA((REDUCE_COPIES,)),
            pltpu.SemaphoreType.DMA((REDUCE_COPIES,)),
            sems, sems, sems,
        ],
        compiler_params=pltpu.CompilerParams(
            collective_id=1, has_side_effects=True, vmem_limit_bytes=VMEM_LIMIT
        ),
        name="reduce_parts",
    )(dq_part.reshape(NZ, CORES, COLS, BLK), dk_part, dv_part)


def body(q, k, v, out, do, lse, block_pairs, counts):
    lists = block_pairs.transpose(0, 2, 3, 1).reshape(2 * SLOTS, KEY_SHARDS)
    arguments = (q, do, k, v, out, lse, lists, counts)
    held = [pltpu.with_memory_space_constraint(array, pltpu.HBM) for array in arguments]
    parts = pairs_over_blocks(*gather(*held))
    return tuple(reduce_parts(*parts))


def solution(mesh):
    placed = (
        P(("pb", "ka"), None),
        P(("ka", "pb"), None),
        P(("ka", "pb"), None),
        P(("pb", "ka"), None),
        P(("pb", "ka"), None),
        P(None, ("pb", "ka")),
        P("pb", None, None, None),
        P("pb", None),
    )
    return jax.shard_map(
        body,
        mesh=mesh,
        in_specs=placed,
        out_specs=(P(("pb", "ka"), None), P(("ka", "pb"), None), P(("ka", "pb"), None)),
        check_vma=False,
    )
```

```python
import jax
import jax.numpy as jnp
from jax import lax
from jax.experimental import pallas as pl
from jax.experimental.pallas import tpu as pltpu
from jax.sharding import PartitionSpec as P

NX, NY, NZ, CORES = 4, 4, 8, 2
HEADS = 16
OWN_HEADS = HEADS // CORES
BLK = 128
HALF = BLK // 2
WIDTH = 1024
COLS = WIDTH // CORES
HEAD_PAIRS = COLS // 128
SLOTS = 24
KEY_SHARDS = NX * NZ
QUERY_BLOCKS = NZ * CORES
KEY_BLOCKS = NX * NY
CELLS = KEY_BLOCKS * QUERY_BLOCKS
NEAR = 5
FIRST = 8
SECOND = 17
EARLY = FIRST + SECOND
BEFORE_HOP = 5
LINES = 3
TABLE = (8, 128)
SCALE = 64**-0.5
LOG2E = 1.4426950408889634
VMEM_LIMIT = 24 << 20
GATHER_LIMIT = 16 << 20
PAIR_LIMIT = 16 << 20
MESH = pl.DeviceIdType.MESH
HBM = pl.BlockSpec(memory_space=pltpu.HBM)
VMEM = pl.BlockSpec(memory_space=pltpu.VMEM)
F32 = jnp.float32
BF16 = jnp.bfloat16


class Place:
    def __init__(self):
        pb = lax.axis_index("pb")
        ka = lax.axis_index("ka")
        self.y = lax.div(pb, CORES)
        self.core = lax.rem(pb, CORES)
        self.x = lax.div(ka, NZ)
        self.z = lax.rem(ka, NZ)
        self.sibling = (self.y * CORES + 1 - self.core, ka)

    def aim(self, crossed, owner):
        if owner is not None:
            return owner
        return 1 - self.core if crossed else self.core

    def over_x(self, step, crossed=0, owner=None):
        return (self.y * CORES + self.aim(crossed, owner), self.xs(step) * NZ + self.z)

    def over_y(self, step, crossed=0, owner=None):
        return (self.ys(step) * CORES + self.aim(crossed, owner), self.x * NZ + self.z)

    def over_z(self, step, crossed=0, owner=None):
        return (self.y * CORES + self.aim(crossed, owner), self.x * NZ + self.zs(step))

    def xs(self, step):
        return lax.rem(self.x + step + NX, NX)

    def ys(self, step):
        return lax.rem(self.y + step + NY, NY)

    def zs(self, step):
        return lax.rem(self.z + step + NZ, NZ)

    def greet(self, both_cores=False):
        barrier = pltpu.get_barrier_semaphore()
        neighbours = [self.sibling]
        for step in (1, -1):
            for crossed in (0, 1) if both_cores else (0,):
                for over in (self.over_x, self.over_y, self.over_z):
                    neighbours.append(over(step, crossed))
        for neighbour in neighbours:
            pl.semaphore_signal(barrier, inc=1, device_id=neighbour, device_id_type=MESH)
        pl.semaphore_wait(barrier, len(neighbours))


class Sender:
    def __init__(self, send_sems, recv_sems):
        self.send_sems = send_sems
        self.recv_sems = recv_sems
        self.copies = []

    def __call__(self, source, target, device, recv_sem=None):
        index = len(self.copies)
        copy = pltpu.make_async_remote_copy(
            src_ref=source,
            dst_ref=target,
            send_sem=self.send_sems.at[index],
            recv_sem=self.recv_sems.at[index] if recv_sem is None else recv_sem,
            device_id=device,
            device_id_type=MESH,
        )
        copy.start()
        self.copies.append(copy)
        return copy

    def finish(self):
        for copy in self.copies:
            copy.wait_send()


NT = (((1,), (1,)), ((), ()))
NN = (((1,), (0,)), ((), ()))


def pair_lanes(pair):
    return slice(pair * 128, pair * 128 + 128)


def head_halves():
    lane = lax.broadcasted_iota(jnp.int32, (1, 128), 1)
    return (
        jnp.where(lane < 64, 1.0, 0.0).astype(BF16),
        jnp.where(lane < 64, 0.0, 1.0).astype(BF16),
    )


def both_heads(block, halves):
    return jnp.concatenate([block * halves[0], block * halves[1]], axis=0)


def turn_keys(keys, k_turned):
    for pair in range(HEAD_PAIRS):
        turned = jnp.transpose(keys(pair_lanes(pair)).astype(F32)).astype(BF16)
        k_turned[pair_lanes(pair), :] = turned


def pair_products(keys, values, queries, douts, stats, halves, p_buf, ds_buf, keep=None):
    for pair in range(HEAD_PAIRS):
        lanes = pair_lanes(pair)
        scores = lax.dot_general(
            keys(lanes), both_heads(queries(lanes), halves), NT, preferred_element_type=F32
        )
        dprob = lax.dot_general(
            values(lanes), both_heads(douts(lanes), halves), NT, preferred_element_type=F32
        )
        for side in range(2):
            head = 2 * pair + side
            cut = slice(side * BLK, side * BLK + BLK)
            prob = jnp.exp2(scores[:, cut] * (SCALE * LOG2E) - stats(head))
            if keep is not None:
                prob = jnp.where(keep, prob, 0.0)
            p_buf[pair, :, cut] = prob.astype(BF16)
            ds_buf[pair, :, cut] = (prob * (dprob[:, cut] - stats(OWN_HEADS + head))).astype(BF16)


def pair_gradients(queries, douts, halves, p_buf, ds_buf, k_turned, add_dv, add_dk, add_dq):
    for pair in range(HEAD_PAIRS):
        lanes = pair_lanes(pair)
        add_dv(
            lanes,
            lax.dot_general(
                p_buf[pair], both_heads(douts(lanes), halves), NN, preferred_element_type=F32
            ),
        )
        add_dk(
            lanes,
            lax.dot_general(
                ds_buf[pair], both_heads(queries(lanes), halves), NN, preferred_element_type=F32
            ),
        )
        both = lax.dot_general(k_turned[lanes, :], ds_buf[pair], NN, preferred_element_type=F32)
        for side in range(2):
            rows = slice(side * 64, side * 64 + 64)
            low = pair * 128 + side * 64
            add_dq(slice(low, low + 64), both[rows, side * BLK : side * BLK + BLK])


def tabulate(lists, counts, x, y, z, table):
    cell = lax.broadcasted_iota(jnp.int32, (CELLS, KEY_SHARDS), 0)
    shard = lax.broadcasted_iota(jnp.int32, (SLOTS, KEY_SHARDS), 1)
    slot = lax.broadcasted_iota(jnp.int32, (SLOTS, KEY_SHARDS), 0)
    used = jnp.zeros((CELLS, KEY_SHARDS), F32)
    for owner in range(CORES):
        queries = lists[owner, 0:SLOTS, :]
        blocks = lists[owner, SLOTS : 2 * SLOTS, :]
        column = lax.shift_right_logical(shard, 3)
        ok = (slot < counts[owner]) & ((shard & 7) == z) & (lax.shift_right_logical(queries, 3) == x)
        code = (blocks * NX + column) * QUERY_BLOCKS + (queries & 7) * CORES + owner
        code = jnp.where(ok, code, -1)
        for row in range(SLOTS):
            used = jnp.where(cell == code[row : row + 1, :], 1.0, used)
    used = jnp.max(used, axis=1, keepdims=True)
    order = lax.broadcasted_iota(jnp.int32, (CELLS, 1), 0)
    away = (lax.shift_right_logical(order & 15, 1) - z + 2 + NZ) & 7
    near = jnp.where(away < NEAR, used, 0.0)
    before = lax.broadcasted_iota(jnp.int32, (CELLS, CELLS), 0)
    before = before > lax.broadcasted_iota(jnp.int32, (CELLS, CELLS), 1)
    before = jnp.where(before, 1.0, 0.0).astype(BF16)
    spread = jnp.zeros((CELLS, 128), F32)
    up_block = lax.shift_right_logical(order, 6)
    across_block = lax.shift_right_logical(order, 4) & 3
    close = (((up_block - y + 1 + NY) & 3) < LINES) & (((across_block - x + 1 + NX) & 3) < LINES)

    def ranks(cells):
        return lax.dot_general(before, cells.astype(BF16), NN, preferred_element_type=F32)

    closest = jnp.where(close, near, 0.0) + spread
    first_rank = ranks(closest)
    first = jnp.where(first_rank < FIRST, closest, 0.0)
    second = (near + spread) - first
    second_rank = ranks(second)
    second = jnp.where(second_rank < SECOND, second, 0.0)
    others = (used + spread) - first - second
    other_rank = ranks(others)
    lane = lax.broadcasted_iota(jnp.int32, (CELLS, 128), 1)
    line = lax.broadcasted_iota(jnp.int32, (CELLS, 128), 0)
    number = line.astype(F32)

    def total(values):
        return jnp.sum(values, axis=0, keepdims=True)

    place = lane.astype(F32)
    rows = [
        total(jnp.where(first_rank == place, first * number, 0.0))
        + total(jnp.where(second_rank + FIRST == place, second * number, 0.0)),
        total(jnp.where(other_rank == place, others * number, 0.0)),
        total(jnp.where(other_rank == place + 128.0, others * number, 0.0)),
        total(jnp.where(line < lane * QUERY_BLOCKS, first, 0.0)),
        total(jnp.where(line < lane * QUERY_BLOCKS, others, 0.0)),
        total(jnp.where(line < lane * QUERY_BLOCKS, second, 0.0)),
    ]
    table[...] = jnp.zeros(TABLE, jnp.int32)
    for index, row in enumerate(rows):
        table[index : index + 1, :] = row.astype(jnp.int32)


def half_of(core, size):
    return pl.ds(pl.multiple_of(core * size, size), size)


GATHER_COPIES = 58


def gather_kernel(
    q_ref, do_ref, k_ref, v_ref, out_ref, lse_ref, list_ref, count_ref,
    q_all, do_all, st_all, k_all, v_all, table_out, dk_early, dv_early, dq_early,
    do_buf, out_buf, lse_buf, st_buf, list_all, count_all, q_near, do_near, st_near, k_near, v_near,
    k_turned, p_buf, ds_buf, table, table_s, send_sems, recv_sems, local_sems, near_sems,
):
    me = Place()
    x, y, z, core = me.x, me.y, me.z, me.core
    every = slice(None)
    rows = half_of(core, HALF)
    mine = half_of(core, COLS)
    theirs = half_of(1 - core, COLS)

    loads = [
        pltpu.make_async_copy(do_ref, do_buf, local_sems.at[5]),
        pltpu.make_async_copy(out_ref, out_buf, local_sems.at[6]),
        pltpu.make_async_copy(lse_ref, lse_buf, local_sems.at[7]),
    ]
    for load in loads:
        load.start()
    owns = [
        pltpu.make_async_copy(q_ref.at[every, mine], q_all.at[z, core], local_sems.at[0]),
        pltpu.make_async_copy(do_ref.at[every, mine], do_all.at[z, core], local_sems.at[1]),
        pltpu.make_async_copy(k_ref.at[every, mine], k_all.at[y, x, rows], local_sems.at[2]),
        pltpu.make_async_copy(v_ref.at[every, mine], v_all.at[x, y, rows], local_sems.at[3]),
        pltpu.make_async_copy(list_ref, list_all.at[core], local_sems.at[4]),
        pltpu.make_async_copy(count_ref, count_all.at[core], local_sems.at[8]),
    ]
    for own in owns:
        own.start()
    me.greet(both_cores=True)
    send = Sender(send_sems, recv_sems)
    up, down = me.over_z(1), me.over_z(-1)

    def to_both(ref, target, straight, crossed):
        return [
            send(ref.at[every, mine], target, straight),
            send(ref.at[every, theirs], target, crossed),
        ]

    cross_up, cross_down = me.over_z(1, 1), me.over_z(-1, 1)
    q_up = [to_both(q_ref, q_all.at[z, core], up, cross_up)]
    do_down = [to_both(do_ref, do_all.at[z, core], down, cross_down)]
    k_swap = send(k_ref.at[every, theirs], k_all.at[y, x, rows], me.sibling)
    v_swap = send(v_ref.at[every, theirs], v_all.at[x, y, rows], me.sibling)
    k_right = to_both(k_ref, k_all.at[y, x, rows], me.over_x(1), me.over_x(1, 1))
    k_left = to_both(k_ref, k_all.at[y, x, rows], me.over_x(-1), me.over_x(-1, 1))
    v_right = to_both(v_ref, v_all.at[x, y, rows], me.over_y(1), me.over_y(1, 1))
    v_left = to_both(v_ref, v_all.at[x, y, rows], me.over_y(-1), me.over_y(-1, 1))
    do_up = [to_both(do_ref, do_all.at[z, core], up, cross_up)]
    q_down = [to_both(q_ref, q_all.at[z, core], down, cross_down)]
    swaps = [
        send(q_ref.at[every, theirs], q_all.at[z, core], me.sibling),
        send(do_ref.at[every, theirs], do_all.at[z, core], me.sibling),
        send(list_ref, list_all.at[core], me.sibling),
        send(count_ref, count_all.at[core], me.sibling),
    ]

    for load in loads:
        load.wait()
    products = do_buf[...].astype(F32) * out_buf[...].astype(F32)
    high = products.astype(BF16)
    low = (products - high.astype(F32)).astype(BF16)
    head = lax.broadcasted_iota(jnp.int32, (HEADS, WIDTH), 0) * 64
    feature = lax.broadcasted_iota(jnp.int32, (HEADS, WIDTH), 1)
    member = jnp.where((feature >= head) & (feature < head + 64), 1.0, 0.0).astype(BF16)
    over_features = (((1,), (1,)), ((), ()))
    delta = lax.dot_general(member, high, over_features, preferred_element_type=F32)
    delta = delta + lax.dot_general(member, low, over_features, preferred_element_type=F32)
    for side in range(CORES):
        heads = slice(side * OWN_HEADS, side * OWN_HEADS + OWN_HEADS)
        st_buf[side, 0:OWN_HEADS, :] = lse_buf[heads, :] * LOG2E
        st_buf[side, OWN_HEADS : 2 * OWN_HEADS, :] = delta[heads, :]
    for own in owns:
        own.wait()
    nears = []

    def bring_near(arrays, distance):
        for blocks, held in arrays:
            copy = pltpu.make_async_copy(
                blocks.at[me.zs(distance)], held.at[distance + 2], near_sems.at[len(nears)]
            )
            copy.start()
            nears.append(copy)

    st_own = pltpu.make_async_copy(st_buf.at[core], st_all.at[z, core], local_sems.at[0])
    st_own.start()
    swaps.append(send(st_buf.at[1 - core], st_all.at[z, core], me.sibling))
    st_up, st_down = [], []
    for stats, straight, crossed in ((st_up, up, cross_up), (st_down, down, cross_down)):
        stats.append(
            [
                send(st_buf.at[core], st_all.at[z, core], straight),
                send(st_buf.at[1 - core], st_all.at[z, core], crossed),
            ]
        )

    def arrived(*groups):
        for group in groups:
            for copy in group:
                copy.wait_recv()

    upper, lower = pl.ds(0, HALF), pl.ds(HALF, HALF)
    arrived(k_right)
    k_part = k_all.at[y, me.xs(-1), upper]
    k_far = [send(k_part, k_part, me.over_x(1))]
    arrived(v_right)
    v_part = v_all.at[x, me.ys(-1), upper]
    v_far = [send(v_part, v_part, me.over_y(1))]
    arrived(k_left)
    k_part = k_all.at[y, me.xs(1), lower]
    k_far.append(send(k_part, k_part, me.over_x(-1)))
    arrived(v_left)
    v_part = v_all.at[x, me.ys(1), lower]
    v_far.append(send(v_part, v_part, me.over_y(-1)))

    first, second = pl.ds(0, 2), pl.ds(2, 2)

    def lines(blocks, place, over):
        ahead, back = [], []
        for part_ahead, part_back in ((first, second), (second, first)):
            part = blocks.at[place, part_ahead]
            ahead.append(send(part, part, over(1)))
            part = blocks.at[place, part_back]
            back.append(send(part, part, over(-1)))
        return ahead, back

    arrived([k_swap], k_far)
    k_right, k_left = lines(k_all, y, me.over_y)
    arrived([v_swap], v_far)
    v_right, v_left = lines(v_all, x, me.over_x)

    def forward(hop, sign, blocks, copies):
        arrived(copies[hop - 1])
        block = blocks.at[me.zs(-sign * hop)]
        copies.append([send(block, block, up if sign > 0 else down)])

    forward(1, 1, q_all, q_up)
    forward(1, -1, do_all, do_down)
    arrived(swaps)
    st_own.wait()
    tabulate(list_all, count_all, x, y, z, table)
    to_scalars = pltpu.make_async_copy(table, table_s, local_sems.at[1])
    to_scalars.start()
    table_store = pltpu.make_async_copy(table, table_out, local_sems.at[2])
    table_store.start()
    every_array = ((q_all, q_near), (do_all, do_near), (st_all, st_near))
    bring_near(every_array, 0)

    def across(copies, blocks, start, part, device):
        arrived(copies[:1])
        part = blocks.at[start, part]
        return send(part, part, device)

    k_far = [across(k_right, k_all, me.ys(-1), first, me.over_y(1))]
    v_far = [across(v_right, v_all, me.xs(-1), first, me.over_x(1))]
    k_far.append(across(k_left, k_all, me.ys(1), second, me.over_y(-1)))
    v_far.append(across(v_left, v_all, me.xs(1), second, me.over_x(-1)))
    forward(1, 1, do_all, do_up)
    forward(1, -1, q_all, q_down)
    forward(1, 1, st_all, st_up)
    forward(1, -1, st_all, st_down)
    bring_near(every_array, 1)
    bring_near(every_array, -1)

    forward(2, 1, q_all, q_up)
    forward(2, -1, do_all, do_down)
    forward(2, 1, do_all, do_up)
    forward(2, -1, q_all, q_down)
    forward(2, 1, st_all, st_up)
    forward(2, -1, st_all, st_down)

    bring_near(every_array, 2)
    bring_near(every_array, -2)
    arrived(k_right[1:], k_left[1:], v_right[1:], v_left[1:])
    for step in (-1, 0, 1):
        for blocks, line, held in ((k_all, me.ys(step), k_near), (v_all, me.xs(step), v_near)):
            copy = pltpu.make_async_copy(blocks.at[line], held.at[step + 1], near_sems.at[len(nears)])
            copy.start()
            nears.append(copy)
    for copy in nears:
        copy.wait()
    to_scalars.wait()
    halves = head_halves()
    firsts, seconds = table_s[3, KEY_BLOCKS], table_s[5, KEY_BLOCKS]

    def early(index, carry, close=False):
        entry = jnp.clip(table_s[0, index], 0, CELLS - 1)
        block = lax.div(entry, QUERY_BLOCKS)
        up_block, across_block = lax.div(block, NX), lax.rem(block, NX)
        query = lax.rem(lax.div(lax.rem(entry, QUERY_BLOCKS), CORES) - z + 2 + NZ, NZ)
        query = jnp.minimum(query, NEAR - 1)
        owner = lax.rem(entry, CORES)
        keep = index < firsts if close else index - FIRST < seconds
        up_line = jnp.minimum(lax.rem(up_block - y + 1 + NY, NY), LINES - 1)
        across_line = jnp.minimum(lax.rem(across_block - x + 1 + NX, NX), LINES - 1)

        def keys(lanes):
            if close:
                return k_near[up_line, across_block, :, lanes]
            return k_all[up_block, across_block, :, lanes]

        def values(lanes):
            if close:
                return v_near[across_line, up_block, :, lanes]
            return v_all[across_block, up_block, :, lanes]

        def queries(lanes):
            return q_near[query, owner, :, lanes]

        def douts(lanes):
            return do_near[query, owner, :, lanes]

        def stats(row):
            return st_near[query, owner, row : row + 1, :]

        turn_keys(keys, k_turned)
        pair_products(keys, values, queries, douts, stats, halves, p_buf, ds_buf, keep=keep)

        def put_dv(lanes, value):
            dv_early[index, :, lanes] = value

        def put_dk(lanes, value):
            dk_early[index, :, lanes] = value

        def put_dq(rows, value):
            dq_early[index, rows, :] = value

        pair_gradients(queries, douts, halves, p_buf, ds_buf, k_turned, put_dv, put_dk, put_dq)
        return carry

    lax.fori_loop(0, FIRST, lambda index, carry: early(index, carry, close=True), 0)
    arrived(k_far, v_far)
    lax.fori_loop(FIRST, FIRST + BEFORE_HOP, early, 0)
    forward(3, 1, q_all, q_up)
    forward(3, -1, do_all, do_down)
    forward(3, 1, st_all, st_up)
    lax.fori_loop(FIRST + BEFORE_HOP, EARLY, early, 0)
    arrived(do_up[2], q_down[2], st_down[2], q_up[3], do_down[3], st_up[3])
    table_store.wait()
    send.finish()
    assert len(send.copies) == GATHER_COPIES, len(send.copies)


def gather(q, do, k, v, out, lse, lists, counts):
    return pl.pallas_call(
        gather_kernel,
        out_shape=[
            jax.ShapeDtypeStruct((NZ, CORES, BLK, COLS), BF16),
            jax.ShapeDtypeStruct((NZ, CORES, BLK, COLS), BF16),
            jax.ShapeDtypeStruct((NZ, CORES, 2 * OWN_HEADS, BLK), F32),
            jax.ShapeDtypeStruct((NY, NX, BLK, COLS), BF16),
            jax.ShapeDtypeStruct((NX, NY, BLK, COLS), BF16),
            jax.ShapeDtypeStruct(TABLE, jnp.int32),
            jax.ShapeDtypeStruct((EARLY, BLK, COLS), F32),
            jax.ShapeDtypeStruct((EARLY, BLK, COLS), F32),
            jax.ShapeDtypeStruct((EARLY, COLS, BLK), F32),
        ],
        in_specs=[HBM] * 8,
        out_specs=[VMEM] * 5 + [HBM] + [VMEM] * 3,
        scratch_shapes=[
            pltpu.VMEM((BLK, WIDTH), BF16),
            pltpu.VMEM((BLK, WIDTH), BF16),
            pltpu.VMEM((HEADS, BLK), F32),
            pltpu.VMEM((CORES, 2 * OWN_HEADS, BLK), F32),
            pltpu.VMEM((CORES, 2 * SLOTS, KEY_SHARDS), jnp.int32),
            pltpu.VMEM((CORES, 1, KEY_SHARDS), jnp.int32),
            pltpu.VMEM((NEAR, CORES, BLK, COLS), BF16),
            pltpu.VMEM((NEAR, CORES, BLK, COLS), BF16),
            pltpu.VMEM((NEAR, CORES, 2 * OWN_HEADS, BLK), F32),
            pltpu.VMEM((LINES, 4, BLK, COLS), BF16),
            pltpu.VMEM((LINES, 4, BLK, COLS), BF16),
            pltpu.VMEM((COLS, BLK), BF16),
            pltpu.VMEM((HEAD_PAIRS, BLK, 2 * BLK), BF16),
            pltpu.VMEM((HEAD_PAIRS, BLK, 2 * BLK), BF16),
            pltpu.VMEM(TABLE, jnp.int32),
            pltpu.SMEM(TABLE, jnp.int32),
            pltpu.SemaphoreType.DMA((GATHER_COPIES,)),
            pltpu.SemaphoreType.DMA((GATHER_COPIES,)),
            pltpu.SemaphoreType.DMA((9,)),
            pltpu.SemaphoreType.DMA((3 * NEAR + 2 * LINES,)),
        ],
        compiler_params=pltpu.CompilerParams(
            collective_id=0, has_side_effects=True, vmem_limit_bytes=GATHER_LIMIT
        ),
        name="gather_blocks",
    )(q, do, k, v, out, lse, lists, counts)


def pair_kernel(
    table, q_all, do_all, st_all, k_all, v_all, dk_early, dv_early, dq_early,
    dq_out, dk_out, dv_out,
    k_turned, p_buf, ds_buf, dq_sum, dk_sum, dv_sum,
):
    def clear(query, carry):
        dq_sum[query] = jnp.zeros((COLS, BLK), F32)
        return carry

    lax.fori_loop(0, QUERY_BLOCKS, clear, 0)
    halves = head_halves()

    def key_block(block, carry):
        up, across = lax.div(block, NX), lax.rem(block, NX)
        first_low, first_high = table[3, block], table[3, block + 1]
        second_low, second_high = FIRST + table[5, block], FIRST + table[5, block + 1]
        low, high = table[4, block], table[4, block + 1]
        have = (first_high - first_low) + (second_high - second_low) + (high - low)

        @pl.when(have == 0)
        def _():
            dk_out[up, across] = jnp.zeros((BLK, COLS), BF16)
            dv_out[across, up] = jnp.zeros((BLK, COLS), BF16)

        def keys(lanes):
            return k_all[up, across, :, lanes]

        def values(lanes):
            return v_all[across, up, :, lanes]

        def take(slot, carry):
            query = lax.rem(table[0, slot], QUERY_BLOCKS)
            dk_sum[...] += dk_early[slot]
            dv_sum[...] += dv_early[slot]
            dq_sum[query] += dq_early[slot]
            return carry

        def used(slot, carry):
            query = lax.rem(table[1 + lax.div(slot, 128), lax.rem(slot, 128)], QUERY_BLOCKS)

            def queries(lanes):
                return q_all[query, :, lanes]

            def douts(lanes):
                return do_all[query, :, lanes]

            def stats(row):
                return st_all[query, row : row + 1, :]

            pair_products(keys, values, queries, douts, stats, halves, p_buf, ds_buf)

            def add_dv(lanes, value):
                dv_sum[:, lanes] += value

            def add_dk(lanes, value):
                dk_sum[:, lanes] += value

            def add_dq(rows, value):
                dq_sum[query, rows, :] += value

            pair_gradients(queries, douts, halves, p_buf, ds_buf, k_turned, add_dv, add_dk, add_dq)
            return carry

        @pl.when(have > 0)
        def _():
            dk_sum[...] = jnp.zeros_like(dk_sum)
            dv_sum[...] = jnp.zeros_like(dv_sum)
            lax.fori_loop(first_low, first_high, take, 0)
            lax.fori_loop(second_low, second_high, take, 0)

            @pl.when(high > low)
            def _():
                turn_keys(keys, k_turned)

            lax.fori_loop(low, high, used, 0)
            dk_out[up, across] = (dk_sum[...] * SCALE).astype(BF16)
            dv_out[across, up] = dv_sum[...].astype(BF16)

        return carry

    lax.fori_loop(0, KEY_BLOCKS, key_block, 0)

    def turn_in(query, carry):
        dq_out[query] = (dq_sum[query] * SCALE).astype(BF16)
        return carry

    lax.fori_loop(0, QUERY_BLOCKS, turn_in, 0)


def pairs_over_blocks(q_all, do_all, st_all, k_all, v_all, table, dk_early, dv_early, dq_early):
    return pl.pallas_call(
        pair_kernel,
        out_shape=[
            jax.ShapeDtypeStruct((QUERY_BLOCKS, COLS, BLK), BF16),
            jax.ShapeDtypeStruct((NY, NX, BLK, COLS), BF16),
            jax.ShapeDtypeStruct((NX, NY, BLK, COLS), BF16),
        ],
        in_specs=[pl.BlockSpec(memory_space=pltpu.SMEM)] + [VMEM] * 8,
        out_specs=[VMEM] * 3,
        scratch_shapes=[
            pltpu.VMEM((COLS, BLK), BF16),
            pltpu.VMEM((HEAD_PAIRS, BLK, 2 * BLK), BF16),
            pltpu.VMEM((HEAD_PAIRS, BLK, 2 * BLK), BF16),
            pltpu.VMEM((QUERY_BLOCKS, COLS, BLK), F32),
            pltpu.VMEM((BLK, COLS), F32),
            pltpu.VMEM((BLK, COLS), F32),
        ],
        compiler_params=pltpu.CompilerParams(vmem_limit_bytes=PAIR_LIMIT),
        name="used_pairs",
    )(
        table,
        q_all.reshape(QUERY_BLOCKS, BLK, COLS),
        do_all.reshape(QUERY_BLOCKS, BLK, COLS),
        st_all.reshape(QUERY_BLOCKS, 2 * OWN_HEADS, BLK),
        k_all,
        v_all,
        dk_early,
        dv_early,
        dq_early,
    )


REDUCE_COPIES = 41
ROW_STEP = 16


def reduce_kernel(
    dq_part, dk_part, dv_part,
    gq_out, gk_out, gv_out,
    dq_own, dq_in_up, dq_in_down, dq_end,
    k_out, k_far, k_near, k_mid, k_mid_far, k_end,
    v_out, v_far, v_near, v_mid, v_mid_far, v_end,
    send_sems, recv_sems, q_end_sems, k_end_sems, v_end_sems,
):
    me = Place()
    x, y, z, core = me.x, me.y, me.z, me.core
    first, second = pl.ds(0, 2), pl.ds(2, 2)
    me.greet(both_cores=True)
    send = Sender(send_sems, recv_sems)
    up, down = me.over_z(1), me.over_z(-1)

    def add_rows(total, terms, count):
        def one(index, carry):
            at = pl.ds(pl.multiple_of(index * ROW_STEP, ROW_STEP), ROW_STEP)
            value = terms[0][at, :].astype(F32)
            for term in terms[1:]:
                value = value + term[at, :].astype(F32)
            total[at, :] = value.astype(total.dtype)
            return carry

        lax.fori_loop(0, count // ROW_STEP, one, 0, unroll=4)

    arrive = {
        ("up", 0, 1): send(dq_part.at[me.zs(4), 0], dq_in_up.at[0, 0], up),
        ("down", 1, 1): send(dq_part.at[me.zs(4), 1], dq_in_down.at[0, 1], down),
    }
    k_a = send(dk_part.at[me.ys(2), first], k_far.at[0], me.over_y(1))
    k_b = send(dk_part.at[me.ys(2), second], k_far.at[1], me.over_y(-1))
    v_a = send(dv_part.at[me.xs(2), first], v_far.at[0], me.over_x(1))
    v_b = send(dv_part.at[me.xs(2), second], v_far.at[1], me.over_x(-1))
    arrive["up", 1, 2] = send(dq_part.at[me.zs(3), 1], dq_in_up.at[1, 1], up)
    arrive["down", 0, 2] = send(dq_part.at[me.zs(-3), 0], dq_in_down.at[1, 0], down)
    k_in = [
        send(dk_part.at[me.ys(1), second], k_near.at[0, second], me.over_y(1)),
        send(dk_part.at[me.ys(-1), first], k_near.at[1, first], me.over_y(-1)),
    ]
    v_in = [
        send(dv_part.at[me.xs(1), second], v_near.at[0, second], me.over_x(1)),
        send(dv_part.at[me.xs(-1), first], v_near.at[1, first], me.over_x(-1)),
    ]
    q_sib = send(dq_part.at[z, 1 - core], dq_end.at[2, core], me.sibling, q_end_sems.at[2, core])

    def hop_q(direction, shard, hop):
        if direction == "up":
            side, step, inbox, way = 0, 4 - hop, dq_in_up, 1
        else:
            side, step, inbox, way = 1, hop - 4, dq_in_down, -1
        own = dq_own.at[me.zs(step), shard]
        arrive[direction, shard, hop].wait_recv()
        add_rows(own, [dq_part.at[me.zs(step), shard], inbox.at[hop - 1, shard]], COLS)
        if hop < 3:
            arrive[direction, shard, hop + 1] = send(own, inbox.at[hop, shard], me.over_z(way))
        else:
            send(own, dq_end.at[side, core], me.over_z(way, owner=shard), q_end_sems.at[side, core])

    add_rows(dq_end.at[2, core], [dq_part.at[z, core]], COLS)
    hop_q("up", 0, 1)
    hop_q("down", 1, 1)

    def onward(arrival, part, place, base, inbox, outbox):
        arrival.wait_recv()
        for row in range(2):
            add_rows(outbox.at[row], [part.at[place, base + row], inbox.at[row]], BLK)

    onward(k_a, dk_part, me.ys(1), 0, k_far.at[0], k_out.at[0])
    k_in.append(send(k_out.at[0], k_near.at[0, first], me.over_y(1)))
    onward(v_a, dv_part, me.xs(1), 0, v_far.at[0], v_out.at[0])
    v_in.append(send(v_out.at[0], v_near.at[0, first], me.over_x(1)))
    onward(k_b, dk_part, me.ys(-1), 2, k_far.at[1], k_out.at[1])
    k_in.append(send(k_out.at[1], k_near.at[1, second], me.over_y(-1)))
    onward(v_b, dv_part, me.xs(-1), 2, v_far.at[1], v_out.at[1])
    v_in.append(send(v_out.at[1], v_near.at[1, second], me.over_x(-1)))
    for hop, shard in ((2, 1), (2, 0), (3, 1), (3, 0)):
        hop_q("up", shard, hop)
        hop_q("down", 1 - shard, hop)

    half_rows = (pl.ds(0, HALF), pl.ds(HALF, HALF))

    def mix(own, here, near, middle, row):
        add_rows(middle.at[row], [own.at[here, row], near.at[0, row], near.at[1, row]], BLK)

    def turn_far(arrivals, own, here, near, middle, far, axis, over):
        for arrival in arrivals:
            arrival.wait_recv()
        farthest = axis(2)
        mix(own, here, near, middle, farthest)
        far_a = send(middle.at[farthest, half_rows[0]], far.at[0], over(1))
        far_b = send(middle.at[farthest, half_rows[1]], far.at[1], over(-1))
        return far_a, far_b

    def turn_near(own, here, near, middle, end, sems, axis, over, place):
        for side, step in enumerate((1, -1)):
            row, owner = axis(step), 1 - side
            mix(own, here, near, middle, row)
            part = middle.at[row, half_rows[owner]]
            send(part, end.at[side, core], over(step, owner=owner), sems.at[side, core])
        mix(own, here, near, middle, place)
        send(middle.at[place, half_of(1 - core, HALF)], end.at[2, core], me.sibling, sems.at[2, core])
        end[2, core] = middle[place, half_of(core, HALF), :]

    def last(arrival, middle, at, half, far, end, sems, side, device):
        arrival.wait_recv()
        part = middle.at[at, half_rows[half]]
        add_rows(part, [part, far], HALF)
        send(part, end.at[side, core], device, sems.at[side, core])

    kx_a, kx_b = turn_far(k_in, dk_part, y, k_near, k_mid, k_mid_far, me.xs, me.over_x)
    vy_a, vy_b = turn_far(v_in, dv_part, x, v_near, v_mid, v_mid_far, me.ys, me.over_y)
    turn_near(dk_part, y, k_near, k_mid, k_end, k_end_sems, me.xs, me.over_x, x)
    turn_near(dv_part, x, v_near, v_mid, v_end, v_end_sems, me.ys, me.over_y, y)
    last(kx_a, k_mid, me.xs(1), 0, k_mid_far.at[0], k_end, k_end_sems, 0, me.over_x(1, owner=0))
    last(kx_b, k_mid, me.xs(-1), 1, k_mid_far.at[1], k_end, k_end_sems, 1, me.over_x(-1, owner=1))
    last(vy_a, v_mid, me.ys(1), 0, v_mid_far.at[0], v_end, v_end_sems, 0, me.over_y(1, owner=0))
    last(vy_b, v_mid, me.ys(-1), 1, v_mid_far.at[1], v_end, v_end_sems, 1, me.over_y(-1, owner=1))

    def ended(end, sems):
        for side in range(2):
            for column in range(CORES):
                pltpu.make_async_copy(end.at[side, column], end.at[side, column], sems.at[side, column]).wait()
        other = end.at[2, 1 - core]
        pltpu.make_async_copy(other, other, sems.at[2, 1 - core]).wait()

    ended(dq_end, q_end_sems)
    for column in range(CORES):
        for tile in range(COLS // 128):
            at = pl.ds(tile * 128, 128)
            value = (
                dq_end[0, column, at, :].astype(F32)
                + dq_end[1, column, at, :].astype(F32)
                + dq_end[2, column, at, :].astype(F32)
            )
            gq_out[:, pl.ds(column * COLS + tile * 128, 128)] = jnp.transpose(value).astype(BF16)
    for out, end, sems in ((gk_out, k_end, k_end_sems), (gv_out, v_end, v_end_sems)):
        ended(end, sems)
        for column in range(CORES):
            target = out.at[:, pl.ds(column * COLS, COLS)]
            add_rows(target, [end.at[side, column] for side in range(3)], HALF)
    send.finish()
    assert len(send.copies) == REDUCE_COPIES, len(send.copies)


def reduce_parts(dq_part, dk_part, dv_part):
    two = pltpu.VMEM((2, 2, BLK, COLS), BF16)
    near = pltpu.VMEM((2, 4, BLK, COLS), BF16)
    four = pltpu.VMEM((4, BLK, COLS), BF16)
    half = pltpu.VMEM((2, HALF, COLS), BF16)
    end = pltpu.VMEM((3, CORES, HALF, COLS), BF16)
    inbox = pltpu.VMEM((3, CORES, COLS, BLK), BF16)
    sems = pltpu.SemaphoreType.DMA((3, CORES))
    return pl.pallas_call(
        reduce_kernel,
        out_shape=[
            jax.ShapeDtypeStruct((BLK, WIDTH), BF16),
            jax.ShapeDtypeStruct((HALF, WIDTH), BF16),
            jax.ShapeDtypeStruct((HALF, WIDTH), BF16),
        ],
        in_specs=[VMEM] * 3,
        out_specs=[VMEM] * 3,
        scratch_shapes=[
            pltpu.VMEM((NZ, CORES, COLS, BLK), BF16), inbox, inbox, inbox,
            two, two, near, four, half, end,
            two, two, near, four, half, end,
            pltpu.SemaphoreType.DMA((REDUCE_COPIES,)),
            pltpu.SemaphoreType.DMA((REDUCE_COPIES,)),
            sems, sems, sems,
        ],
        compiler_params=pltpu.CompilerParams(
            collective_id=1, has_side_effects=True, vmem_limit_bytes=VMEM_LIMIT
        ),
        name="reduce_parts",
    )(dq_part.reshape(NZ, CORES, COLS, BLK), dk_part, dv_part)


def body(q, k, v, out, do, lse, block_pairs, counts):
    lists = block_pairs.transpose(0, 2, 3, 1).reshape(2 * SLOTS, KEY_SHARDS)
    arguments = (q, do, k, v, out, lse, lists, counts)
    held = [pltpu.with_memory_space_constraint(array, pltpu.HBM) for array in arguments]
    parts = pairs_over_blocks(*gather(*held))
    return tuple(reduce_parts(*parts))


def solution(mesh):
    placed = (
        P(("pb", "ka"), None),
        P(("ka", "pb"), None),
        P(("ka", "pb"), None),
        P(("pb", "ka"), None),
        P(("pb", "ka"), None),
        P(None, ("pb", "ka")),
        P("pb", None, None, None),
        P("pb", None),
    )
    return jax.shard_map(
        body,
        mesh=mesh,
        in_specs=placed,
        out_specs=(P(("pb", "ka"), None), P(("ka", "pb"), None), P(("ka", "pb"), None)),
        check_vma=False,
    )
```

```python
import jax
import jax.numpy as jnp
from jax import lax
from jax.experimental import pallas as pl
from jax.experimental.pallas import tpu as pltpu
from jax.sharding import PartitionSpec as P

NX, NY, NZ, CORES = 4, 4, 8, 2
HEADS = 16
OWN_HEADS = HEADS // CORES
BLK = 128
HALF = BLK // 2
WIDTH = 1024
COLS = WIDTH // CORES
HEAD_PAIRS = COLS // 128
SLOTS = 24
KEY_SHARDS = NX * NZ
QUERY_BLOCKS = NZ * CORES
KEY_BLOCKS = NX * NY
CELLS = KEY_BLOCKS * QUERY_BLOCKS
REACH = 3
NEAR = 2 * REACH + 1
FIRST = 8
SECOND = 17
EARLY = FIRST + SECOND
LINES = 3
TABLE = (8, 128)
SCALE = 64**-0.5
LOG2E = 1.4426950408889634
VMEM_LIMIT = 24 << 20
GATHER_LIMIT = 16 << 20
PAIR_LIMIT = 16 << 20
MESH = pl.DeviceIdType.MESH
HBM = pl.BlockSpec(memory_space=pltpu.HBM)
VMEM = pl.BlockSpec(memory_space=pltpu.VMEM)
F32 = jnp.float32
BF16 = jnp.bfloat16


class Place:
    def __init__(self):
        pb = lax.axis_index("pb")
        ka = lax.axis_index("ka")
        self.y = lax.div(pb, CORES)
        self.core = lax.rem(pb, CORES)
        self.x = lax.div(ka, NZ)
        self.z = lax.rem(ka, NZ)
        self.sibling = (self.y * CORES + 1 - self.core, ka)

    def aim(self, crossed, owner):
        if owner is not None:
            return owner
        return 1 - self.core if crossed else self.core

    def over_x(self, step, crossed=0, owner=None):
        return (self.y * CORES + self.aim(crossed, owner), self.xs(step) * NZ + self.z)

    def over_y(self, step, crossed=0, owner=None):
        return (self.ys(step) * CORES + self.aim(crossed, owner), self.x * NZ + self.z)

    def over_z(self, step, crossed=0, owner=None):
        return (self.y * CORES + self.aim(crossed, owner), self.x * NZ + self.zs(step))

    def xs(self, step):
        return lax.rem(self.x + step + NX, NX)

    def ys(self, step):
        return lax.rem(self.y + step + NY, NY)

    def zs(self, step):
        return lax.rem(self.z + step + NZ, NZ)

    def greet(self, both_cores=False):
        barrier = pltpu.get_barrier_semaphore()
        neighbours = [self.sibling]
        for step in (1, -1):
            for crossed in (0, 1) if both_cores else (0,):
                for over in (self.over_x, self.over_y, self.over_z):
                    neighbours.append(over(step, crossed))
        for neighbour in neighbours:
            pl.semaphore_signal(barrier, inc=1, device_id=neighbour, device_id_type=MESH)
        pl.semaphore_wait(barrier, len(neighbours))


class Sender:
    def __init__(self, send_sems, recv_sems):
        self.send_sems = send_sems
        self.recv_sems = recv_sems
        self.copies = []

    def __call__(self, source, target, device, recv_sem=None):
        index = len(self.copies)
        copy = pltpu.make_async_remote_copy(
            src_ref=source,
            dst_ref=target,
            send_sem=self.send_sems.at[index],
            recv_sem=self.recv_sems.at[index] if recv_sem is None else recv_sem,
            device_id=device,
            device_id_type=MESH,
        )
        copy.start()
        self.copies.append(copy)
        return copy

    def finish(self):
        for copy in self.copies:
            copy.wait_send()


NT = (((1,), (1,)), ((), ()))
NN = (((1,), (0,)), ((), ()))


def pair_lanes(pair):
    return slice(pair * 128, pair * 128 + 128)


def head_halves():
    lane = lax.broadcasted_iota(jnp.int32, (1, 128), 1)
    return (
        jnp.where(lane < 64, 1.0, 0.0).astype(BF16),
        jnp.where(lane < 64, 0.0, 1.0).astype(BF16),
    )


def both_heads(block, halves):
    return jnp.concatenate([block * halves[0], block * halves[1]], axis=0)


def turn_keys(keys, k_turned):
    for pair in range(HEAD_PAIRS):
        turned = jnp.transpose(keys(pair_lanes(pair)).astype(F32)).astype(BF16)
        k_turned[pair_lanes(pair), :] = turned


def pair_products(keys, values, queries, douts, stats, halves, p_buf, ds_buf, keep=None):
    for pair in range(HEAD_PAIRS):
        lanes = pair_lanes(pair)
        scores = lax.dot_general(
            keys(lanes), both_heads(queries(lanes), halves), NT, preferred_element_type=F32
        )
        dprob = lax.dot_general(
            values(lanes), both_heads(douts(lanes), halves), NT, preferred_element_type=F32
        )
        for side in range(2):
            head = 2 * pair + side
            cut = slice(side * BLK, side * BLK + BLK)
            prob = jnp.exp2(scores[:, cut] * (SCALE * LOG2E) - stats(head))
            if keep is not None:
                prob = jnp.where(keep, prob, 0.0)
            p_buf[pair, :, cut] = prob.astype(BF16)
            ds_buf[pair, :, cut] = (prob * (dprob[:, cut] - stats(OWN_HEADS + head))).astype(BF16)


def pair_gradients(queries, douts, halves, p_buf, ds_buf, k_turned, add_dv, add_dk, add_dq):
    for pair in range(HEAD_PAIRS):
        lanes = pair_lanes(pair)
        add_dv(
            lanes,
            lax.dot_general(
                p_buf[pair], both_heads(douts(lanes), halves), NN, preferred_element_type=F32
            ),
        )
        add_dk(
            lanes,
            lax.dot_general(
                ds_buf[pair], both_heads(queries(lanes), halves), NN, preferred_element_type=F32
            ),
        )
        both = lax.dot_general(k_turned[lanes, :], ds_buf[pair], NN, preferred_element_type=F32)
        for side in range(2):
            rows = slice(side * 64, side * 64 + 64)
            low = pair * 128 + side * 64
            add_dq(slice(low, low + 64), both[rows, side * BLK : side * BLK + BLK])


def tabulate(lists, counts, x, y, z, table):
    cell = lax.broadcasted_iota(jnp.int32, (CELLS, KEY_SHARDS), 0)
    shard = lax.broadcasted_iota(jnp.int32, (SLOTS, KEY_SHARDS), 1)
    slot = lax.broadcasted_iota(jnp.int32, (SLOTS, KEY_SHARDS), 0)
    used = jnp.zeros((CELLS, KEY_SHARDS), F32)
    for owner in range(CORES):
        queries = lists[owner, 0:SLOTS, :]
        blocks = lists[owner, SLOTS : 2 * SLOTS, :]
        column = lax.shift_right_logical(shard, 3)
        ok = (slot < counts[owner]) & ((shard & 7) == z) & (lax.shift_right_logical(queries, 3) == x)
        code = (blocks * NX + column) * QUERY_BLOCKS + (queries & 7) * CORES + owner
        code = jnp.where(ok, code, -1)
        for row in range(SLOTS):
            used = jnp.where(cell == code[row : row + 1, :], 1.0, used)
    used = jnp.max(used, axis=1, keepdims=True)
    order = lax.broadcasted_iota(jnp.int32, (CELLS, 1), 0)
    away = (lax.shift_right_logical(order & 15, 1) - z + REACH + NZ) & 7
    near = jnp.where(away < NEAR, used, 0.0)
    nearer = jnp.where((away > 0) & (away < NEAR - 1), used, 0.0)
    before = lax.broadcasted_iota(jnp.int32, (CELLS, CELLS), 0)
    before = before > lax.broadcasted_iota(jnp.int32, (CELLS, CELLS), 1)
    before = jnp.where(before, 1.0, 0.0).astype(BF16)
    spread = jnp.zeros((CELLS, 128), F32)
    up_block = lax.shift_right_logical(order, 6)
    across_block = lax.shift_right_logical(order, 4) & 3
    close = (((up_block - y + 1 + NY) & 3) < LINES) & (((across_block - x + 1 + NX) & 3) < LINES)

    def ranks(cells):
        return lax.dot_general(before, cells.astype(BF16), NN, preferred_element_type=F32)

    closest = jnp.where(close, nearer, 0.0) + spread
    first_rank = ranks(closest)
    first = jnp.where(first_rank < FIRST, closest, 0.0)
    second = (near + spread) - first
    second_rank = ranks(second)
    second = jnp.where(second_rank < SECOND, second, 0.0)
    others = (used + spread) - first - second
    other_rank = ranks(others)
    lane = lax.broadcasted_iota(jnp.int32, (CELLS, 128), 1)
    line = lax.broadcasted_iota(jnp.int32, (CELLS, 128), 0)
    number = line.astype(F32)

    def total(values):
        return jnp.sum(values, axis=0, keepdims=True)

    place = lane.astype(F32)
    rows = [
        total(jnp.where(first_rank == place, first * number, 0.0))
        + total(jnp.where(second_rank + FIRST == place, second * number, 0.0)),
        total(jnp.where(other_rank == place, others * number, 0.0)),
        total(jnp.where(other_rank == place + 128.0, others * number, 0.0)),
        total(jnp.where(line < lane * QUERY_BLOCKS, first, 0.0)),
        total(jnp.where(line < lane * QUERY_BLOCKS, others, 0.0)),
        total(jnp.where(line < lane * QUERY_BLOCKS, second, 0.0)),
    ]
    table[...] = jnp.zeros(TABLE, jnp.int32)
    for index, row in enumerate(rows):
        table[index : index + 1, :] = row.astype(jnp.int32)


def half_of(core, size):
    return pl.ds(pl.multiple_of(core * size, size), size)


GATHER_COPIES = 58


def gather_kernel(
    q_ref, do_ref, k_ref, v_ref, out_ref, lse_ref, list_ref, count_ref,
    q_all, do_all, st_all, k_all, v_all, table_out, dk_early, dv_early, dq_early,
    do_buf, out_buf, lse_buf, st_buf, list_all, count_all, q_near, do_near, st_near, k_near, v_near,
    k_turned, p_buf, ds_buf, table, table_s, send_sems, recv_sems, local_sems, near_sems, far_sems,
):
    me = Place()
    x, y, z, core = me.x, me.y, me.z, me.core
    every = slice(None)
    rows = half_of(core, HALF)
    mine = half_of(core, COLS)
    theirs = half_of(1 - core, COLS)

    loads = [
        pltpu.make_async_copy(do_ref, do_buf, local_sems.at[5]),
        pltpu.make_async_copy(out_ref, out_buf, local_sems.at[6]),
        pltpu.make_async_copy(lse_ref, lse_buf, local_sems.at[7]),
    ]
    for load in loads:
        load.start()
    owns = [
        pltpu.make_async_copy(q_ref.at[every, mine], q_all.at[z, core], local_sems.at[0]),
        pltpu.make_async_copy(do_ref.at[every, mine], do_all.at[z, core], local_sems.at[1]),
        pltpu.make_async_copy(k_ref.at[every, mine], k_all.at[y, x, rows], local_sems.at[2]),
        pltpu.make_async_copy(v_ref.at[every, mine], v_all.at[x, y, rows], local_sems.at[3]),
        pltpu.make_async_copy(list_ref, list_all.at[core], local_sems.at[4]),
        pltpu.make_async_copy(count_ref, count_all.at[core], local_sems.at[8]),
    ]
    for own in owns:
        own.start()
    me.greet(both_cores=True)
    send = Sender(send_sems, recv_sems)
    up, down = me.over_z(1), me.over_z(-1)

    def to_both(ref, target, straight, crossed):
        return [
            send(ref.at[every, mine], target, straight),
            send(ref.at[every, theirs], target, crossed),
        ]

    cross_up, cross_down = me.over_z(1, 1), me.over_z(-1, 1)
    q_up = [to_both(q_ref, q_all.at[z, core], up, cross_up)]
    do_down = [to_both(do_ref, do_all.at[z, core], down, cross_down)]
    k_swap = send(k_ref.at[every, theirs], k_all.at[y, x, rows], me.sibling)
    v_swap = send(v_ref.at[every, theirs], v_all.at[x, y, rows], me.sibling)
    k_right = to_both(k_ref, k_all.at[y, x, rows], me.over_x(1), me.over_x(1, 1))
    k_left = to_both(k_ref, k_all.at[y, x, rows], me.over_x(-1), me.over_x(-1, 1))
    v_right = to_both(v_ref, v_all.at[x, y, rows], me.over_y(1), me.over_y(1, 1))
    v_left = to_both(v_ref, v_all.at[x, y, rows], me.over_y(-1), me.over_y(-1, 1))
    do_up = [to_both(do_ref, do_all.at[z, core], up, cross_up)]
    q_down = [to_both(q_ref, q_all.at[z, core], down, cross_down)]
    swaps = [
        send(q_ref.at[every, theirs], q_all.at[z, core], me.sibling),
        send(do_ref.at[every, theirs], do_all.at[z, core], me.sibling),
        send(list_ref, list_all.at[core], me.sibling),
        send(count_ref, count_all.at[core], me.sibling),
    ]

    for load in loads:
        load.wait()
    products = do_buf[...].astype(F32) * out_buf[...].astype(F32)
    high = products.astype(BF16)
    low = (products - high.astype(F32)).astype(BF16)
    head = lax.broadcasted_iota(jnp.int32, (HEADS, WIDTH), 0) * 64
    feature = lax.broadcasted_iota(jnp.int32, (HEADS, WIDTH), 1)
    member = jnp.where((feature >= head) & (feature < head + 64), 1.0, 0.0).astype(BF16)
    over_features = (((1,), (1,)), ((), ()))
    delta = lax.dot_general(member, high, over_features, preferred_element_type=F32)
    delta = delta + lax.dot_general(member, low, over_features, preferred_element_type=F32)
    for side in range(CORES):
        heads = slice(side * OWN_HEADS, side * OWN_HEADS + OWN_HEADS)
        st_buf[side, 0:OWN_HEADS, :] = lse_buf[heads, :] * LOG2E
        st_buf[side, OWN_HEADS : 2 * OWN_HEADS, :] = delta[heads, :]
    for own in owns:
        own.wait()
    nears = []

    def bring_near(arrays, distance):
        for blocks, held in arrays:
            copy = pltpu.make_async_copy(
                blocks.at[me.zs(distance)], held.at[distance + REACH], near_sems.at[len(nears)]
            )
            copy.start()
            nears.append(copy)

    st_own = pltpu.make_async_copy(st_buf.at[core], st_all.at[z, core], local_sems.at[0])
    st_own.start()
    swaps.append(send(st_buf.at[1 - core], st_all.at[z, core], me.sibling))
    st_up, st_down = [], []
    for stats, straight, crossed in ((st_up, up, cross_up), (st_down, down, cross_down)):
        stats.append(
            [
                send(st_buf.at[core], st_all.at[z, core], straight),
                send(st_buf.at[1 - core], st_all.at[z, core], crossed),
            ]
        )

    def arrived(*groups):
        for group in groups:
            for copy in group:
                copy.wait_recv()

    upper, lower = pl.ds(0, HALF), pl.ds(HALF, HALF)
    arrived(k_right)
    k_part = k_all.at[y, me.xs(-1), upper]
    k_far = [send(k_part, k_part, me.over_x(1))]
    arrived(v_right)
    v_part = v_all.at[x, me.ys(-1), upper]
    v_far = [send(v_part, v_part, me.over_y(1))]
    arrived(k_left)
    k_part = k_all.at[y, me.xs(1), lower]
    k_far.append(send(k_part, k_part, me.over_x(-1)))
    arrived(v_left)
    v_part = v_all.at[x, me.ys(1), lower]
    v_far.append(send(v_part, v_part, me.over_y(-1)))

    first, second = pl.ds(0, 2), pl.ds(2, 2)

    def lines(blocks, place, over):
        ahead, back = [], []
        for part_ahead, part_back in ((first, second), (second, first)):
            part = blocks.at[place, part_ahead]
            ahead.append(send(part, part, over(1)))
            part = blocks.at[place, part_back]
            back.append(send(part, part, over(-1)))
        return ahead, back

    arrived([k_swap], k_far)
    k_right, k_left = lines(k_all, y, me.over_y)
    arrived([v_swap], v_far)
    v_right, v_left = lines(v_all, x, me.over_x)

    def forward(hop, sign, blocks, copies):
        arrived(copies[hop - 1])
        block = blocks.at[me.zs(-sign * hop)]
        copies.append([send(block, block, up if sign > 0 else down)])

    forward(1, 1, q_all, q_up)
    forward(1, -1, do_all, do_down)
    arrived(swaps)
    st_own.wait()
    tabulate(list_all, count_all, x, y, z, table)
    to_scalars = pltpu.make_async_copy(table, table_s, local_sems.at[1])
    to_scalars.start()
    table_store = pltpu.make_async_copy(table, table_out, local_sems.at[2])
    table_store.start()
    every_array = ((q_all, q_near), (do_all, do_near), (st_all, st_near))
    bring_near(every_array, 0)

    def across(copies, blocks, start, part, device):
        arrived(copies[:1])
        part = blocks.at[start, part]
        return send(part, part, device)

    k_far = [across(k_right, k_all, me.ys(-1), first, me.over_y(1))]
    v_far = [across(v_right, v_all, me.xs(-1), first, me.over_x(1))]
    k_far.append(across(k_left, k_all, me.ys(1), second, me.over_y(-1)))
    v_far.append(across(v_left, v_all, me.xs(1), second, me.over_x(-1)))
    forward(1, 1, do_all, do_up)
    forward(1, -1, q_all, q_down)
    forward(1, 1, st_all, st_up)
    forward(1, -1, st_all, st_down)
    bring_near(every_array, 1)
    bring_near(every_array, -1)

    forward(2, 1, q_all, q_up)
    forward(2, -1, do_all, do_down)
    forward(2, 1, do_all, do_up)
    forward(2, -1, q_all, q_down)
    forward(2, 1, st_all, st_up)
    forward(2, -1, st_all, st_down)

    bring_near(every_array, 2)
    bring_near(every_array, -2)
    arrived(k_right[1:], k_left[1:], v_right[1:], v_left[1:])
    for step in (-1, 0, 1):
        for blocks, line, held in ((k_all, me.ys(step), k_near), (v_all, me.xs(step), v_near)):
            copy = pltpu.make_async_copy(blocks.at[line], held.at[step + 1], near_sems.at[len(nears)])
            copy.start()
            nears.append(copy)
    for copy in nears:
        copy.wait()
    to_scalars.wait()
    halves = head_halves()
    firsts, seconds = table_s[3, KEY_BLOCKS], table_s[5, KEY_BLOCKS]

    def early(index, carry, close=False):
        entry = jnp.clip(table_s[0, index], 0, CELLS - 1)
        block = lax.div(entry, QUERY_BLOCKS)
        up_block, across_block = lax.div(block, NX), lax.rem(block, NX)
        query = lax.rem(lax.div(lax.rem(entry, QUERY_BLOCKS), CORES) - z + REACH + NZ, NZ)
        query = jnp.minimum(query, NEAR - 1)
        owner = lax.rem(entry, CORES)
        keep = index < firsts if close else index - FIRST < seconds
        up_line = jnp.minimum(lax.rem(up_block - y + 1 + NY, NY), LINES - 1)
        across_line = jnp.minimum(lax.rem(across_block - x + 1 + NX, NX), LINES - 1)

        def keys(lanes):
            if close:
                return k_near[up_line, across_block, :, lanes]
            return k_all[up_block, across_block, :, lanes]

        def values(lanes):
            if close:
                return v_near[across_line, up_block, :, lanes]
            return v_all[across_block, up_block, :, lanes]

        def queries(lanes):
            return q_near[query, owner, :, lanes]

        def douts(lanes):
            return do_near[query, owner, :, lanes]

        def stats(row):
            return st_near[query, owner, row : row + 1, :]

        turn_keys(keys, k_turned)
        pair_products(keys, values, queries, douts, stats, halves, p_buf, ds_buf, keep=keep)

        def put_dv(lanes, value):
            dv_early[index, :, lanes] = value

        def put_dk(lanes, value):
            dk_early[index, :, lanes] = value

        def put_dq(rows, value):
            dq_early[index, rows, :] = value

        pair_gradients(queries, douts, halves, p_buf, ds_buf, k_turned, put_dv, put_dk, put_dq)
        return carry

    lax.fori_loop(0, FIRST, lambda index, carry: early(index, carry, close=True), 0)
    arrived(k_far, v_far)
    forward(3, 1, q_all, q_up)
    forward(3, -1, do_all, do_down)
    forward(3, 1, st_all, st_up)
    arrived(do_up[2], q_down[2], st_down[2])
    nears.clear()
    for distance in (REACH, -REACH):
        for blocks, held in every_array:
            copy = pltpu.make_async_copy(
                blocks.at[me.zs(distance)], held.at[distance + REACH], far_sems.at[len(nears)]
            )
            copy.start()
            nears.append(copy)
    for copy in nears:
        copy.wait()
    lax.fori_loop(FIRST, EARLY, early, 0)
    arrived(q_up[3], do_down[3], st_up[3])
    table_store.wait()
    send.finish()
    assert len(send.copies) == GATHER_COPIES, len(send.copies)


def gather(q, do, k, v, out, lse, lists, counts):
    return pl.pallas_call(
        gather_kernel,
        out_shape=[
            jax.ShapeDtypeStruct((NZ, CORES, BLK, COLS), BF16),
            jax.ShapeDtypeStruct((NZ, CORES, BLK, COLS), BF16),
            jax.ShapeDtypeStruct((NZ, CORES, 2 * OWN_HEADS, BLK), F32),
            jax.ShapeDtypeStruct((NY, NX, BLK, COLS), BF16),
            jax.ShapeDtypeStruct((NX, NY, BLK, COLS), BF16),
            jax.ShapeDtypeStruct(TABLE, jnp.int32),
            jax.ShapeDtypeStruct((EARLY, BLK, COLS), F32),
            jax.ShapeDtypeStruct((EARLY, BLK, COLS), F32),
            jax.ShapeDtypeStruct((EARLY, COLS, BLK), F32),
        ],
        in_specs=[HBM] * 8,
        out_specs=[VMEM] * 5 + [HBM] + [VMEM] * 3,
        scratch_shapes=[
            pltpu.VMEM((BLK, WIDTH), BF16),
            pltpu.VMEM((BLK, WIDTH), BF16),
            pltpu.VMEM((HEADS, BLK), F32),
            pltpu.VMEM((CORES, 2 * OWN_HEADS, BLK), F32),
            pltpu.VMEM((CORES, 2 * SLOTS, KEY_SHARDS), jnp.int32),
            pltpu.VMEM((CORES, 1, KEY_SHARDS), jnp.int32),
            pltpu.VMEM((NEAR, CORES, BLK, COLS), BF16),
            pltpu.VMEM((NEAR, CORES, BLK, COLS), BF16),
            pltpu.VMEM((NEAR, CORES, 2 * OWN_HEADS, BLK), F32),
            pltpu.VMEM((LINES, 4, BLK, COLS), BF16),
            pltpu.VMEM((LINES, 4, BLK, COLS), BF16),
            pltpu.VMEM((COLS, BLK), BF16),
            pltpu.VMEM((HEAD_PAIRS, BLK, 2 * BLK), BF16),
            pltpu.VMEM((HEAD_PAIRS, BLK, 2 * BLK), BF16),
            pltpu.VMEM(TABLE, jnp.int32),
            pltpu.SMEM(TABLE, jnp.int32),
            pltpu.SemaphoreType.DMA((GATHER_COPIES,)),
            pltpu.SemaphoreType.DMA((GATHER_COPIES,)),
            pltpu.SemaphoreType.DMA((9,)),
            pltpu.SemaphoreType.DMA((3 * (NEAR - 2) + 2 * LINES,)),
            pltpu.SemaphoreType.DMA((6,)),
        ],
        compiler_params=pltpu.CompilerParams(
            collective_id=0, has_side_effects=True, vmem_limit_bytes=GATHER_LIMIT
        ),
        name="gather_blocks",
    )(q, do, k, v, out, lse, lists, counts)


def pair_kernel(
    table, q_all, do_all, st_all, k_all, v_all, dk_early, dv_early, dq_early,
    dq_out, dk_out, dv_out,
    k_turned, p_buf, ds_buf, dq_sum, dk_sum, dv_sum,
):
    def clear(query, carry):
        dq_sum[query] = jnp.zeros((COLS, BLK), F32)
        return carry

    lax.fori_loop(0, QUERY_BLOCKS, clear, 0)
    halves = head_halves()

    def key_block(block, carry):
        up, across = lax.div(block, NX), lax.rem(block, NX)
        first_low, first_high = table[3, block], table[3, block + 1]
        second_low, second_high = FIRST + table[5, block], FIRST + table[5, block + 1]
        low, high = table[4, block], table[4, block + 1]
        have = (first_high - first_low) + (second_high - second_low) + (high - low)

        @pl.when(have == 0)
        def _():
            dk_out[up, across] = jnp.zeros((BLK, COLS), BF16)
            dv_out[across, up] = jnp.zeros((BLK, COLS), BF16)

        def keys(lanes):
            return k_all[up, across, :, lanes]

        def values(lanes):
            return v_all[across, up, :, lanes]

        def take(slot, carry):
            query = lax.rem(table[0, slot], QUERY_BLOCKS)
            dk_sum[...] += dk_early[slot]
            dv_sum[...] += dv_early[slot]
            dq_sum[query] += dq_early[slot]
            return carry

        def used(slot, carry):
            query = lax.rem(table[1 + lax.div(slot, 128), lax.rem(slot, 128)], QUERY_BLOCKS)

            def queries(lanes):
                return q_all[query, :, lanes]

            def douts(lanes):
                return do_all[query, :, lanes]

            def stats(row):
                return st_all[query, row : row + 1, :]

            pair_products(keys, values, queries, douts, stats, halves, p_buf, ds_buf)

            def add_dv(lanes, value):
                dv_sum[:, lanes] += value

            def add_dk(lanes, value):
                dk_sum[:, lanes] += value

            def add_dq(rows, value):
                dq_sum[query, rows, :] += value

            pair_gradients(queries, douts, halves, p_buf, ds_buf, k_turned, add_dv, add_dk, add_dq)
            return carry

        @pl.when(have > 0)
        def _():
            dk_sum[...] = jnp.zeros_like(dk_sum)
            dv_sum[...] = jnp.zeros_like(dv_sum)
            lax.fori_loop(first_low, first_high, take, 0)
            lax.fori_loop(second_low, second_high, take, 0)

            @pl.when(high > low)
            def _():
                turn_keys(keys, k_turned)

            lax.fori_loop(low, high, used, 0)
            dk_out[up, across] = (dk_sum[...] * SCALE).astype(BF16)
            dv_out[across, up] = dv_sum[...].astype(BF16)

        return carry

    lax.fori_loop(0, KEY_BLOCKS, key_block, 0)

    def turn_in(query, carry):
        dq_out[query] = (dq_sum[query] * SCALE).astype(BF16)
        return carry

    lax.fori_loop(0, QUERY_BLOCKS, turn_in, 0)


def pairs_over_blocks(q_all, do_all, st_all, k_all, v_all, table, dk_early, dv_early, dq_early):
    return pl.pallas_call(
        pair_kernel,
        out_shape=[
            jax.ShapeDtypeStruct((QUERY_BLOCKS, COLS, BLK), BF16),
            jax.ShapeDtypeStruct((NY, NX, BLK, COLS), BF16),
            jax.ShapeDtypeStruct((NX, NY, BLK, COLS), BF16),
        ],
        in_specs=[pl.BlockSpec(memory_space=pltpu.SMEM)] + [VMEM] * 8,
        out_specs=[VMEM] * 3,
        scratch_shapes=[
            pltpu.VMEM((COLS, BLK), BF16),
            pltpu.VMEM((HEAD_PAIRS, BLK, 2 * BLK), BF16),
            pltpu.VMEM((HEAD_PAIRS, BLK, 2 * BLK), BF16),
            pltpu.VMEM((QUERY_BLOCKS, COLS, BLK), F32),
            pltpu.VMEM((BLK, COLS), F32),
            pltpu.VMEM((BLK, COLS), F32),
        ],
        compiler_params=pltpu.CompilerParams(vmem_limit_bytes=PAIR_LIMIT),
        name="used_pairs",
    )(
        table,
        q_all.reshape(QUERY_BLOCKS, BLK, COLS),
        do_all.reshape(QUERY_BLOCKS, BLK, COLS),
        st_all.reshape(QUERY_BLOCKS, 2 * OWN_HEADS, BLK),
        k_all,
        v_all,
        dk_early,
        dv_early,
        dq_early,
    )


REDUCE_COPIES = 41
ROW_STEP = 16


def reduce_kernel(
    dq_part, dk_part, dv_part,
    gq_out, gk_out, gv_out,
    dq_own, dq_in_up, dq_in_down, dq_end,
    k_out, k_far, k_near, k_mid, k_mid_far, k_end,
    v_out, v_far, v_near, v_mid, v_mid_far, v_end,
    send_sems, recv_sems, q_end_sems, k_end_sems, v_end_sems,
):
    me = Place()
    x, y, z, core = me.x, me.y, me.z, me.core
    first, second = pl.ds(0, 2), pl.ds(2, 2)
    me.greet(both_cores=True)
    send = Sender(send_sems, recv_sems)
    up, down = me.over_z(1), me.over_z(-1)

    def add_rows(total, terms, count):
        def one(index, carry):
            at = pl.ds(pl.multiple_of(index * ROW_STEP, ROW_STEP), ROW_STEP)
            value = terms[0][at, :].astype(F32)
            for term in terms[1:]:
                value = value + term[at, :].astype(F32)
            total[at, :] = value.astype(total.dtype)
            return carry

        lax.fori_loop(0, count // ROW_STEP, one, 0, unroll=4)

    arrive = {
        ("up", 0, 1): send(dq_part.at[me.zs(4), 0], dq_in_up.at[0, 0], up),
        ("down", 1, 1): send(dq_part.at[me.zs(4), 1], dq_in_down.at[0, 1], down),
    }
    k_a = send(dk_part.at[me.ys(2), first], k_far.at[0], me.over_y(1))
    k_b = send(dk_part.at[me.ys(2), second], k_far.at[1], me.over_y(-1))
    v_a = send(dv_part.at[me.xs(2), first], v_far.at[0], me.over_x(1))
    v_b = send(dv_part.at[me.xs(2), second], v_far.at[1], me.over_x(-1))
    arrive["up", 1, 2] = send(dq_part.at[me.zs(3), 1], dq_in_up.at[1, 1], up)
    arrive["down", 0, 2] = send(dq_part.at[me.zs(-3), 0], dq_in_down.at[1, 0], down)
    k_in = [
        send(dk_part.at[me.ys(1), second], k_near.at[0, second], me.over_y(1)),
        send(dk_part.at[me.ys(-1), first], k_near.at[1, first], me.over_y(-1)),
    ]
    v_in = [
        send(dv_part.at[me.xs(1), second], v_near.at[0, second], me.over_x(1)),
        send(dv_part.at[me.xs(-1), first], v_near.at[1, first], me.over_x(-1)),
    ]
    q_sib = send(dq_part.at[z, 1 - core], dq_end.at[2, core], me.sibling, q_end_sems.at[2, core])

    def hop_q(direction, shard, hop):
        if direction == "up":
            side, step, inbox, way = 0, 4 - hop, dq_in_up, 1
        else:
            side, step, inbox, way = 1, hop - 4, dq_in_down, -1
        own = dq_own.at[me.zs(step), shard]
        arrive[direction, shard, hop].wait_recv()
        add_rows(own, [dq_part.at[me.zs(step), shard], inbox.at[hop - 1, shard]], COLS)
        if hop < 3:
            arrive[direction, shard, hop + 1] = send(own, inbox.at[hop, shard], me.over_z(way))
        else:
            send(own, dq_end.at[side, core], me.over_z(way, owner=shard), q_end_sems.at[side, core])

    add_rows(dq_end.at[2, core], [dq_part.at[z, core]], COLS)
    hop_q("up", 0, 1)
    hop_q("down", 1, 1)

    def onward(arrival, part, place, base, inbox, outbox):
        arrival.wait_recv()
        for row in range(2):
            add_rows(outbox.at[row], [part.at[place, base + row], inbox.at[row]], BLK)

    onward(k_a, dk_part, me.ys(1), 0, k_far.at[0], k_out.at[0])
    k_in.append(send(k_out.at[0], k_near.at[0, first], me.over_y(1)))
    onward(v_a, dv_part, me.xs(1), 0, v_far.at[0], v_out.at[0])
    v_in.append(send(v_out.at[0], v_near.at[0, first], me.over_x(1)))
    onward(k_b, dk_part, me.ys(-1), 2, k_far.at[1], k_out.at[1])
    k_in.append(send(k_out.at[1], k_near.at[1, second], me.over_y(-1)))
    onward(v_b, dv_part, me.xs(-1), 2, v_far.at[1], v_out.at[1])
    v_in.append(send(v_out.at[1], v_near.at[1, second], me.over_x(-1)))
    for hop, shard in ((2, 1), (2, 0), (3, 1), (3, 0)):
        hop_q("up", shard, hop)
        hop_q("down", 1 - shard, hop)

    half_rows = (pl.ds(0, HALF), pl.ds(HALF, HALF))

    def mix(own, here, near, middle, row):
        add_rows(middle.at[row], [own.at[here, row], near.at[0, row], near.at[1, row]], BLK)

    def turn_far(arrivals, own, here, near, middle, far, axis, over):
        for arrival in arrivals:
            arrival.wait_recv()
        farthest = axis(2)
        mix(own, here, near, middle, farthest)
        far_a = send(middle.at[farthest, half_rows[0]], far.at[0], over(1))
        far_b = send(middle.at[farthest, half_rows[1]], far.at[1], over(-1))
        return far_a, far_b

    def turn_near(own, here, near, middle, end, sems, axis, over, place):
        for side, step in enumerate((1, -1)):
            row, owner = axis(step), 1 - side
            mix(own, here, near, middle, row)
            part = middle.at[row, half_rows[owner]]
            send(part, end.at[side, core], over(step, owner=owner), sems.at[side, core])
        mix(own, here, near, middle, place)
        send(middle.at[place, half_of(1 - core, HALF)], end.at[2, core], me.sibling, sems.at[2, core])
        end[2, core] = middle[place, half_of(core, HALF), :]

    def last(arrival, middle, at, half, far, end, sems, side, device):
        arrival.wait_recv()
        part = middle.at[at, half_rows[half]]
        add_rows(part, [part, far], HALF)
        send(part, end.at[side, core], device, sems.at[side, core])

    kx_a, kx_b = turn_far(k_in, dk_part, y, k_near, k_mid, k_mid_far, me.xs, me.over_x)
    vy_a, vy_b = turn_far(v_in, dv_part, x, v_near, v_mid, v_mid_far, me.ys, me.over_y)
    turn_near(dk_part, y, k_near, k_mid, k_end, k_end_sems, me.xs, me.over_x, x)
    turn_near(dv_part, x, v_near, v_mid, v_end, v_end_sems, me.ys, me.over_y, y)
    last(kx_a, k_mid, me.xs(1), 0, k_mid_far.at[0], k_end, k_end_sems, 0, me.over_x(1, owner=0))
    last(kx_b, k_mid, me.xs(-1), 1, k_mid_far.at[1], k_end, k_end_sems, 1, me.over_x(-1, owner=1))
    last(vy_a, v_mid, me.ys(1), 0, v_mid_far.at[0], v_end, v_end_sems, 0, me.over_y(1, owner=0))
    last(vy_b, v_mid, me.ys(-1), 1, v_mid_far.at[1], v_end, v_end_sems, 1, me.over_y(-1, owner=1))

    def ended(end, sems):
        for side in range(2):
            for column in range(CORES):
                pltpu.make_async_copy(end.at[side, column], end.at[side, column], sems.at[side, column]).wait()
        other = end.at[2, 1 - core]
        pltpu.make_async_copy(other, other, sems.at[2, 1 - core]).wait()

    ended(dq_end, q_end_sems)
    for column in range(CORES):
        for tile in range(COLS // 128):
            at = pl.ds(tile * 128, 128)
            value = (
                dq_end[0, column, at, :].astype(F32)
                + dq_end[1, column, at, :].astype(F32)
                + dq_end[2, column, at, :].astype(F32)
            )
            gq_out[:, pl.ds(column * COLS + tile * 128, 128)] = jnp.transpose(value).astype(BF16)
    for out, end, sems in ((gk_out, k_end, k_end_sems), (gv_out, v_end, v_end_sems)):
        ended(end, sems)
        for column in range(CORES):
            target = out.at[:, pl.ds(column * COLS, COLS)]
            add_rows(target, [end.at[side, column] for side in range(3)], HALF)
    send.finish()
    assert len(send.copies) == REDUCE_COPIES, len(send.copies)


def reduce_parts(dq_part, dk_part, dv_part):
    two = pltpu.VMEM((2, 2, BLK, COLS), BF16)
    near = pltpu.VMEM((2, 4, BLK, COLS), BF16)
    four = pltpu.VMEM((4, BLK, COLS), BF16)
    half = pltpu.VMEM((2, HALF, COLS), BF16)
    end = pltpu.VMEM((3, CORES, HALF, COLS), BF16)
    inbox = pltpu.VMEM((3, CORES, COLS, BLK), BF16)
    sems = pltpu.SemaphoreType.DMA((3, CORES))
    return pl.pallas_call(
        reduce_kernel,
        out_shape=[
            jax.ShapeDtypeStruct((BLK, WIDTH), BF16),
            jax.ShapeDtypeStruct((HALF, WIDTH), BF16),
            jax.ShapeDtypeStruct((HALF, WIDTH), BF16),
        ],
        in_specs=[VMEM] * 3,
        out_specs=[VMEM] * 3,
        scratch_shapes=[
            pltpu.VMEM((NZ, CORES, COLS, BLK), BF16), inbox, inbox, inbox,
            two, two, near, four, half, end,
            two, two, near, four, half, end,
            pltpu.SemaphoreType.DMA((REDUCE_COPIES,)),
            pltpu.SemaphoreType.DMA((REDUCE_COPIES,)),
            sems, sems, sems,
        ],
        compiler_params=pltpu.CompilerParams(
            collective_id=1, has_side_effects=True, vmem_limit_bytes=VMEM_LIMIT
        ),
        name="reduce_parts",
    )(dq_part.reshape(NZ, CORES, COLS, BLK), dk_part, dv_part)


def body(q, k, v, out, do, lse, block_pairs, counts):
    lists = block_pairs.transpose(0, 2, 3, 1).reshape(2 * SLOTS, KEY_SHARDS)
    arguments = (q, do, k, v, out, lse, lists, counts)
    held = [pltpu.with_memory_space_constraint(array, pltpu.HBM) for array in arguments]
    parts = pairs_over_blocks(*gather(*held))
    return tuple(reduce_parts(*parts))


def solution(mesh):
    placed = (
        P(("pb", "ka"), None),
        P(("ka", "pb"), None),
        P(("ka", "pb"), None),
        P(("pb", "ka"), None),
        P(("pb", "ka"), None),
        P(None, ("pb", "ka")),
        P("pb", None, None, None),
        P("pb", None),
    )
    return jax.shard_map(
        body,
        mesh=mesh,
        in_specs=placed,
        out_specs=(P(("pb", "ka"), None), P(("ka", "pb"), None), P(("ka", "pb"), None)),
        check_vma=False,
    )
```

```python
import jax
import jax.numpy as jnp
from jax import lax
from jax.experimental import pallas as pl
from jax.experimental.pallas import tpu as pltpu
from jax.sharding import PartitionSpec as P

NX, NY, NZ, CORES = 4, 4, 8, 2
HEADS = 16
OWN_HEADS = HEADS // CORES
BLK = 128
HALF = BLK // 2
WIDTH = 1024
COLS = WIDTH // CORES
HEAD_PAIRS = COLS // 128
SLOTS = 24
KEY_SHARDS = NX * NZ
QUERY_BLOCKS = NZ * CORES
KEY_BLOCKS = NX * NY
CELLS = KEY_BLOCKS * QUERY_BLOCKS
REACH = 3
NEAR = 2 * REACH + 1
FIRST = 8
MIDDLE = 6
SECOND = 10
EARLY = FIRST + MIDDLE + SECOND
LINES = 3
TABLE = (8, 128)
SCALE = 64**-0.5
LOG2E = 1.4426950408889634
VMEM_LIMIT = 24 << 20
GATHER_LIMIT = 16 << 20
PAIR_LIMIT = 16 << 20
MESH = pl.DeviceIdType.MESH
HBM = pl.BlockSpec(memory_space=pltpu.HBM)
VMEM = pl.BlockSpec(memory_space=pltpu.VMEM)
F32 = jnp.float32
BF16 = jnp.bfloat16


class Place:
    def __init__(self):
        pb = lax.axis_index("pb")
        ka = lax.axis_index("ka")
        self.y = lax.div(pb, CORES)
        self.core = lax.rem(pb, CORES)
        self.x = lax.div(ka, NZ)
        self.z = lax.rem(ka, NZ)
        self.sibling = (self.y * CORES + 1 - self.core, ka)

    def aim(self, crossed, owner):
        if owner is not None:
            return owner
        return 1 - self.core if crossed else self.core

    def over_x(self, step, crossed=0, owner=None):
        return (self.y * CORES + self.aim(crossed, owner), self.xs(step) * NZ + self.z)

    def over_y(self, step, crossed=0, owner=None):
        return (self.ys(step) * CORES + self.aim(crossed, owner), self.x * NZ + self.z)

    def over_z(self, step, crossed=0, owner=None):
        return (self.y * CORES + self.aim(crossed, owner), self.x * NZ + self.zs(step))

    def xs(self, step):
        return lax.rem(self.x + step + NX, NX)

    def ys(self, step):
        return lax.rem(self.y + step + NY, NY)

    def zs(self, step):
        return lax.rem(self.z + step + NZ, NZ)

    def greet(self, both_cores=False):
        barrier = pltpu.get_barrier_semaphore()
        neighbours = [self.sibling]
        for step in (1, -1):
            for crossed in (0, 1) if both_cores else (0,):
                for over in (self.over_x, self.over_y, self.over_z):
                    neighbours.append(over(step, crossed))
        for neighbour in neighbours:
            pl.semaphore_signal(barrier, inc=1, device_id=neighbour, device_id_type=MESH)
        pl.semaphore_wait(barrier, len(neighbours))


class Sender:
    def __init__(self, send_sems, recv_sems):
        self.send_sems = send_sems
        self.recv_sems = recv_sems
        self.copies = []

    def __call__(self, source, target, device, recv_sem=None):
        index = len(self.copies)
        copy = pltpu.make_async_remote_copy(
            src_ref=source,
            dst_ref=target,
            send_sem=self.send_sems.at[index],
            recv_sem=self.recv_sems.at[index] if recv_sem is None else recv_sem,
            device_id=device,
            device_id_type=MESH,
        )
        copy.start()
        self.copies.append(copy)
        return copy

    def finish(self):
        for copy in self.copies:
            copy.wait_send()


NT = (((1,), (1,)), ((), ()))
NN = (((1,), (0,)), ((), ()))


def pair_lanes(pair):
    return slice(pair * 128, pair * 128 + 128)


def head_halves():
    lane = lax.broadcasted_iota(jnp.int32, (1, 128), 1)
    return (
        jnp.where(lane < 64, 1.0, 0.0).astype(BF16),
        jnp.where(lane < 64, 0.0, 1.0).astype(BF16),
    )


def both_heads(block, halves):
    return jnp.concatenate([block * halves[0], block * halves[1]], axis=0)


def turn_keys(keys, k_turned):
    for pair in range(HEAD_PAIRS):
        turned = jnp.transpose(keys(pair_lanes(pair)).astype(F32)).astype(BF16)
        k_turned[pair_lanes(pair), :] = turned


def pair_products(keys, values, queries, douts, stats, halves, p_buf, ds_buf, keep=None):
    for pair in range(HEAD_PAIRS):
        lanes = pair_lanes(pair)
        scores = lax.dot_general(
            keys(lanes), both_heads(queries(lanes), halves), NT, preferred_element_type=F32
        )
        dprob = lax.dot_general(
            values(lanes), both_heads(douts(lanes), halves), NT, preferred_element_type=F32
        )
        for side in range(2):
            head = 2 * pair + side
            cut = slice(side * BLK, side * BLK + BLK)
            prob = jnp.exp2(scores[:, cut] * (SCALE * LOG2E) - stats(head))
            if keep is not None:
                prob = jnp.where(keep, prob, 0.0)
            p_buf[pair, :, cut] = prob.astype(BF16)
            ds_buf[pair, :, cut] = (prob * (dprob[:, cut] - stats(OWN_HEADS + head))).astype(BF16)


def pair_gradients(queries, douts, halves, p_buf, ds_buf, k_turned, add_dv, add_dk, add_dq):
    for pair in range(HEAD_PAIRS):
        lanes = pair_lanes(pair)
        add_dv(
            lanes,
            lax.dot_general(
                p_buf[pair], both_heads(douts(lanes), halves), NN, preferred_element_type=F32
            ),
        )
        add_dk(
            lanes,
            lax.dot_general(
                ds_buf[pair], both_heads(queries(lanes), halves), NN, preferred_element_type=F32
            ),
        )
        both = lax.dot_general(k_turned[lanes, :], ds_buf[pair], NN, preferred_element_type=F32)
        for side in range(2):
            rows = slice(side * 64, side * 64 + 64)
            low = pair * 128 + side * 64
            add_dq(slice(low, low + 64), both[rows, side * BLK : side * BLK + BLK])


def tabulate(lists, counts, x, y, z, table):
    cell = lax.broadcasted_iota(jnp.int32, (CELLS, KEY_SHARDS), 0)
    shard = lax.broadcasted_iota(jnp.int32, (SLOTS, KEY_SHARDS), 1)
    slot = lax.broadcasted_iota(jnp.int32, (SLOTS, KEY_SHARDS), 0)
    used = jnp.zeros((CELLS, KEY_SHARDS), F32)
    for owner in range(CORES):
        queries = lists[owner, 0:SLOTS, :]
        blocks = lists[owner, SLOTS : 2 * SLOTS, :]
        column = lax.shift_right_logical(shard, 3)
        ok = (slot < counts[owner]) & ((shard & 7) == z) & (lax.shift_right_logical(queries, 3) == x)
        code = (blocks * NX + column) * QUERY_BLOCKS + (queries & 7) * CORES + owner
        code = jnp.where(ok, code, -1)
        for row in range(SLOTS):
            used = jnp.where(cell == code[row : row + 1, :], 1.0, used)
    used = jnp.max(used, axis=1, keepdims=True)
    order = lax.broadcasted_iota(jnp.int32, (CELLS, 1), 0)
    away = (lax.shift_right_logical(order & 15, 1) - z + REACH + NZ) & 7
    near = jnp.where(away < NEAR, used, 0.0)
    nearer = jnp.where((away > 0) & (away < NEAR - 1), used, 0.0)
    before = lax.broadcasted_iota(jnp.int32, (CELLS, CELLS), 0)
    before = before > lax.broadcasted_iota(jnp.int32, (CELLS, CELLS), 1)
    before = jnp.where(before, 1.0, 0.0).astype(BF16)
    spread = jnp.zeros((CELLS, 128), F32)
    up_block = lax.shift_right_logical(order, 6)
    across_block = lax.shift_right_logical(order, 4) & 3
    close = (((up_block - y + 1 + NY) & 3) < LINES) & (((across_block - x + 1 + NX) & 3) < LINES)

    def ranks(cells):
        return lax.dot_general(before, cells.astype(BF16), NN, preferred_element_type=F32)

    closest = jnp.where(close, nearer, 0.0) + spread
    first_rank = ranks(closest)
    first = jnp.where(first_rank < FIRST, closest, 0.0)
    middle = (nearer + spread) - first
    middle_rank = ranks(middle)
    middle = jnp.where(middle_rank < MIDDLE, middle, 0.0)
    second = (near + spread) - first - middle
    second_rank = ranks(second)
    second = jnp.where(second_rank < SECOND, second, 0.0)
    others = (used + spread) - first - middle - second
    other_rank = ranks(others)
    lane = lax.broadcasted_iota(jnp.int32, (CELLS, 128), 1)
    line = lax.broadcasted_iota(jnp.int32, (CELLS, 128), 0)
    number = line.astype(F32)

    def total(values):
        return jnp.sum(values, axis=0, keepdims=True)

    place = lane.astype(F32)
    rows = [
        total(jnp.where(first_rank == place, first * number, 0.0))
        + total(jnp.where(middle_rank + FIRST == place, middle * number, 0.0))
        + total(jnp.where(second_rank + (FIRST + MIDDLE) == place, second * number, 0.0)),
        total(jnp.where(other_rank == place, others * number, 0.0)),
        total(jnp.where(other_rank == place + 128.0, others * number, 0.0)),
        total(jnp.where(line < lane * QUERY_BLOCKS, first, 0.0)),
        total(jnp.where(line < lane * QUERY_BLOCKS, others, 0.0)),
        total(jnp.where(line < lane * QUERY_BLOCKS, second, 0.0)),
        total(jnp.where(line < lane * QUERY_BLOCKS, middle, 0.0)),
    ]
    table[...] = jnp.zeros(TABLE, jnp.int32)
    for index, row in enumerate(rows):
        table[index : index + 1, :] = row.astype(jnp.int32)


def half_of(core, size):
    return pl.ds(pl.multiple_of(core * size, size), size)


GATHER_COPIES = 58


def gather_kernel(
    q_ref, do_ref, k_ref, v_ref, out_ref, lse_ref, list_ref, count_ref,
    q_all, do_all, st_all, k_all, v_all, table_out, dk_early, dv_early, dq_early,
    do_buf, out_buf, lse_buf, st_buf, list_all, count_all, q_near, do_near, st_near, k_near, v_near,
    k_turned, p_buf, ds_buf, table, table_s, send_sems, recv_sems, local_sems, near_sems, far_sems,
):
    me = Place()
    x, y, z, core = me.x, me.y, me.z, me.core
    every = slice(None)
    rows = half_of(core, HALF)
    mine = half_of(core, COLS)
    theirs = half_of(1 - core, COLS)

    loads = [
        pltpu.make_async_copy(do_ref, do_buf, local_sems.at[5]),
        pltpu.make_async_copy(out_ref, out_buf, local_sems.at[6]),
        pltpu.make_async_copy(lse_ref, lse_buf, local_sems.at[7]),
    ]
    for load in loads:
        load.start()
    owns = [
        pltpu.make_async_copy(q_ref.at[every, mine], q_all.at[z, core], local_sems.at[0]),
        pltpu.make_async_copy(do_ref.at[every, mine], do_all.at[z, core], local_sems.at[1]),
        pltpu.make_async_copy(k_ref.at[every, mine], k_all.at[y, x, rows], local_sems.at[2]),
        pltpu.make_async_copy(v_ref.at[every, mine], v_all.at[x, y, rows], local_sems.at[3]),
        pltpu.make_async_copy(list_ref, list_all.at[core], local_sems.at[4]),
        pltpu.make_async_copy(count_ref, count_all.at[core], local_sems.at[8]),
    ]
    for own in owns:
        own.start()
    me.greet(both_cores=True)
    send = Sender(send_sems, recv_sems)
    up, down = me.over_z(1), me.over_z(-1)

    def to_both(ref, target, straight, crossed):
        return [
            send(ref.at[every, mine], target, straight),
            send(ref.at[every, theirs], target, crossed),
        ]

    cross_up, cross_down = me.over_z(1, 1), me.over_z(-1, 1)
    q_up = [to_both(q_ref, q_all.at[z, core], up, cross_up)]
    do_down = [to_both(do_ref, do_all.at[z, core], down, cross_down)]
    k_swap = send(k_ref.at[every, theirs], k_all.at[y, x, rows], me.sibling)
    v_swap = send(v_ref.at[every, theirs], v_all.at[x, y, rows], me.sibling)
    k_right = to_both(k_ref, k_all.at[y, x, rows], me.over_x(1), me.over_x(1, 1))
    k_left = to_both(k_ref, k_all.at[y, x, rows], me.over_x(-1), me.over_x(-1, 1))
    v_right = to_both(v_ref, v_all.at[x, y, rows], me.over_y(1), me.over_y(1, 1))
    v_left = to_both(v_ref, v_all.at[x, y, rows], me.over_y(-1), me.over_y(-1, 1))
    do_up = [to_both(do_ref, do_all.at[z, core], up, cross_up)]
    q_down = [to_both(q_ref, q_all.at[z, core], down, cross_down)]
    swaps = [
        send(q_ref.at[every, theirs], q_all.at[z, core], me.sibling),
        send(do_ref.at[every, theirs], do_all.at[z, core], me.sibling),
        send(list_ref, list_all.at[core], me.sibling),
        send(count_ref, count_all.at[core], me.sibling),
    ]

    for load in loads:
        load.wait()
    products = do_buf[...].astype(F32) * out_buf[...].astype(F32)
    high = products.astype(BF16)
    low = (products - high.astype(F32)).astype(BF16)
    head = lax.broadcasted_iota(jnp.int32, (HEADS, WIDTH), 0) * 64
    feature = lax.broadcasted_iota(jnp.int32, (HEADS, WIDTH), 1)
    member = jnp.where((feature >= head) & (feature < head + 64), 1.0, 0.0).astype(BF16)
    over_features = (((1,), (1,)), ((), ()))
    delta = lax.dot_general(member, high, over_features, preferred_element_type=F32)
    delta = delta + lax.dot_general(member, low, over_features, preferred_element_type=F32)
    for side in range(CORES):
        heads = slice(side * OWN_HEADS, side * OWN_HEADS + OWN_HEADS)
        st_buf[side, 0:OWN_HEADS, :] = lse_buf[heads, :] * LOG2E
        st_buf[side, OWN_HEADS : 2 * OWN_HEADS, :] = delta[heads, :]
    for own in owns:
        own.wait()
    nears = []

    def bring_near(arrays, distance):
        for blocks, held in arrays:
            copy = pltpu.make_async_copy(
                blocks.at[me.zs(distance)], held.at[distance + REACH], near_sems.at[len(nears)]
            )
            copy.start()
            nears.append(copy)

    st_own = pltpu.make_async_copy(st_buf.at[core], st_all.at[z, core], local_sems.at[0])
    st_own.start()
    swaps.append(send(st_buf.at[1 - core], st_all.at[z, core], me.sibling))
    st_up, st_down = [], []
    for stats, straight, crossed in ((st_up, up, cross_up), (st_down, down, cross_down)):
        stats.append(
            [
                send(st_buf.at[core], st_all.at[z, core], straight),
                send(st_buf.at[1 - core], st_all.at[z, core], crossed),
            ]
        )

    def arrived(*groups):
        for group in groups:
            for copy in group:
                copy.wait_recv()

    upper, lower = pl.ds(0, HALF), pl.ds(HALF, HALF)
    arrived(k_right)
    k_part = k_all.at[y, me.xs(-1), upper]
    k_far = [send(k_part, k_part, me.over_x(1))]
    arrived(v_right)
    v_part = v_all.at[x, me.ys(-1), upper]
    v_far = [send(v_part, v_part, me.over_y(1))]
    arrived(k_left)
    k_part = k_all.at[y, me.xs(1), lower]
    k_far.append(send(k_part, k_part, me.over_x(-1)))
    arrived(v_left)
    v_part = v_all.at[x, me.ys(1), lower]
    v_far.append(send(v_part, v_part, me.over_y(-1)))

    first, second = pl.ds(0, 2), pl.ds(2, 2)

    def lines(blocks, place, over):
        ahead, back = [], []
        for part_ahead, part_back in ((first, second), (second, first)):
            part = blocks.at[place, part_ahead]
            ahead.append(send(part, part, over(1)))
            part = blocks.at[place, part_back]
            back.append(send(part, part, over(-1)))
        return ahead, back

    arrived([k_swap], k_far)
    k_right, k_left = lines(k_all, y, me.over_y)
    arrived([v_swap], v_far)
    v_right, v_left = lines(v_all, x, me.over_x)

    def forward(hop, sign, blocks, copies):
        arrived(copies[hop - 1])
        block = blocks.at[me.zs(-sign * hop)]
        copies.append([send(block, block, up if sign > 0 else down)])

    forward(1, 1, q_all, q_up)
    forward(1, -1, do_all, do_down)
    arrived(swaps)
    st_own.wait()
    tabulate(list_all, count_all, x, y, z, table)
    to_scalars = pltpu.make_async_copy(table, table_s, local_sems.at[1])
    to_scalars.start()
    table_store = pltpu.make_async_copy(table, table_out, local_sems.at[2])
    table_store.start()
    every_array = ((q_all, q_near), (do_all, do_near), (st_all, st_near))
    bring_near(every_array, 0)

    def across(copies, blocks, start, part, device):
        arrived(copies[:1])
        part = blocks.at[start, part]
        return send(part, part, device)

    k_far = [across(k_right, k_all, me.ys(-1), first, me.over_y(1))]
    v_far = [across(v_right, v_all, me.xs(-1), first, me.over_x(1))]
    k_far.append(across(k_left, k_all, me.ys(1), second, me.over_y(-1)))
    v_far.append(across(v_left, v_all, me.xs(1), second, me.over_x(-1)))
    forward(1, 1, do_all, do_up)
    forward(1, -1, q_all, q_down)
    forward(1, 1, st_all, st_up)
    forward(1, -1, st_all, st_down)
    bring_near(every_array, 1)
    bring_near(every_array, -1)

    forward(2, 1, q_all, q_up)
    forward(2, -1, do_all, do_down)
    forward(2, 1, do_all, do_up)
    forward(2, -1, q_all, q_down)
    forward(2, 1, st_all, st_up)
    forward(2, -1, st_all, st_down)

    bring_near(every_array, 2)
    bring_near(every_array, -2)
    arrived(k_right[1:], k_left[1:], v_right[1:], v_left[1:])
    for step in (-1, 0, 1):
        for blocks, line, held in ((k_all, me.ys(step), k_near), (v_all, me.xs(step), v_near)):
            copy = pltpu.make_async_copy(blocks.at[line], held.at[step + 1], near_sems.at[len(nears)])
            copy.start()
            nears.append(copy)
    for copy in nears:
        copy.wait()
    to_scalars.wait()
    halves = head_halves()
    firsts, middles, seconds = (table_s[row, KEY_BLOCKS] for row in (3, 6, 5))

    def early(index, low, count, close=False):
        entry = jnp.clip(table_s[0, index], 0, CELLS - 1)
        block = lax.div(entry, QUERY_BLOCKS)
        up_block, across_block = lax.div(block, NX), lax.rem(block, NX)
        query = lax.rem(lax.div(lax.rem(entry, QUERY_BLOCKS), CORES) - z + REACH + NZ, NZ)
        query = jnp.minimum(query, NEAR - 1)
        owner = lax.rem(entry, CORES)
        keep = index - low < count
        up_line = jnp.minimum(lax.rem(up_block - y + 1 + NY, NY), LINES - 1)
        across_line = jnp.minimum(lax.rem(across_block - x + 1 + NX, NX), LINES - 1)

        def keys(lanes):
            if close:
                return k_near[up_line, across_block, :, lanes]
            return k_all[up_block, across_block, :, lanes]

        def values(lanes):
            if close:
                return v_near[across_line, up_block, :, lanes]
            return v_all[across_block, up_block, :, lanes]

        def queries(lanes):
            return q_near[query, owner, :, lanes]

        def douts(lanes):
            return do_near[query, owner, :, lanes]

        def stats(row):
            return st_near[query, owner, row : row + 1, :]

        turn_keys(keys, k_turned)
        pair_products(keys, values, queries, douts, stats, halves, p_buf, ds_buf, keep=keep)

        def put_dv(lanes, value):
            dv_early[index, :, lanes] = value

        def put_dk(lanes, value):
            dk_early[index, :, lanes] = value

        def put_dq(rows, value):
            dq_early[index, rows, :] = value

        pair_gradients(queries, douts, halves, p_buf, ds_buf, k_turned, put_dv, put_dk, put_dq)

    def early_pairs(low, slots, count, close=False):
        def one(index, carry):
            early(index, low, count, close)
            return carry

        lax.fori_loop(low, low + slots, one, 0)

    early_pairs(0, FIRST, firsts, close=True)
    arrived(k_far, v_far)
    early_pairs(FIRST, MIDDLE, middles)
    forward(3, 1, q_all, q_up)
    forward(3, -1, do_all, do_down)
    forward(3, 1, st_all, st_up)
    arrived(do_up[2], q_down[2], st_down[2])
    nears.clear()
    for distance in (REACH, -REACH):
        for blocks, held in every_array:
            copy = pltpu.make_async_copy(
                blocks.at[me.zs(distance)], held.at[distance + REACH], far_sems.at[len(nears)]
            )
            copy.start()
            nears.append(copy)
    for copy in nears:
        copy.wait()
    early_pairs(FIRST + MIDDLE, SECOND, seconds)
    arrived(q_up[3], do_down[3], st_up[3])
    table_store.wait()
    send.finish()
    assert len(send.copies) == GATHER_COPIES, len(send.copies)


def gather(q, do, k, v, out, lse, lists, counts):
    return pl.pallas_call(
        gather_kernel,
        out_shape=[
            jax.ShapeDtypeStruct((NZ, CORES, BLK, COLS), BF16),
            jax.ShapeDtypeStruct((NZ, CORES, BLK, COLS), BF16),
            jax.ShapeDtypeStruct((NZ, CORES, 2 * OWN_HEADS, BLK), F32),
            jax.ShapeDtypeStruct((NY, NX, BLK, COLS), BF16),
            jax.ShapeDtypeStruct((NX, NY, BLK, COLS), BF16),
            jax.ShapeDtypeStruct(TABLE, jnp.int32),
            jax.ShapeDtypeStruct((EARLY, BLK, COLS), F32),
            jax.ShapeDtypeStruct((EARLY, BLK, COLS), F32),
            jax.ShapeDtypeStruct((EARLY, COLS, BLK), F32),
        ],
        in_specs=[HBM] * 8,
        out_specs=[VMEM] * 5 + [HBM] + [VMEM] * 3,
        scratch_shapes=[
            pltpu.VMEM((BLK, WIDTH), BF16),
            pltpu.VMEM((BLK, WIDTH), BF16),
            pltpu.VMEM((HEADS, BLK), F32),
            pltpu.VMEM((CORES, 2 * OWN_HEADS, BLK), F32),
            pltpu.VMEM((CORES, 2 * SLOTS, KEY_SHARDS), jnp.int32),
            pltpu.VMEM((CORES, 1, KEY_SHARDS), jnp.int32),
            pltpu.VMEM((NEAR, CORES, BLK, COLS), BF16),
            pltpu.VMEM((NEAR, CORES, BLK, COLS), BF16),
            pltpu.VMEM((NEAR, CORES, 2 * OWN_HEADS, BLK), F32),
            pltpu.VMEM((LINES, 4, BLK, COLS), BF16),
            pltpu.VMEM((LINES, 4, BLK, COLS), BF16),
            pltpu.VMEM((COLS, BLK), BF16),
            pltpu.VMEM((HEAD_PAIRS, BLK, 2 * BLK), BF16),
            pltpu.VMEM((HEAD_PAIRS, BLK, 2 * BLK), BF16),
            pltpu.VMEM(TABLE, jnp.int32),
            pltpu.SMEM(TABLE, jnp.int32),
            pltpu.SemaphoreType.DMA((GATHER_COPIES,)),
            pltpu.SemaphoreType.DMA((GATHER_COPIES,)),
            pltpu.SemaphoreType.DMA((9,)),
            pltpu.SemaphoreType.DMA((3 * (NEAR - 2) + 2 * LINES,)),
            pltpu.SemaphoreType.DMA((6,)),
        ],
        compiler_params=pltpu.CompilerParams(
            collective_id=0, has_side_effects=True, vmem_limit_bytes=GATHER_LIMIT
        ),
        name="gather_blocks",
    )(q, do, k, v, out, lse, lists, counts)


def pair_kernel(
    table, q_all, do_all, st_all, k_all, v_all, dk_early, dv_early, dq_early,
    dq_out, dk_out, dv_out,
    k_turned, p_buf, ds_buf, dq_sum, dk_sum, dv_sum,
):
    def clear(query, carry):
        dq_sum[query] = jnp.zeros((COLS, BLK), F32)
        return carry

    lax.fori_loop(0, QUERY_BLOCKS, clear, 0)
    halves = head_halves()

    def key_block(block, carry):
        up, across = lax.div(block, NX), lax.rem(block, NX)
        first_low, first_high = table[3, block], table[3, block + 1]
        middle_low, middle_high = FIRST + table[6, block], FIRST + table[6, block + 1]
        second_low = FIRST + MIDDLE + table[5, block]
        second_high = FIRST + MIDDLE + table[5, block + 1]
        low, high = table[4, block], table[4, block + 1]
        have = (first_high - first_low) + (middle_high - middle_low)
        have += (second_high - second_low) + (high - low)

        @pl.when(have == 0)
        def _():
            dk_out[up, across] = jnp.zeros((BLK, COLS), BF16)
            dv_out[across, up] = jnp.zeros((BLK, COLS), BF16)

        def keys(lanes):
            return k_all[up, across, :, lanes]

        def values(lanes):
            return v_all[across, up, :, lanes]

        def take(slot, carry):
            query = lax.rem(table[0, slot], QUERY_BLOCKS)
            dk_sum[...] += dk_early[slot]
            dv_sum[...] += dv_early[slot]
            dq_sum[query] += dq_early[slot]
            return carry

        def used(slot, carry):
            query = lax.rem(table[1 + lax.div(slot, 128), lax.rem(slot, 128)], QUERY_BLOCKS)

            def queries(lanes):
                return q_all[query, :, lanes]

            def douts(lanes):
                return do_all[query, :, lanes]

            def stats(row):
                return st_all[query, row : row + 1, :]

            pair_products(keys, values, queries, douts, stats, halves, p_buf, ds_buf)

            def add_dv(lanes, value):
                dv_sum[:, lanes] += value

            def add_dk(lanes, value):
                dk_sum[:, lanes] += value

            def add_dq(rows, value):
                dq_sum[query, rows, :] += value

            pair_gradients(queries, douts, halves, p_buf, ds_buf, k_turned, add_dv, add_dk, add_dq)
            return carry

        @pl.when(have > 0)
        def _():
            dk_sum[...] = jnp.zeros_like(dk_sum)
            dv_sum[...] = jnp.zeros_like(dv_sum)
            lax.fori_loop(first_low, first_high, take, 0)
            lax.fori_loop(middle_low, middle_high, take, 0)
            lax.fori_loop(second_low, second_high, take, 0)

            @pl.when(high > low)
            def _():
                turn_keys(keys, k_turned)

            lax.fori_loop(low, high, used, 0)
            dk_out[up, across] = (dk_sum[...] * SCALE).astype(BF16)
            dv_out[across, up] = dv_sum[...].astype(BF16)

        return carry

    lax.fori_loop(0, KEY_BLOCKS, key_block, 0)

    def turn_in(query, carry):
        dq_out[query] = (dq_sum[query] * SCALE).astype(BF16)
        return carry

    lax.fori_loop(0, QUERY_BLOCKS, turn_in, 0)


def pairs_over_blocks(q_all, do_all, st_all, k_all, v_all, table, dk_early, dv_early, dq_early):
    return pl.pallas_call(
        pair_kernel,
        out_shape=[
            jax.ShapeDtypeStruct((QUERY_BLOCKS, COLS, BLK), BF16),
            jax.ShapeDtypeStruct((NY, NX, BLK, COLS), BF16),
            jax.ShapeDtypeStruct((NX, NY, BLK, COLS), BF16),
        ],
        in_specs=[pl.BlockSpec(memory_space=pltpu.SMEM)] + [VMEM] * 8,
        out_specs=[VMEM] * 3,
        scratch_shapes=[
            pltpu.VMEM((COLS, BLK), BF16),
            pltpu.VMEM((HEAD_PAIRS, BLK, 2 * BLK), BF16),
            pltpu.VMEM((HEAD_PAIRS, BLK, 2 * BLK), BF16),
            pltpu.VMEM((QUERY_BLOCKS, COLS, BLK), F32),
            pltpu.VMEM((BLK, COLS), F32),
            pltpu.VMEM((BLK, COLS), F32),
        ],
        compiler_params=pltpu.CompilerParams(vmem_limit_bytes=PAIR_LIMIT),
        name="used_pairs",
    )(
        table,
        q_all.reshape(QUERY_BLOCKS, BLK, COLS),
        do_all.reshape(QUERY_BLOCKS, BLK, COLS),
        st_all.reshape(QUERY_BLOCKS, 2 * OWN_HEADS, BLK),
        k_all,
        v_all,
        dk_early,
        dv_early,
        dq_early,
    )


REDUCE_COPIES = 41
ROW_STEP = 16


def reduce_kernel(
    dq_part, dk_part, dv_part,
    gq_out, gk_out, gv_out,
    dq_own, dq_in_up, dq_in_down, dq_end,
    k_out, k_far, k_near, k_mid, k_mid_far, k_end,
    v_out, v_far, v_near, v_mid, v_mid_far, v_end,
    send_sems, recv_sems, q_end_sems, k_end_sems, v_end_sems,
):
    me = Place()
    x, y, z, core = me.x, me.y, me.z, me.core
    first, second = pl.ds(0, 2), pl.ds(2, 2)
    me.greet(both_cores=True)
    send = Sender(send_sems, recv_sems)
    up, down = me.over_z(1), me.over_z(-1)

    def add_rows(total, terms, count):
        def one(index, carry):
            at = pl.ds(pl.multiple_of(index * ROW_STEP, ROW_STEP), ROW_STEP)
            value = terms[0][at, :].astype(F32)
            for term in terms[1:]:
                value = value + term[at, :].astype(F32)
            total[at, :] = value.astype(total.dtype)
            return carry

        lax.fori_loop(0, count // ROW_STEP, one, 0, unroll=4)

    arrive = {
        ("up", 0, 1): send(dq_part.at[me.zs(4), 0], dq_in_up.at[0, 0], up),
        ("down", 1, 1): send(dq_part.at[me.zs(4), 1], dq_in_down.at[0, 1], down),
    }
    k_a = send(dk_part.at[me.ys(2), first], k_far.at[0], me.over_y(1))
    k_b = send(dk_part.at[me.ys(2), second], k_far.at[1], me.over_y(-1))
    v_a = send(dv_part.at[me.xs(2), first], v_far.at[0], me.over_x(1))
    v_b = send(dv_part.at[me.xs(2), second], v_far.at[1], me.over_x(-1))
    arrive["up", 1, 2] = send(dq_part.at[me.zs(3), 1], dq_in_up.at[1, 1], up)
    arrive["down", 0, 2] = send(dq_part.at[me.zs(-3), 0], dq_in_down.at[1, 0], down)
    k_in = [
        send(dk_part.at[me.ys(1), second], k_near.at[0, second], me.over_y(1)),
        send(dk_part.at[me.ys(-1), first], k_near.at[1, first], me.over_y(-1)),
    ]
    v_in = [
        send(dv_part.at[me.xs(1), second], v_near.at[0, second], me.over_x(1)),
        send(dv_part.at[me.xs(-1), first], v_near.at[1, first], me.over_x(-1)),
    ]
    q_sib = send(dq_part.at[z, 1 - core], dq_end.at[2, core], me.sibling, q_end_sems.at[2, core])

    def hop_q(direction, shard, hop):
        if direction == "up":
            side, step, inbox, way = 0, 4 - hop, dq_in_up, 1
        else:
            side, step, inbox, way = 1, hop - 4, dq_in_down, -1
        own = dq_own.at[me.zs(step), shard]
        arrive[direction, shard, hop].wait_recv()
        add_rows(own, [dq_part.at[me.zs(step), shard], inbox.at[hop - 1, shard]], COLS)
        if hop < 3:
            arrive[direction, shard, hop + 1] = send(own, inbox.at[hop, shard], me.over_z(way))
        else:
            send(own, dq_end.at[side, core], me.over_z(way, owner=shard), q_end_sems.at[side, core])

    add_rows(dq_end.at[2, core], [dq_part.at[z, core]], COLS)
    hop_q("up", 0, 1)
    hop_q("down", 1, 1)

    def onward(arrival, part, place, base, inbox, outbox):
        arrival.wait_recv()
        for row in range(2):
            add_rows(outbox.at[row], [part.at[place, base + row], inbox.at[row]], BLK)

    onward(k_a, dk_part, me.ys(1), 0, k_far.at[0], k_out.at[0])
    k_in.append(send(k_out.at[0], k_near.at[0, first], me.over_y(1)))
    onward(v_a, dv_part, me.xs(1), 0, v_far.at[0], v_out.at[0])
    v_in.append(send(v_out.at[0], v_near.at[0, first], me.over_x(1)))
    onward(k_b, dk_part, me.ys(-1), 2, k_far.at[1], k_out.at[1])
    k_in.append(send(k_out.at[1], k_near.at[1, second], me.over_y(-1)))
    onward(v_b, dv_part, me.xs(-1), 2, v_far.at[1], v_out.at[1])
    v_in.append(send(v_out.at[1], v_near.at[1, second], me.over_x(-1)))
    for hop, shard in ((2, 1), (2, 0), (3, 1), (3, 0)):
        hop_q("up", shard, hop)
        hop_q("down", 1 - shard, hop)

    half_rows = (pl.ds(0, HALF), pl.ds(HALF, HALF))

    def mix(own, here, near, middle, row):
        add_rows(middle.at[row], [own.at[here, row], near.at[0, row], near.at[1, row]], BLK)

    def turn_far(arrivals, own, here, near, middle, far, axis, over):
        for arrival in arrivals:
            arrival.wait_recv()
        farthest = axis(2)
        mix(own, here, near, middle, farthest)
        far_a = send(middle.at[farthest, half_rows[0]], far.at[0], over(1))
        far_b = send(middle.at[farthest, half_rows[1]], far.at[1], over(-1))
        return far_a, far_b

    def turn_near(own, here, near, middle, end, sems, axis, over, place):
        for side, step in enumerate((1, -1)):
            row, owner = axis(step), 1 - side
            mix(own, here, near, middle, row)
            part = middle.at[row, half_rows[owner]]
            send(part, end.at[side, core], over(step, owner=owner), sems.at[side, core])
        mix(own, here, near, middle, place)
        send(middle.at[place, half_of(1 - core, HALF)], end.at[2, core], me.sibling, sems.at[2, core])
        end[2, core] = middle[place, half_of(core, HALF), :]

    def last(arrival, middle, at, half, far, end, sems, side, device):
        arrival.wait_recv()
        part = middle.at[at, half_rows[half]]
        add_rows(part, [part, far], HALF)
        send(part, end.at[side, core], device, sems.at[side, core])

    kx_a, kx_b = turn_far(k_in, dk_part, y, k_near, k_mid, k_mid_far, me.xs, me.over_x)
    vy_a, vy_b = turn_far(v_in, dv_part, x, v_near, v_mid, v_mid_far, me.ys, me.over_y)
    turn_near(dk_part, y, k_near, k_mid, k_end, k_end_sems, me.xs, me.over_x, x)
    turn_near(dv_part, x, v_near, v_mid, v_end, v_end_sems, me.ys, me.over_y, y)
    last(kx_a, k_mid, me.xs(1), 0, k_mid_far.at[0], k_end, k_end_sems, 0, me.over_x(1, owner=0))
    last(kx_b, k_mid, me.xs(-1), 1, k_mid_far.at[1], k_end, k_end_sems, 1, me.over_x(-1, owner=1))
    last(vy_a, v_mid, me.ys(1), 0, v_mid_far.at[0], v_end, v_end_sems, 0, me.over_y(1, owner=0))
    last(vy_b, v_mid, me.ys(-1), 1, v_mid_far.at[1], v_end, v_end_sems, 1, me.over_y(-1, owner=1))

    def ended(end, sems):
        for side in range(2):
            for column in range(CORES):
                pltpu.make_async_copy(end.at[side, column], end.at[side, column], sems.at[side, column]).wait()
        other = end.at[2, 1 - core]
        pltpu.make_async_copy(other, other, sems.at[2, 1 - core]).wait()

    ended(dq_end, q_end_sems)
    for column in range(CORES):
        for tile in range(COLS // 128):
            at = pl.ds(tile * 128, 128)
            value = (
                dq_end[0, column, at, :].astype(F32)
                + dq_end[1, column, at, :].astype(F32)
                + dq_end[2, column, at, :].astype(F32)
            )
            gq_out[:, pl.ds(column * COLS + tile * 128, 128)] = jnp.transpose(value).astype(BF16)
    for out, end, sems in ((gk_out, k_end, k_end_sems), (gv_out, v_end, v_end_sems)):
        ended(end, sems)
        for column in range(CORES):
            target = out.at[:, pl.ds(column * COLS, COLS)]
            add_rows(target, [end.at[side, column] for side in range(3)], HALF)
    send.finish()
    assert len(send.copies) == REDUCE_COPIES, len(send.copies)


def reduce_parts(dq_part, dk_part, dv_part):
    two = pltpu.VMEM((2, 2, BLK, COLS), BF16)
    near = pltpu.VMEM((2, 4, BLK, COLS), BF16)
    four = pltpu.VMEM((4, BLK, COLS), BF16)
    half = pltpu.VMEM((2, HALF, COLS), BF16)
    end = pltpu.VMEM((3, CORES, HALF, COLS), BF16)
    inbox = pltpu.VMEM((3, CORES, COLS, BLK), BF16)
    sems = pltpu.SemaphoreType.DMA((3, CORES))
    return pl.pallas_call(
        reduce_kernel,
        out_shape=[
            jax.ShapeDtypeStruct((BLK, WIDTH), BF16),
            jax.ShapeDtypeStruct((HALF, WIDTH), BF16),
            jax.ShapeDtypeStruct((HALF, WIDTH), BF16),
        ],
        in_specs=[VMEM] * 3,
        out_specs=[VMEM] * 3,
        scratch_shapes=[
            pltpu.VMEM((NZ, CORES, COLS, BLK), BF16), inbox, inbox, inbox,
            two, two, near, four, half, end,
            two, two, near, four, half, end,
            pltpu.SemaphoreType.DMA((REDUCE_COPIES,)),
            pltpu.SemaphoreType.DMA((REDUCE_COPIES,)),
            sems, sems, sems,
        ],
        compiler_params=pltpu.CompilerParams(
            collective_id=1, has_side_effects=True, vmem_limit_bytes=VMEM_LIMIT
        ),
        name="reduce_parts",
    )(dq_part.reshape(NZ, CORES, COLS, BLK), dk_part, dv_part)


def body(q, k, v, out, do, lse, block_pairs, counts):
    lists = block_pairs.transpose(0, 2, 3, 1).reshape(2 * SLOTS, KEY_SHARDS)
    arguments = (q, do, k, v, out, lse, lists, counts)
    held = [pltpu.with_memory_space_constraint(array, pltpu.HBM) for array in arguments]
    parts = pairs_over_blocks(*gather(*held))
    return tuple(reduce_parts(*parts))


def solution(mesh):
    placed = (
        P(("pb", "ka"), None),
        P(("ka", "pb"), None),
        P(("ka", "pb"), None),
        P(("pb", "ka"), None),
        P(("pb", "ka"), None),
        P(None, ("pb", "ka")),
        P("pb", None, None, None),
        P("pb", None),
    )
    return jax.shard_map(
        body,
        mesh=mesh,
        in_specs=placed,
        out_specs=(P(("pb", "ka"), None), P(("ka", "pb"), None), P(("ka", "pb"), None)),
        check_vma=False,
    )
```
